128 devices in a mesh: dp: 8 (over z_lo, x), tensor: 16 (over y, z_hi, core).
Axes of the slice: x: 4, y: 4, z: 4 (z_hi: 2, z_lo: 2; z = z_hi * 2 + z_lo), core: 2. Of those that a mesh axis runs over, the one named last changes fastest.
Arguments:
- tokens: bfloat16 [4096, 8192], P(('dp', 'tensor')), parts along dimension 0, may hold values from -6 to 6
- positions: int32 [16, 256], P('dp'), parts along dimension 0, may hold values from 0 to 511, as said below
- mask_embed: bfloat16 [8192], replicated, may hold values from -6 to 6
- norm_gain: bfloat16 [8192], replicated, may hold values from 0.099609375 to 1.8984375
- w_query: bfloat16 [8192, 8192], P(None, 'tensor')
- w_key: bfloat16 [8192, 1024], P(None, 'tensor')
- w_value: bfloat16 [8192, 1024], P(None, 'tensor'), may hold values from -0.0625 to 0.0625
- w_out: bfloat16 [8192, 8192], P('tensor'), may hold values from -0.25 to 0.25
Outputs:
- denoised: bfloat16 [4096, 8192], P(('dp', 'tensor')), parts along dimension 0
The draws below stay inside these ranges and needn't reach their ends.
There are 8 independent parts, one for each index of `dp`. The reference program is written for one: setup_inputs(seed, part) draws one part's arguments, and reference() takes and returns one part's arrays. A program takes and returns all parts, laid end to end along the dimension named above; an argument that names none is the same for every part. Nothing has to cross between parts.
Inputs may be any that keep to these rules, and one draw needn't show every extreme that they name: Each row holds 256 distinct positions.
All inputs are finite; a program needn't handle non-finite values.
Results may differ from the reference program's by a relative error of at most 0.039.
Values may be sent and summed in bfloat16 or wider, within the bound.
No kernel may reach another device: no remote copies, remote signals or barrier semaphores. Data moves between devices by JAX's collectives and lax.ppermute only.
A program may use at most 128 MiB of HBM per device.

```python
import jax
import jax.numpy as jnp
from jax import lax

D = 8192
HEADS = 64
KV_HEADS = 8
HD = 128
SEQ_LEN = 512
STEPS = 2
NMASK = 256
N_TENSOR = 16


def shared_parts(key):
    base = jax.random.normal(key, (D, HEADS * HD), jnp.float32) * D ** (-0.5)
    return base


def draw_w_query(key, part):
    base = shared_parts(key)
    return base.astype(jnp.bfloat16)


def draw_w_key(key, part):
    key = jax.random.fold_in(key, 2)
    fresh = jax.random.normal(key, (D, KV_HEADS * HD), jnp.float32) * D ** (-0.5)
    return fresh.astype(jnp.bfloat16)


def draw_positions(key, part):
    key = jax.random.fold_in(key, 3)
    rows_out = []
    for step in range(STEPS):
        order = jax.random.permutation(jax.random.fold_in(key, step), SEQ_LEN).astype(jnp.int32)
        last_at = jnp.argmax(order == SEQ_LEN - 1)
        order = order.at[last_at].set(order[0]).at[0].set(SEQ_LEN - 1)
        zero_at = jnp.argmax(order == 0)
        order = order.at[zero_at].set(order[1]).at[1].set(0)
        rows_out.append(order[:NMASK])
    return jnp.stack(rows_out).astype(jnp.int32)


def shard_levels(key, shape, pieces, least, largest):
    loudness, own = 1.0, jax.random.fold_in(key, 6)
    for dim, parts in pieces:
        steps = jnp.exp(jax.random.uniform(jax.random.fold_in(own, dim), (parts,), jnp.float32, least / len(pieces), largest / len(pieces)))
        loudness = loudness * jnp.repeat(steps, shape[dim] // parts).reshape([-1 if axis == dim else 1 for axis in range(len(shape))])
    return loudness


def normal_values(stream_key, shape, deviation, most, shards=(), kind=jnp.bfloat16):
    values = deviation * jax.random.normal(stream_key, shape, jnp.float32)
    if shards:
        values = values * shard_levels(stream_key, shape, shards, -0.22, 0.18)
    return jnp.clip(values, -most, most).astype(kind)


def setup_inputs(seed: int = 0, part: int = 0) -> dict:
    streams_of = jax.random.split(jax.random.key(seed), 9)
    own_keys = jax.random.split(jax.random.fold_in(streams_of[8], part), 9)
    return {
        "tokens": normal_values(own_keys[0], (SEQ_LEN, D), 1.0, 6.0, ((0, 16),)),
        "positions": draw_positions(jax.random.fold_in(jax.random.fold_in(streams_of[8], part), 71), part),
        "mask_embed": normal_values(streams_of[2], (D,), 1.0, 6.0),
        "norm_gain": jnp.clip(1.0 + 0.18 * jax.random.normal(streams_of[3], (D,), jnp.float32), 0.099609375, 1.8984375).astype(jnp.bfloat16),
        "w_query": draw_w_query(jax.random.fold_in(streams_of[8], 71), part),
        "w_key": draw_w_key(jax.random.fold_in(streams_of[8], 71), part),
        "w_value": normal_values(streams_of[6], (D, KV_HEADS * HD), D ** -0.5, 0.0625, ((1, 16),)),
        "w_out": normal_values(streams_of[7], (HEADS * HD, D), (HD * 4) ** -0.5, 0.25, ((0, 16),)),
    }


def normalize(rows, gain):
    values = rows.astype(jnp.float32)
    scale = lax.rsqrt(lax.optimization_barrier(jnp.mean(values * values, axis=-1, keepdims=True)) + 1e-05)
    return (values * scale * gain.astype(jnp.float32)).astype(jnp.bfloat16)

def rotate(values, first):
    count = values.shape[0]
    half = HD // 2
    where_at = (first + jnp.arange(count, dtype=jnp.int32)).astype(jnp.float32)
    freq = 500000.0 ** (-(jnp.arange(half, dtype=jnp.float32) * 2.0 / HD))
    angle = where_at[:, None] * freq[None, :]
    cosine = jnp.cos(angle)[:, None, :]
    sine = jnp.sin(angle)[:, None, :]
    left = values[..., :half]
    right = values[..., half:]
    return jnp.concatenate([left * cosine - right * sine, right * cosine + left * sine], axis=-1)

def one_head(args):
    query, keys, values = args
    scores = jnp.dot(query, keys.T, preferred_element_type=jnp.float32) * HD ** (-0.5)
    top = lax.optimization_barrier(jnp.max(scores, axis=-1, keepdims=True))
    weights = jnp.exp(scores - top)
    probs = (weights / lax.optimization_barrier(jnp.sum(weights, axis=-1, keepdims=True))).astype(jnp.bfloat16)
    return jnp.dot(probs, values, preferred_element_type=jnp.float32).astype(jnp.bfloat16)

def layer(hidden, norm_gain, w_query, w_key, w_value, w_out):
    length = hidden.shape[0]
    normed = normalize(hidden, norm_gain)
    query = jnp.dot(normed, w_query, preferred_element_type=jnp.float32).reshape(length, HEADS, HD)
    query = rotate(query, 0).astype(jnp.bfloat16)
    keys = jnp.dot(normed, w_key, preferred_element_type=jnp.float32).reshape(length, KV_HEADS, HD)
    keys = rotate(keys, 0).astype(jnp.bfloat16)
    values = jnp.dot(normed, w_value, preferred_element_type=jnp.float32).astype(jnp.bfloat16)
    values = values.reshape(length, KV_HEADS, HD)
    group = HEADS // KV_HEADS
    keys = jnp.repeat(keys, group, axis=1)
    values = jnp.repeat(values, group, axis=1)
    attn = lax.map(one_head, (query.transpose(1, 0, 2), keys.transpose(1, 0, 2), values.transpose(1, 0, 2)))
    attn = attn.transpose(1, 0, 2).reshape(length, HEADS * HD)
    span = HEADS * HD // N_TENSOR
    blocks = attn.reshape(length, N_TENSOR, span).transpose(1, 0, 2)
    weights = w_out.reshape(N_TENSOR, span, D)

    def add_group(total, pair):
        partial_value = jnp.dot(pair[0], pair[1], preferred_element_type=jnp.float32).astype(jnp.bfloat16)
        partial_value = lax.optimization_barrier(partial_value)
        return (total + partial_value.astype(jnp.float32), None)
    summed = lax.scan(add_group, jnp.zeros((length, D), jnp.float32), (blocks, weights))[0]
    return (hidden.astype(jnp.float32) + summed).astype(jnp.bfloat16)

def reference(tokens, positions, mask_embed, norm_gain, w_query, w_key, w_value, w_out):
    state = tokens
    spots = jnp.arange(SEQ_LEN, dtype=jnp.int32)
    result = tokens
    for step in range(STEPS):
        masked = jnp.any(spots[:, None] == positions[step][None, :], axis=1)
        hidden = jnp.where(masked[:, None], mask_embed[None, :], state)
        result = layer(hidden, norm_gain, w_query, w_key, w_value, w_out)
        if step + 1 < STEPS:
            state = jnp.where(masked[:, None], result, state)
    return result
```

```python
import jax
import jax.numpy as jnp
from jax import lax
from jax.sharding import PartitionSpec as P

HD = 128
HALF = HD // 2
PARTS = 16
CORE, ZED, NEAR, FAR = 1, 2, 4, 12
LINKS = (NEAR, FAR, ZED)
PIECES = (
    (0, 2816, (NEAR, FAR, ZED)),
    (2816, 2816, (FAR, ZED, NEAR)),
    (5632, 2560, (ZED, NEAR, FAR)),
)
BLOCKS = [a ^ b ^ c for a in (0, NEAR) for b in (0, FAR) for c in (0, ZED)]


def swap(value, mask):
    return lax.ppermute(value, "tensor", [(i, i ^ mask) for i in range(PARTS)])


def normalize(rows, gain):
    values = rows.astype(jnp.float32)
    scale = lax.rsqrt(jnp.mean(values * values, axis=-1, keepdims=True) + 1e-05)
    return (values * scale * gain.astype(jnp.float32)).astype(jnp.bfloat16)


def turns(spots):
    freq = 500000.0 ** (-(jnp.arange(HALF, dtype=jnp.float32) * 2.0 / HD))
    angle = spots.astype(jnp.float32)[:, None] * freq[None, :]
    return jnp.cos(angle), jnp.sin(angle)


def turn(left, right, cosine, sine):
    return jnp.concatenate(
        [left * cosine - right * sine, right * cosine + left * sine], axis=-1
    ).astype(jnp.bfloat16)


def gather_links(own, order):
    have = {0: own}
    for mask in order:
        have.update({key ^ mask: swap(block, mask) for key, block in list(have.items())})
    return have


def reduce_links(total, order):
    left = list(LINKS)
    for mask in order:
        at = left.index(mask)
        left.remove(mask)
        send = lax.index_in_dim(total, 1, at, keepdims=False)
        keep = lax.index_in_dim(total, 0, at, keepdims=False)
        got = swap(send, mask)
        total = (keep.astype(jnp.float32) + got.astype(jnp.float32)).astype(jnp.bfloat16)
    return total


def project_and_scatter(mixed, w_out):
    rows = mixed.shape[0] // PARTS
    half = mixed.shape[0] // 2
    outs = []
    for first, width, order in PIECES:
        weights = w_out[:, first : first + width]
        send = jnp.dot(mixed[half:], weights, preferred_element_type=jnp.float32).astype(jnp.bfloat16)
        keep = jnp.dot(mixed[:half], weights, preferred_element_type=jnp.float32).astype(jnp.bfloat16)
        got = swap(send, CORE)
        total = (keep.astype(jnp.float32) + got.astype(jnp.float32)).astype(jnp.bfloat16)
        outs.append(reduce_links(total.reshape(2, 2, 2, rows, width), order))
    return outs


def attend(query, keys, values):
    scores = jnp.einsum("hqd,kd->hqk", query, keys, preferred_element_type=jnp.float32) * HD ** (-0.5)
    top = jnp.max(scores, axis=-1, keepdims=True)
    weights = jnp.exp(scores - top)
    probs = (weights / jnp.sum(weights, axis=-1, keepdims=True)).astype(jnp.bfloat16)
    mixed = jnp.einsum("hqk,kd->hqd", probs, values, preferred_element_type=jnp.float32).astype(jnp.bfloat16)
    return jnp.concatenate([mixed[h] for h in range(mixed.shape[0])], axis=1)


def chosen(spots, positions):
    return jnp.any(spots[:, None] == positions[None, :], axis=1)


def pick(one_hot, rows):
    return jnp.dot(
        one_hot.astype(jnp.bfloat16), rows, preferred_element_type=jnp.float32
    ).astype(jnp.bfloat16)


def shards(tokens, positions, mask_embed, norm_gain, w_query, w_key, w_value, w_out):
    place = lax.axis_index("tensor")
    rows = tokens.shape[0]
    length = rows * PARTS
    heads = w_query.shape[1] // HD
    even = place % 2 == 0
    relative = jnp.array([m ^ c for c in (0, CORE) for m in BLOCKS], jnp.int32)
    owners = place ^ relative

    own_spots = place * rows + jnp.arange(rows, dtype=jnp.int32)
    own_masked_0 = chosen(own_spots, positions[0])
    own_masked_1 = chosen(own_spots, positions[1])
    hidden_0 = jnp.where(own_masked_0[:, None], mask_embed[None, :], tokens)
    normed_0 = normalize(hidden_0, norm_gain)
    parts = []
    for first, width, order in PIECES:
        have = gather_links(normed_0[:, first : first + width], order)
        parts.append(jnp.concatenate([have[m] for m in BLOCKS], axis=0))
    x_own = jnp.concatenate(parts, axis=1)

    kv_own = jnp.concatenate([w_key.T, w_value.T], axis=0)
    kv_weights = jnp.concatenate([kv_own, swap(kv_own, CORE)], axis=0)

    def split_kv(x):
        both = lax.dot_general(x, kv_weights, (((1,), (1,)), ((), ())), preferred_element_type=jnp.float32)
        k_own, v_own, k_other, v_other = (both[:, HALF * i : HALF * (i + 1)] for i in range(4))
        key = (jnp.where(even, k_own, k_other), jnp.where(even, k_other, k_own))
        value = jnp.where(
            even, jnp.concatenate([v_own, v_other], axis=1), jnp.concatenate([v_other, v_own], axis=1)
        )
        return key, value.astype(jnp.bfloat16)

    mask_normed = jnp.broadcast_to(normalize(mask_embed[None, :], norm_gain), (8, mask_embed.shape[0]))
    mask_query = jnp.dot(mask_normed, w_query, preferred_element_type=jnp.float32)[0].reshape(heads, 1, HD)
    mask_key, mask_value = split_kv(mask_normed)
    mask_key = (mask_key[0][:1], mask_key[1][:1])
    mask_value = mask_value[:1]

    spots = (owners[:, None] * rows + jnp.arange(rows, dtype=jnp.int32)[None, :]).reshape(-1)
    masked_1 = chosen(spots, positions[1])
    every = jnp.arange(length, dtype=jnp.int32)
    every_0 = chosen(every, positions[0])
    every_1 = chosen(every, positions[1])
    fresh = every_0 & ~every_1
    before = every[None, :] < every[:, None]
    fresh_count = jnp.sum(fresh.astype(jnp.int32))
    rank = jnp.where(
        fresh,
        jnp.sum((before & fresh[None, :]).astype(jnp.int32), axis=1),
        fresh_count + jnp.sum((before & (every_0 & every_1)[None, :]).astype(jnp.int32), axis=1),
    )
    rank = jnp.where(every_0, rank, -1)
    count = positions.shape[1]
    share = count // PARTS
    listed = (owners[:, None] * share + jnp.arange(share, dtype=jnp.int32)[None, :]).reshape(-1)
    list_spots = jnp.sum(jnp.where(rank[None, :] == listed[:, None], every[None, :], 0), axis=1)
    list_fresh = listed < fresh_count

    cosine, sine = turns(spots)
    list_cosine, list_sine = turns(list_spots)

    key_own, value_own = split_kv(x_own)
    key_own = turn(*key_own, cosine[: length // 2], sine[: length // 2])
    pair_own = jnp.concatenate([key_own, value_own], axis=1)
    pair = jnp.concatenate([pair_own, swap(pair_own, CORE)], axis=0)
    key_0, value_0 = pair[:, :HD], pair[:, HD:]
    query_0 = turn(mask_query[..., :HALF], mask_query[..., HALF:], list_cosine[None], list_sine[None])
    mixed_0 = attend(query_0, key_0, value_0)
    sums_0 = project_and_scatter(mixed_0, w_out)

    raw = []
    for (first, width, order), summed in zip(PIECES, sums_0):
        state = mask_embed[None, first : first + width].astype(jnp.float32) + summed.astype(jnp.float32)
        have = gather_links(state.astype(jnp.bfloat16), order)
        near = jnp.concatenate([have[m] for m in BLOCKS], axis=0)
        raw.append(jnp.concatenate([near, swap(near, CORE)], axis=0))
    raw = jnp.concatenate(raw, axis=1)

    x_all = jnp.concatenate([x_own, swap(x_own, CORE)], axis=0)

    def split_query(x, cosine, sine):
        query = jnp.dot(x, w_query, preferred_element_type=jnp.float32).reshape(-1, heads, HD)
        query = query.transpose(1, 0, 2)
        return turn(query[..., :HALF], query[..., HALF:], cosine[None], sine[None])

    query_tokens = split_query(x_all, cosine, sine)

    normed_1 = normalize(raw, norm_gain)
    key_list, value_list = split_kv(normed_1)
    key_list = turn(*key_list, list_cosine, list_sine)
    query_list = split_query(normed_1, list_cosine, list_sine)
    match = (spots[:, None] == list_spots[None, :]) & list_fresh[None, :]
    is_list = jnp.any(match, axis=1)
    moved = pick(match, jnp.concatenate([key_list, value_list] + [query_list[h] for h in range(heads)], axis=1))
    query_mask = turn(mask_query[..., :HALF], mask_query[..., HALF:], cosine[None], sine[None])
    key_mask = turn(*mask_key, cosine, sine)
    key_1 = jnp.where(masked_1[:, None], key_mask, jnp.where(is_list[:, None], moved[:, :HD], key_0))
    value_1 = jnp.where(masked_1[:, None], mask_value, jnp.where(is_list[:, None], moved[:, HD : 2 * HD], value_0))
    moved_query = jnp.stack([moved[:, HD * (h + 2) : HD * (h + 3)] for h in range(heads)])
    query_1 = jnp.where(
        masked_1[None, :, None],
        query_mask,
        jnp.where(is_list[None, :, None], moved_query, query_tokens),
    )
    mixed_1 = attend(query_1, key_1, value_1)
    sums_1 = project_and_scatter(mixed_1, w_out)

    own_match = (own_spots[:, None] == list_spots[None, :]) & list_fresh[None, :]
    own_list = jnp.any(own_match, axis=1)
    hidden_1 = jnp.where(
        own_masked_1[:, None],
        mask_embed[None, :],
        jnp.where(own_list[:, None], pick(own_match, raw), tokens),
    )
    summed_1 = jnp.concatenate(sums_1, axis=1)
    return (hidden_1.astype(jnp.float32) + summed_1.astype(jnp.float32)).astype(jnp.bfloat16)


def solution(mesh):
    placed = (
        P(("dp", "tensor"), None),
        P("dp", None),
        P(),
        P(),
        P(None, "tensor"),
        P(None, "tensor"),
        P(None, "tensor"),
        P("tensor", None),
    )
    return jax.shard_map(
        shards, mesh=mesh, in_specs=placed, out_specs=P(("dp", "tensor"), None), check_vma=False
    )
```

```python
import jax
import jax.numpy as jnp
from jax import lax
from jax.sharding import PartitionSpec as P

HD = 128
HALF = HD // 2
PARTS = 16
CORE, ZED, NEAR, FAR = 1, 2, 4, 12
LINKS = (NEAR, FAR, ZED)
PIECES = (
    (0, 2816, (NEAR, FAR, ZED)),
    (2816, 2816, (FAR, ZED, NEAR)),
    (5632, 2560, (ZED, NEAR, FAR)),
)
BLOCKS = [a ^ b ^ c for a in (0, NEAR) for b in (0, FAR) for c in (0, ZED)]


def swap(value, mask):
    return lax.ppermute(value, "tensor", [(i, i ^ mask) for i in range(PARTS)])


def normalize(rows, gain):
    values = rows.astype(jnp.float32)
    scale = lax.rsqrt(jnp.mean(values * values, axis=-1, keepdims=True) + 1e-05)
    return (values * scale * gain.astype(jnp.float32)).astype(jnp.bfloat16)


def turns(spots):
    freq = 500000.0 ** (-(jnp.arange(HALF, dtype=jnp.float32) * 2.0 / HD))
    angle = spots.astype(jnp.float32)[:, None] * freq[None, :]
    return jnp.cos(angle), jnp.sin(angle)


def turn(left, right, cosine, sine):
    return jnp.concatenate(
        [left * cosine - right * sine, right * cosine + left * sine], axis=-1
    ).astype(jnp.bfloat16)


def together(*values):
    return lax.optimization_barrier(values)


def keys_after(order, steps):
    keys = [0]
    for mask in order[:steps]:
        keys = keys + [key ^ mask for key in keys]
    return keys


def step_up(have, step):
    return [swap(block, order[step]) for block, (_, _, order) in zip(have, PIECES)]


def joined(have, got):
    return [jnp.concatenate(pair, axis=0) for pair in zip(have, got)]


def in_order(blocks, order, rows):
    keys = keys_after(order, 3)
    at = [keys.index(m) * rows for m in BLOCKS]
    return jnp.concatenate([blocks[i : i + rows] for i in at], axis=0)


def add(one, two):
    return (one.astype(jnp.float32) + two.astype(jnp.float32)).astype(jnp.bfloat16)


def project(mixed, w_out):
    rows = mixed.shape[0] // PARTS
    half = mixed.shape[0] // 2

    def product(some, first, width):
        weights = w_out[:, first : first + width]
        return jnp.dot(some, weights, preferred_element_type=jnp.float32).astype(jnp.bfloat16)

    send = [product(mixed[half:], first, width) for first, width, _ in PIECES]
    got = [swap(block, CORE) for block in send]
    keep = [product(mixed[:half], first, width) for first, width, _ in PIECES]
    return [
        add(one, two).reshape(2, 2, 2, rows, one.shape[1]) for one, two in zip(keep, got)
    ]


def step_down(totals, step):
    keep, got = [], []
    for total, (_, _, order) in zip(totals, PIECES):
        left = [mask for mask in LINKS if mask not in order[:step]]
        at = left.index(order[step])
        keep.append(lax.index_in_dim(total, 0, at, keepdims=False))
        got.append(swap(lax.index_in_dim(total, 1, at, keepdims=False), order[step]))
    return keep, got


def added(keep, got):
    return [add(one, two) for one, two in zip(keep, got)]


def attend(query, keys, values):
    scores = jnp.einsum("hqd,kd->hqk", query, keys, preferred_element_type=jnp.float32) * HD ** (-0.5)
    top = jnp.max(scores, axis=-1, keepdims=True)
    weights = jnp.exp(scores - top)
    probs = (weights / jnp.sum(weights, axis=-1, keepdims=True)).astype(jnp.bfloat16)
    mixed = jnp.einsum("hqk,kd->hqd", probs, values, preferred_element_type=jnp.float32).astype(jnp.bfloat16)
    return jnp.concatenate([mixed[h] for h in range(mixed.shape[0])], axis=1)


def chosen(spots, positions):
    return jnp.any(spots[:, None] == positions[None, :], axis=1)


def pick(one_hot, rows):
    return jnp.dot(
        one_hot.astype(jnp.bfloat16), rows, preferred_element_type=jnp.float32
    ).astype(jnp.bfloat16)


def shards(tokens, positions, mask_embed, norm_gain, w_query, w_key, w_value, w_out):
    place = lax.axis_index("tensor")
    rows = tokens.shape[0]
    length = rows * PARTS
    heads = w_query.shape[1] // HD
    relative = jnp.array([m ^ c for c in (0, CORE) for m in BLOCKS], jnp.int32)

    def split_kv(both):
        k_own, v_own, k_other, v_other = (both[:, HALF * i : HALF * (i + 1)] for i in range(4))
        key = (jnp.where(even, k_own, k_other), jnp.where(even, k_other, k_own))
        value = jnp.where(
            even, jnp.concatenate([v_own, v_other], axis=1), jnp.concatenate([v_other, v_own], axis=1)
        )
        return key, value.astype(jnp.bfloat16)

    def dot_kv(x, weights):
        return lax.dot_general(x, weights, (((1,), (1,)), ((), ())), preferred_element_type=jnp.float32)

    def dot_query(x):
        return jnp.dot(x, w_query, preferred_element_type=jnp.float32)

    def turn_query(query, cosine, sine):
        query = query.reshape(-1, heads, HD).transpose(1, 0, 2)
        return turn(query[..., :HALF], query[..., HALF:], cosine[None], sine[None])

    own_spots = place * rows + jnp.arange(rows, dtype=jnp.int32)
    own_masked_0 = chosen(own_spots, positions[0])
    hidden_0 = jnp.where(own_masked_0[:, None], mask_embed[None, :], tokens)
    normed_0 = normalize(hidden_0, norm_gain)
    have = [normed_0[:, first : first + width] for first, width, _ in PIECES]
    got, later = together(step_up(have, 0), (positions, mask_embed, norm_gain, w_key, w_value, place))
    positions, mask_embed, norm_gain, w_key, w_value, place = later
    have = joined(have, got)

    kv_own = jnp.concatenate([w_key.T, w_value.T], axis=0)
    kv_weights = jnp.concatenate([kv_own, swap(kv_own, CORE)], axis=0)
    owners = place ^ relative
    even = place % 2 == 0
    spots = (owners[:, None] * rows + jnp.arange(rows, dtype=jnp.int32)[None, :]).reshape(-1)
    masked_1 = chosen(spots, positions[1])
    own_masked_1 = chosen(own_spots, positions[1])
    every = jnp.arange(length, dtype=jnp.int32)
    every_0 = chosen(every, positions[0])
    every_1 = chosen(every, positions[1])
    fresh = every_0 & ~every_1
    before = every[None, :] < every[:, None]
    fresh_count = jnp.sum(fresh.astype(jnp.int32))
    rank = jnp.where(
        fresh,
        jnp.sum((before & fresh[None, :]).astype(jnp.int32), axis=1),
        fresh_count + jnp.sum((before & (every_0 & every_1)[None, :]).astype(jnp.int32), axis=1),
    )
    rank = jnp.where(every_0, rank, -1)
    share = positions.shape[1] // PARTS
    listed = (owners[:, None] * share + jnp.arange(share, dtype=jnp.int32)[None, :]).reshape(-1)
    list_spots = jnp.sum(jnp.where(rank[None, :] == listed[:, None], every[None, :], 0), axis=1)
    list_fresh = listed < fresh_count
    cosine, sine = turns(spots)
    list_cosine, list_sine = turns(list_spots)
    match = ((spots[:, None] == list_spots[None, :]) & list_fresh[None, :]).astype(jnp.bfloat16)
    own_match = ((own_spots[:, None] == list_spots[None, :]) & list_fresh[None, :]).astype(jnp.bfloat16)
    tables = (kv_weights, masked_1, own_masked_1, cosine, sine, list_cosine, list_sine, match, own_match)
    got, tables = together(step_up(have, 1), tables)
    kv_weights, masked_1, own_masked_1, cosine, sine, list_cosine, list_sine, match, own_match = tables
    have = joined(have, got)

    def kv_pieces(some):
        return [
            dot_kv(block, kv_weights[:, first : first + width])
            for block, (first, width, _) in zip(some, PIECES)
        ]

    mask_normed = normalize(mask_embed[None, :], norm_gain)
    mask_query = dot_query(mask_normed)[0].reshape(heads, 1, HD)
    mask_key, mask_value = split_kv(dot_kv(jnp.broadcast_to(mask_normed, (8, mask_normed.shape[1])), kv_weights))
    mask_key = (mask_key[0][:1], mask_key[1][:1])
    mask_value = mask_value[:1]
    query_0 = turn(mask_query[..., :HALF], mask_query[..., HALF:], list_cosine[None], list_sine[None])
    query_mask = turn(mask_query[..., :HALF], mask_query[..., HALF:], cosine[None], sine[None])
    key_mask = turn(*mask_key, cosine, sine)
    early = kv_pieces(have)
    got, mask_row, early = together(
        step_up(have, 2), (mask_value, query_0, query_mask, key_mask), early
    )
    mask_value, query_0, query_mask, key_mask = mask_row

    late = kv_pieces(got)
    both = sum(
        in_order(jnp.concatenate([one, two], axis=0), order, rows)
        for one, two, (_, _, order) in zip(early, late, PIECES)
    )
    key_own, value_own = split_kv(both)
    key_own = turn(*key_own, cosine[: length // 2], sine[: length // 2])
    pair_own = jnp.concatenate([key_own, value_own], axis=1)
    pair = jnp.concatenate([pair_own, swap(pair_own, CORE)], axis=0)
    key_0, value_0 = pair[:, :HD], pair[:, HD:]
    mixed_0 = attend(query_0, key_0, value_0)
    totals = project(mixed_0, w_out)

    keep, incoming = step_down(totals, 0)
    incoming, have, got = together(incoming, have, got)
    x_own = jnp.concatenate(
        [in_order(block, order, rows) for block, (_, _, order) in zip(joined(have, got), PIECES)], axis=1
    )
    keep, incoming = step_down(added(keep, incoming), 1)
    incoming, x_own = together(incoming, x_own)
    keep, incoming = step_down(added(keep, incoming), 2)
    x_other = swap(x_own, CORE)
    incoming, x_own = together(incoming, x_own)
    sums_0 = added(keep, incoming)

    have = [
        add(mask_embed[None, first : first + width], summed)
        for (first, width, _), summed in zip(PIECES, sums_0)
    ]
    got = together(*step_up(have, 0))
    have = joined(have, got)
    query_own = dot_query(x_own)
    got, query_own, x_other = together(step_up(have, 1), query_own, x_other)
    have = joined(have, got)
    query_tokens = turn_query(jnp.concatenate([query_own, dot_query(x_other)], axis=0), cosine, sine)
    got, query_tokens = together(step_up(have, 2), query_tokens)
    raw = []
    for block, (_, _, order) in zip(joined(have, got), PIECES):
        both_cores = jnp.concatenate([block, swap(block, CORE)], axis=0)
        half = block.shape[0]
        raw.append(
            jnp.concatenate(
                [in_order(both_cores[:half], order, share), in_order(both_cores[half:], order, share)], axis=0
            )
        )
    raw = jnp.concatenate(raw, axis=1)

    normed_1 = normalize(raw, norm_gain)
    key_list, value_list = split_kv(dot_kv(normed_1, kv_weights))
    key_list = turn(*key_list, list_cosine, list_sine)
    query_list = turn_query(dot_query(normed_1), list_cosine, list_sine)
    is_list = jnp.any(match > 0, axis=1)
    moved = pick(match, jnp.concatenate([key_list, value_list] + [query_list[h] for h in range(heads)], axis=1))
    key_1 = jnp.where(masked_1[:, None], key_mask, jnp.where(is_list[:, None], moved[:, :HD], key_0))
    value_1 = jnp.where(masked_1[:, None], mask_value, jnp.where(is_list[:, None], moved[:, HD : 2 * HD], value_0))
    moved_query = jnp.stack([moved[:, HD * (h + 2) : HD * (h + 3)] for h in range(heads)])
    query_1 = jnp.where(
        masked_1[None, :, None],
        query_mask,
        jnp.where(is_list[None, :, None], moved_query, query_tokens),
    )
    mixed_1 = attend(query_1, key_1, value_1)
    totals = project(mixed_1, w_out)
    keep, incoming = step_down(totals, 0)
    own_list = jnp.any(own_match > 0, axis=1)
    hidden_1 = jnp.where(
        own_masked_1[:, None],
        mask_embed[None, :],
        jnp.where(own_list[:, None], pick(own_match, raw), tokens),
    )
    incoming, hidden_1 = together(incoming, hidden_1)
    keep, incoming = step_down(added(keep, incoming), 1)
    incoming = together(*incoming)
    keep, incoming = step_down(added(keep, incoming), 2)
    incoming = together(*incoming)
    summed_1 = jnp.concatenate(added(keep, incoming), axis=1)
    return (hidden_1.astype(jnp.float32) + summed_1.astype(jnp.float32)).astype(jnp.bfloat16)


def solution(mesh):
    placed = (
        P(("dp", "tensor"), None),
        P("dp", None),
        P(),
        P(),
        P(None, "tensor"),
        P(None, "tensor"),
        P(None, "tensor"),
        P("tensor", None),
    )
    return jax.shard_map(
        shards, mesh=mesh, in_specs=placed, out_specs=P(("dp", "tensor"), None), check_vma=False
    )
```

```python
import jax
import jax.numpy as jnp
from jax import lax
from jax.experimental import pallas as pl
from jax.experimental.pallas import tpu as pltpu
from jax.sharding import PartitionSpec as P

HD = 128
HALF = HD // 2
PARTS = 16
CORE, ZED, NEAR, FAR = 1, 2, 4, 12
LINKS = (NEAR, FAR, ZED)
PIECES = (
    (0, 2816, (NEAR, FAR, ZED)),
    (2816, 2816, (FAR, ZED, NEAR)),
    (5632, 2560, (ZED, NEAR, FAR)),
)
CHUNKS = [(first + i * width // 2, width // 2) for first, width, _ in PIECES for i in range(2)]
BLOCKS = [a ^ b ^ c for a in (0, NEAR) for b in (0, FAR) for c in (0, ZED)]


def swap(value, mask):
    return lax.ppermute(value, "tensor", [(i, i ^ mask) for i in range(PARTS)])


def normalize(rows, gain):
    values = rows.astype(jnp.float32)
    scale = lax.rsqrt(jnp.mean(values * values, axis=-1, keepdims=True) + 1e-05)
    return (values * scale * gain.astype(jnp.float32)).astype(jnp.bfloat16)


def turns(spots):
    freq = 500000.0 ** (-(jnp.arange(HALF, dtype=jnp.float32) * 2.0 / HD))
    angle = spots.astype(jnp.float32)[:, None] * freq[None, :]
    return jnp.cos(angle), jnp.sin(angle)


def turn_heads(values, cosine, sine):
    out = []
    for at in range(0, values.shape[1], HD):
        left, right = values[:, at : at + HALF], values[:, at + HALF : at + HD]
        out += [left * cosine - right * sine, right * cosine + left * sine]
    return jnp.concatenate(out, axis=1).astype(jnp.bfloat16)


def together(*values):
    return lax.optimization_barrier(values)


def keys_after(order, steps):
    keys = [0]
    for mask in order[:steps]:
        keys = keys + [key ^ mask for key in keys]
    return keys


def step_up(have, step):
    return [swap(block, order[step]) for block, (_, _, order) in zip(have, PIECES)]


def joined(have, got):
    return [jnp.concatenate(pair, axis=0) for pair in zip(have, got)]


def in_order(blocks, order, rows):
    keys = keys_after(order, 3)
    at = [keys.index(m) * rows for m in BLOCKS]
    return jnp.concatenate([blocks[i : i + rows] for i in at], axis=0)


def add(one, two):
    return (one.astype(jnp.float32) + two.astype(jnp.float32)).astype(jnp.bfloat16)


def step_down(totals, step):
    keep, got = [], []
    for total, (_, _, order) in zip(totals, PIECES):
        left = [mask for mask in LINKS if mask not in order[:step]]
        at = left.index(order[step])
        keep.append(lax.index_in_dim(total, 0, at, keepdims=False))
        got.append(swap(lax.index_in_dim(total, 1, at, keepdims=False), order[step]))
    return keep, got


def added(keep, got):
    return [add(one, two) for one, two in zip(keep, got)]


def with_heads(query, key, value, mixed):
    rows, columns = query.shape
    tile = rows // 2
    for h in range(columns // HD):
        for at in range(0, rows, tile):
            scores = lax.dot_general(
                query[at : at + tile, HD * h : HD * (h + 1)],
                key,
                (((1,), (1,)), ((), ())),
                preferred_element_type=jnp.float32,
            ) * HD ** (-0.5)
            weights = jnp.exp(scores - jnp.max(scores, axis=-1, keepdims=True))
            probs = weights * (1.0 / jnp.sum(weights, axis=-1, keepdims=True))
            mixed[at : at + tile, HD * h : HD * (h + 1)] = jnp.dot(
                probs.astype(jnp.bfloat16), value, preferred_element_type=jnp.float32
            ).astype(jnp.bfloat16)


def fetch_out(out_hbm, out_here, sems):
    copies = []
    for i, (first, width) in enumerate(CHUNKS):
        copy = pltpu.make_async_copy(
            out_hbm.at[:, pl.ds(first, width)], out_here.at[:, pl.ds(first, width)], sems.at[i]
        )
        copy.start()
        copies.append(copy)
    return copies


def project_out(mixed, out_here, copies, outs):
    half = mixed.shape[0] // 2
    for i, (first, width) in enumerate(CHUNKS):
        copies[i].wait()
        weights = out_here[:, first : first + width]
        at = (i % 2) * width
        for side in range(2):
            outs[2 * (i // 2) + side][:, at : at + width] = jnp.dot(
                mixed[half * side : half * (side + 1), :], weights, preferred_element_type=jnp.float32
            ).astype(jnp.bfloat16)


def first_kernel(query, pair, out_hbm, *rest):
    outs, (out_here, mixed, sems) = rest[:6], rest[6:]
    copies = fetch_out(out_hbm, out_here, sems)
    with_heads(query, pair[:, :HD], pair[:, HD:], mixed)
    project_out(mixed, out_here, copies, outs)


def second_kernel(*refs):
    raw, refs = refs[:6], refs[6:]
    gain, cosine, sine, match, base, query_hbm, kv_hbm, out_hbm = refs[:8]
    outs, refs = refs[8:14], refs[14:]
    query_here, kv_here, out_here, normed, moving, placed, mixed, sems = refs
    half = raw[0].shape[0]
    width_all = gain.shape[1]
    arrivals = []
    for i, (first, width) in enumerate(CHUNKS):
        rows, columns = pl.ds(first, width), pl.ds(first, width)
        one = pltpu.make_async_copy(query_hbm.at[rows, :], query_here.at[rows, :], sems.at[6 + i])
        two = pltpu.make_async_copy(kv_hbm.at[:, columns], kv_here.at[:, columns], sems.at[12 + i])
        one.start()
        two.start()
        arrivals.append((one, two))
    copies = fetch_out(out_hbm, out_here, sems)
    scales = []
    for side in range(2):
        squares = jnp.zeros((half, HD), jnp.float32)
        for piece in range(3):
            ref = raw[2 * piece + side]

            def add_squares(i, squares, ref=ref):
                values = ref[:, pl.ds(pl.multiple_of(i * HD, HD), HD)].astype(jnp.float32)
                return squares + values * values

            squares = lax.fori_loop(0, ref.shape[1] // HD, add_squares, squares, unroll=2)
        mean = jnp.sum(squares, axis=-1, keepdims=True) * (1.0 / width_all)
        scales.append(lax.rsqrt(mean + 1e-05))
    queries = jnp.zeros((2 * half, query_here.shape[1]), jnp.float32)
    pairs = jnp.zeros((2 * half, kv_here.shape[0]), jnp.float32)
    for i, (first, width) in enumerate(CHUNKS):
        at = (i % 2) * width
        for side in range(2):
            values = raw[2 * (i // 2) + side][:, at : at + width].astype(jnp.float32)
            normed[half * side : half * (side + 1), :width] = (
                values * scales[side] * gain[:, first : first + width]
            ).astype(jnp.bfloat16)
        some = normed[:, :width]
        for copy in arrivals[i]:
            copy.wait()
        queries += jnp.dot(some, query_here[first : first + width, :], preferred_element_type=jnp.float32)
        pairs += lax.dot_general(
            some, kv_here[:, first : first + width], (((1,), (1,)), ((), ())), preferred_element_type=jnp.float32
        )

    def turned(values):
        return (values * cosine[...] + pltpu.roll(values, HALF, 1) * sine[...]).astype(jnp.bfloat16)

    moving[:, :HD] = turned(pairs[:, :HD])
    moving[:, HD : 2 * HD] = pairs[:, HD:].astype(jnp.bfloat16)
    for h in range(queries.shape[1] // HD):
        moving[:, HD * (h + 2) : HD * (h + 3)] = turned(queries[:, HD * h : HD * (h + 1)])
    placed[...] = base[...] + jnp.dot(
        match[...], moving[...], preferred_element_type=jnp.float32
    ).astype(jnp.bfloat16)
    with_heads(placed.at[:, 2 * HD :], placed[:, :HD], placed[:, HD : 2 * HD], mixed)
    project_out(mixed, out_here, copies, outs)


def call_kernel(kernel, operands, in_hbm, rows, w_out, scratch, flops):
    count = len(operands)
    bf16 = jnp.bfloat16
    widths = [width for _, width, _ in PIECES for _ in range(2)]
    outs = pl.pallas_call(
        kernel,
        out_shape=[jax.ShapeDtypeStruct((rows // 2, width), bf16) for width in widths],
        in_specs=[pl.BlockSpec(memory_space=pltpu.VMEM)] * count + [pl.BlockSpec(memory_space=pl.ANY)] * len(in_hbm),
        out_specs=[pl.BlockSpec(memory_space=pltpu.VMEM)] * 6,
        scratch_shapes=scratch,
        compiler_params=pltpu.CompilerParams(vmem_limit_bytes=52 * 2**20),
        cost_estimate=pl.CostEstimate(flops=flops, bytes_accessed=2 * w_out.size, transcendentals=0),
    )(*operands, *in_hbm)
    return [(outs[2 * i], outs[2 * i + 1]) for i in range(3)]


def chosen(spots, positions):
    return jnp.any(spots[:, None] == positions[None, :], axis=1)


def pick(one_hot, rows):
    return jnp.dot(
        one_hot.astype(jnp.bfloat16), rows, preferred_element_type=jnp.float32
    ).astype(jnp.bfloat16)


def shards(tokens, positions, mask_embed, norm_gain, w_query, w_key, w_value, w_out):
    place = lax.axis_index("tensor")
    rows = tokens.shape[0]
    length = rows * PARTS
    relative = jnp.array([m ^ c for c in (0, CORE) for m in BLOCKS], jnp.int32)

    def dot_kv(x, weights):
        return lax.dot_general(x, weights, (((1,), (1,)), ((), ())), preferred_element_type=jnp.float32)

    own_spots = place * rows + jnp.arange(rows, dtype=jnp.int32)
    own_masked_0 = chosen(own_spots, positions[0])
    hidden_0 = jnp.where(own_masked_0[:, None], mask_embed[None, :], tokens)
    normed_0 = normalize(hidden_0, norm_gain)
    have = [normed_0[:, first : first + width] for first, width, _ in PIECES]
    got, later = together(step_up(have, 0), (positions, w_key, w_value, place))
    positions, w_key, w_value, place = later
    have = joined(have, got)

    even = place % 2 == 0
    kv_own = jnp.concatenate([w_key.T, w_value.T], axis=0)
    kv_other = swap(kv_own, CORE)
    low, high = jnp.where(even, kv_own, kv_other), jnp.where(even, kv_other, kv_own)
    kv_weights = jnp.concatenate([low[:HALF], high[:HALF], low[HALF:], high[HALF:]], axis=0)
    owners = place ^ relative
    spots = (owners[:, None] * rows + jnp.arange(rows, dtype=jnp.int32)[None, :]).reshape(-1)
    masked_1 = chosen(spots, positions[1])
    own_masked_1 = chosen(own_spots, positions[1])
    every = jnp.arange(length, dtype=jnp.int32)
    every_0 = chosen(every, positions[0])
    every_1 = chosen(every, positions[1])
    fresh = every_0 & ~every_1
    before = every[None, :] < every[:, None]
    fresh_count = jnp.sum(fresh.astype(jnp.int32))
    rank = jnp.where(
        fresh,
        jnp.sum((before & fresh[None, :]).astype(jnp.int32), axis=1),
        fresh_count + jnp.sum((before & (every_0 & every_1)[None, :]).astype(jnp.int32), axis=1),
    )
    rank = jnp.where(every_0, rank, -1)
    count = positions.shape[1]
    listed = (jnp.arange(count, dtype=jnp.int32) + (place % 2) * (count // 2)) % count
    list_spots = jnp.sum(jnp.where(rank[None, :] == listed[:, None], every[None, :], 0), axis=1)
    list_fresh = listed < fresh_count
    cosine, sine = turns(spots)
    list_cosine, list_sine = turns(list_spots)
    match = ((spots[:, None] == list_spots[None, :]) & list_fresh[None, :]).astype(jnp.bfloat16)
    own_match = ((own_spots[:, None] == list_spots[None, :]) & list_fresh[None, :]).astype(jnp.bfloat16)
    tables = (kv_weights, masked_1, own_masked_1, cosine, sine, list_cosine, list_sine, match, own_match)
    got, tables, mask_embed, norm_gain = together(step_up(have, 1), tables, mask_embed, norm_gain)
    kv_weights, masked_1, own_masked_1, cosine, sine, list_cosine, list_sine, match, own_match = tables
    have = joined(have, got)

    def kv_pieces(some):
        return [
            dot_kv(block, kv_weights[:, first : first + width])
            for block, (first, width, _) in zip(some, PIECES)
        ]

    mask_normed = normalize(mask_embed[None, :], norm_gain)
    mask_query = jnp.dot(mask_normed, w_query, preferred_element_type=jnp.float32)
    mask_pair = dot_kv(jnp.broadcast_to(mask_normed, (8, mask_normed.shape[1])), kv_weights)[:1]
    query_0 = turn_heads(mask_query, list_cosine, list_sine)
    base_mask = jnp.concatenate(
        [
            turn_heads(mask_pair[:, :HD], cosine, sine),
            jnp.broadcast_to(mask_pair[:, HD:].astype(jnp.bfloat16), (length, HD)),
            turn_heads(mask_query, cosine, sine),
        ],
        axis=1,
    )
    early = kv_pieces(have)
    got, query_0, base_mask, early = together(step_up(have, 2), query_0, base_mask, early)

    late_rows = got
    late = kv_pieces(got)
    both = sum(
        in_order(jnp.concatenate([one, two], axis=0), order, rows)
        for one, two, (_, _, order) in zip(early, late, PIECES)
    )
    pair_own = jnp.concatenate(
        [
            turn_heads(both[:, :HD], cosine[: length // 2], sine[: length // 2]),
            both[:, HD:].astype(jnp.bfloat16),
        ],
        axis=1,
    )
    pair = jnp.concatenate([pair_own, swap(pair_own, CORE)], axis=0)
    columns = w_query.shape[1]
    bf16 = jnp.bfloat16
    products = call_kernel(
        first_kernel,
        [query_0, pair],
        [w_out],
        count,
        w_out,
        [
            pltpu.VMEM(w_out.shape, bf16),
            pltpu.VMEM((count, columns), bf16),
            pltpu.SemaphoreType.DMA((6,)),
        ],
        2 * count * w_out.size,
    )

    bits = {NEAR: ((place >> 2) ^ (place >> 3)) % 2 == 1, FAR: (place >> 3) % 2 == 1, ZED: (place >> 1) % 2 == 1}
    sides = [bits[order[0]] for _, _, order in PIECES]
    totals = [add(keep, swap(send, CORE)) for keep, send in products]
    keep, send = [], []
    for total, side in zip(totals, sides):
        middle = total.shape[1] // 2
        left, right = total[:, :middle], total[:, middle:]
        keep.append(jnp.where(side, right, left))
        send.append(jnp.where(side, left, right))
    got = [swap(block, order[0]) for block, (_, _, order) in zip(send, PIECES)]
    x_own = joined(have, late_rows)
    got, x_own = together(got, x_own)
    totals = added(keep, got)

    def queries_of(x):
        return sum(
            in_order(
                jnp.dot(block, w_query[first : first + width], preferred_element_type=jnp.float32), order, rows
            )
            for block, (first, width, order) in zip(x, PIECES)
        )

    x_other = [swap(block, CORE) for block in x_own]
    got, query_own, x_other = together(step_up(totals, 1), queries_of(x_own), x_other)
    totals = added(totals, got)
    got, query_other = together(step_up(totals, 2), queries_of(x_other))
    totals = added(totals, got)
    states = []
    for (first, width, _), total, side in zip(PIECES, totals, sides):
        row = mask_embed[None, first : first + width]
        middle = width // 2
        states.append(add(jnp.where(side, row[:, middle:], row[:, :middle]), total))
    is_list = jnp.any(match > 0, axis=1)[:, None]
    base_tokens = jnp.concatenate(
        [pair, turn_heads(jnp.concatenate([query_own, query_other], axis=0), cosine, sine)], axis=1
    )
    base = jnp.where(masked_1[:, None], base_mask, jnp.where(is_list, jnp.zeros_like(base_tokens), base_tokens))
    got, base = together(step_up(states, 0), base)
    raw = []
    for state, block, side in zip(states, got, sides):
        raw.append(
            jnp.where(
                side, jnp.concatenate([block, state], axis=1), jnp.concatenate([state, block], axis=1)
            )
        )
    raw = [(block, swap(block, CORE)) for block in raw]

    list_turns = (
        jnp.concatenate([list_cosine, list_cosine], axis=1),
        jnp.concatenate([-list_sine, list_sine], axis=1),
    )
    operands = [half for both in raw for half in both]
    operands += [norm_gain[None, :].astype(jnp.float32), *list_turns, match, base]
    products = call_kernel(
        second_kernel,
        operands,
        [w_query, kv_weights, w_out],
        length,
        w_out,
        [
            pltpu.VMEM(w_query.shape, bf16),
            pltpu.VMEM(kv_weights.shape, bf16),
            pltpu.VMEM(w_out.shape, bf16),
            pltpu.VMEM((count, CHUNKS[0][1]), bf16),
            pltpu.VMEM((count, columns + 2 * HD), bf16),
            pltpu.VMEM((length, columns + 2 * HD), bf16),
            pltpu.VMEM((length, columns), bf16),
            pltpu.SemaphoreType.DMA((18,)),
        ],
        2 * (2 * length + count) * w_out.size,
    )
    totals = [add(keep, swap(send, CORE)).reshape(2, 2, 2, rows, keep.shape[1]) for keep, send in products]
    keep, incoming = step_down(totals, 0)
    own_list = jnp.any(own_match > 0, axis=1)
    middle = count // 2
    states = jnp.concatenate(
        [pick(own_match[:, :middle], one) + pick(own_match[:, middle:], two) for one, two in raw], axis=1
    )
    hidden_1 = jnp.where(
        own_masked_1[:, None], mask_embed[None, :], jnp.where(own_list[:, None], states, tokens)
    )
    incoming, hidden_1 = together(incoming, hidden_1)
    keep, incoming = step_down(added(keep, incoming), 1)
    incoming = together(*incoming)
    keep, incoming = step_down(added(keep, incoming), 2)
    incoming = together(*incoming)
    summed_1 = jnp.concatenate(added(keep, incoming), axis=1)
    return (hidden_1.astype(jnp.float32) + summed_1.astype(jnp.float32)).astype(jnp.bfloat16)


def solution(mesh):
    placed = (
        P(("dp", "tensor"), None),
        P("dp", None),
        P(),
        P(),
        P(None, "tensor"),
        P(None, "tensor"),
        P(None, "tensor"),
        P("tensor", None),
    )
    return jax.shard_map(
        shards, mesh=mesh, in_specs=placed, out_specs=P(("dp", "tensor"), None), check_vma=False
    )
```

```python
import jax
import jax.numpy as jnp
from jax import lax
from jax.experimental import pallas as pl
from jax.experimental.pallas import tpu as pltpu
from jax.sharding import PartitionSpec as P

HD = 128
HALF = HD // 2
PARTS = 16
CORE, ZED, NEAR, FAR = 1, 2, 4, 12
LINKS = (NEAR, FAR, ZED)
PIECES = (
    (0, 2816, (NEAR, FAR, ZED)),
    (2816, 2816, (FAR, ZED, NEAR)),
    (5632, 2560, (ZED, NEAR, FAR)),
)
CHUNKS = [(first + i * width // 2, width // 2) for first, width, _ in PIECES for i in range(2)]
BLOCKS = [a ^ b ^ c for a in (0, NEAR) for b in (0, FAR) for c in (0, ZED)]


def swap(value, mask):
    return lax.ppermute(value, "tensor", [(i, i ^ mask) for i in range(PARTS)])


def normalize(rows, gain):
    values = rows.astype(jnp.float32)
    scale = lax.rsqrt(jnp.mean(values * values, axis=-1, keepdims=True) + 1e-05)
    return (values * scale * gain.astype(jnp.float32)).astype(jnp.bfloat16)


def turn_heads(values, cosine, sine):
    out = []
    for at in range(0, values.shape[1], HD):
        left, right = values[:, at : at + HALF], values[:, at + HALF : at + HD]
        out += [left * cosine - right * sine, right * cosine + left * sine]
    return jnp.concatenate(out, axis=1).astype(jnp.bfloat16)


def together(*values):
    return lax.optimization_barrier(values)


def keys_after(order, steps):
    keys = [0]
    for mask in order[:steps]:
        keys = keys + [key ^ mask for key in keys]
    return keys


def step_up(have, step):
    return [swap(block, order[step]) for block, (_, _, order) in zip(have, PIECES)]


def in_order(blocks, order, rows):
    keys = keys_after(order, 3)
    at = [keys.index(m) * rows for m in BLOCKS]
    return jnp.concatenate([blocks[i : i + rows] for i in at], axis=0)


def add(one, two):
    return (one.astype(jnp.float32) + two.astype(jnp.float32)).astype(jnp.bfloat16)


def step_down(totals, step):
    keep, got = [], []
    for total, (_, _, order) in zip(totals, PIECES):
        left = [mask for mask in LINKS if mask not in order[:step]]
        at = left.index(order[step])
        keep.append(lax.index_in_dim(total, 0, at, keepdims=False))
        got.append(swap(lax.index_in_dim(total, 1, at, keepdims=False), order[step]))
    return keep, got


def added(keep, got):
    return [add(one, two) for one, two in zip(keep, got)]


def with_heads(query, key, value, mixed):
    rows, columns = query.shape
    tile = rows // 2
    for h in range(columns // HD):
        for at in range(0, rows, tile):
            scores = lax.dot_general(
                query[at : at + tile, HD * h : HD * (h + 1)],
                key,
                (((1,), (1,)), ((), ())),
                preferred_element_type=jnp.float32,
            ) * HD ** (-0.5)
            weights = jnp.exp(scores - jnp.max(scores, axis=-1, keepdims=True))
            probs = weights * (1.0 / jnp.sum(weights, axis=-1, keepdims=True))
            mixed[at : at + tile, HD * h : HD * (h + 1)] = jnp.dot(
                probs.astype(jnp.bfloat16), value, preferred_element_type=jnp.float32
            ).astype(jnp.bfloat16)


def project_out(mixed, out_here, outs):
    half = mixed.shape[0] // 2
    for i, (first, width) in enumerate(CHUNKS):
        weights = out_here[:, first : first + width]
        at = (i % 2) * width
        for side in range(2):
            outs[2 * (i // 2) + side][:, at : at + width] = jnp.dot(
                mixed[half * side : half * (side + 1), :], weights, preferred_element_type=jnp.float32
            ).astype(jnp.bfloat16)


def first_kernel(query, pair, out_here, *rest):
    outs, (mixed,) = rest[:6], rest[6:]
    with_heads(query, pair[:, :HD], pair[:, HD:], mixed)
    project_out(mixed, out_here, outs)


def turned(values, cosine, sine):
    return (values * cosine + pltpu.roll(values, HALF, 1) * sine).astype(jnp.bfloat16)


def second_kernel(*refs):
    raw, refs = refs[:6], refs[6:]
    gain, cosine, sine, match, base, query_here, kv_here, out_here = refs[:8]
    outs, refs = refs[8:14], refs[14:]
    normed, moving, placed, mixed = refs
    half = raw[0].shape[0]
    width_all = gain.shape[1]
    scales = []
    for side in range(2):
        squares = jnp.zeros((half, HD), jnp.float32)
        for piece in range(3):
            ref = raw[2 * piece + side]

            def add_squares(i, squares, ref=ref):
                values = ref[:, pl.ds(pl.multiple_of(i * HD, HD), HD)].astype(jnp.float32)
                return squares + values * values

            squares = lax.fori_loop(0, ref.shape[1] // HD, add_squares, squares, unroll=2)
        mean = jnp.sum(squares, axis=-1, keepdims=True) * (1.0 / width_all)
        scales.append(lax.rsqrt(mean + 1e-05))
    queries = jnp.zeros((2 * half, query_here.shape[1]), jnp.float32)
    pairs = jnp.zeros((2 * half, kv_here.shape[0]), jnp.float32)
    for i, (first, width) in enumerate(CHUNKS):
        at = (i % 2) * width
        for side in range(2):
            values = raw[2 * (i // 2) + side][:, at : at + width].astype(jnp.float32)
            normed[half * side : half * (side + 1), :width] = (
                values * scales[side] * gain[:, first : first + width]
            ).astype(jnp.bfloat16)
        some = normed[:, :width]
        queries += jnp.dot(some, query_here[first : first + width, :], preferred_element_type=jnp.float32)
        pairs += dot_rows(some, kv_here[:, first : first + width])
    moving[:, :HD] = turned(pairs[:, :HD], cosine[...], sine[...])
    moving[:, HD : 2 * HD] = pairs[:, HD:].astype(jnp.bfloat16)
    for h in range(queries.shape[1] // HD):
        moving[:, HD * (h + 2) : HD * (h + 3)] = turned(queries[:, HD * h : HD * (h + 1)], cosine[...], sine[...])
    placed[...] = base[...] + jnp.dot(
        match[...], moving[...], preferred_element_type=jnp.float32
    ).astype(jnp.bfloat16)
    with_heads(placed.at[:, 2 * HD :], placed[:, :HD], placed[:, HD : 2 * HD], mixed)
    project_out(mixed, out_here, outs)


def dot_rows(x, weights):
    return lax.dot_general(x, weights, (((1,), (1,)), ((), ())), preferred_element_type=jnp.float32)


def call_kernel(kernel, operands, outs, scratch=(), mib=16, scalars=0):
    places = [pltpu.VMEM] * (len(operands) - scalars) + [pltpu.SMEM] * scalars
    return pl.pallas_call(
        kernel,
        out_shape=[jax.ShapeDtypeStruct(*out) for out in outs],
        in_specs=[pl.BlockSpec(memory_space=place) for place in places],
        out_specs=[pl.BlockSpec(memory_space=pltpu.VMEM)] * len(outs),
        scratch_shapes=list(scratch),
        compiler_params=pltpu.CompilerParams(vmem_limit_bytes=mib * 2**20),
        cost_estimate=pl.CostEstimate(flops=1000000, bytes_accessed=100000, transcendentals=0),
    )(*operands)


def call_projected(kernel, operands, rows, scratch, mib):
    outs = [((rows // 2, width), jnp.bfloat16) for _, width, _ in PIECES for _ in range(2)]
    outs = call_kernel(kernel, operands, outs, scratch, mib)
    return [(outs[2 * i], outs[2 * i + 1]) for i in range(3)]


def join_kernel(*refs):
    for i in range(3):
        have, got, out = refs[i], refs[3 + i], refs[6 + i]
        rows = have.shape[0]
        out[:rows, :] = have[...]
        out[rows:, :] = got[...]


def joined(have, got):
    outs = [((2 * block.shape[0], block.shape[1]), block.dtype) for block in have]
    return call_kernel(join_kernel, [*have, *got], outs, mib=12)


def weight_rows_kernel(key, value, other_key, other_value, place, out):
    even = place[0, 0] % 2 == 0

    @pl.when(even)
    def _():
        out[:HALF, :] = key[...]
        out[HALF : 2 * HALF, :] = other_key[...]
        out[2 * HALF : 3 * HALF, :] = value[...]
        out[3 * HALF :, :] = other_value[...]

    @pl.when(jnp.logical_not(even))
    def _():
        out[:HALF, :] = other_key[...]
        out[HALF : 2 * HALF, :] = key[...]
        out[2 * HALF : 3 * HALF, :] = other_value[...]
        out[3 * HALF :, :] = value[...]


def table_kernel(one, two, ones_across, twos_across, freq, spots, listed, cosine, sine, list_cosine, list_sine, match, flags):
    f32, bf16 = jnp.float32, jnp.bfloat16
    count = one.shape[0]
    stale = jnp.max(jnp.where(two[...] == ones_across[...], 1.0, 0.0), axis=0, keepdims=True)
    fresh = 1.0 - stale
    row = lax.broadcasted_iota(jnp.int32, (count, count), 0)
    column = lax.broadcasted_iota(jnp.int32, (count, count), 1)
    before = jnp.where(row < column, 1.0, 0.0).astype(bf16)

    def ahead(flag):
        wide = jnp.broadcast_to(flag, (16, count)).astype(bf16)
        return jnp.dot(wide, before, preferred_element_type=f32)[:1]

    rank = jnp.where(fresh > 0, ahead(fresh), jnp.sum(fresh, axis=1, keepdims=True) + ahead(stale))
    spot = jnp.where(listed[...].astype(f32) == rank, 1.0, 0.0)
    list_spots = jnp.sum(spot * ones_across[...].astype(f32), axis=1, keepdims=True)
    here = jnp.where((spots[...] == ones_across[...]) & (fresh > 0), 1.0, 0.0)
    match[...] = dot_rows(here.astype(bf16), spot.astype(bf16)).astype(bf16)
    is_list = jnp.max(here, axis=1, keepdims=True)
    masked_1 = jnp.max(jnp.where(spots[...] == twos_across[...], 1.0, 0.0), axis=1, keepdims=True)
    lane = lax.broadcasted_iota(jnp.int32, (spots.shape[0], HD), 1)
    flags[...] = jnp.where(lane == 0, masked_1, is_list)
    sign = jnp.where(lax.broadcasted_iota(jnp.int32, (1, HD), 1) < HALF, -1.0, 1.0)
    angle = spots[...].astype(f32) * freq[...]
    cosine[...] = jnp.cos(angle)
    sine[...] = jnp.sin(angle) * sign
    angle = list_spots * freq[...]
    list_cosine[...] = jnp.cos(angle)
    list_sine[...] = jnp.sin(angle) * sign


def mask_kernel(embed, gain, query_here, kv_here, cosine, sine, list_cosine, list_sine, query, base):
    values = embed[...].astype(jnp.float32)
    mean = jnp.sum(values * values, axis=-1, keepdims=True) * (1.0 / embed.shape[1])
    row = (values * lax.rsqrt(mean + 1e-05) * gain[...]).astype(jnp.bfloat16)
    row = jnp.broadcast_to(row, (16, row.shape[1]))
    queries = jnp.dot(row, query_here[...], preferred_element_type=jnp.float32)[:1]
    pairs = dot_rows(row, kv_here[...])[:1]
    length = base.shape[0]
    base[:, :HD] = turned(jnp.broadcast_to(pairs[:, :HD], (length, HD)), cosine[...], sine[...])
    base[:, HD : 2 * HD] = jnp.broadcast_to(pairs[:, HD:], (length, HD)).astype(jnp.bfloat16)
    for at in range(0, queries.shape[1], HD):
        some = queries[:, at : at + HD]
        base[:, 2 * HD + at : 3 * HD + at] = turned(jnp.broadcast_to(some, (length, HD)), cosine[...], sine[...])
        query[:, at : at + HD] = turned(
            jnp.broadcast_to(some, (query.shape[0], HD)), list_cosine[...], list_sine[...]
        )


def add_pairs(pieces, kv_here, total, low, fresh):
    rows = total.shape[0] // 8
    for piece, (first, width, order) in zip(pieces, PIECES):
        product = dot_rows(piece[...], kv_here[:, first : first + width])
        for i, key in enumerate(keys_after(order, 3)[low : low + 4]):
            at = BLOCKS.index(key) * rows
            some = product[i * rows : (i + 1) * rows]
            if key in fresh:
                fresh.remove(key)
                total[at : at + rows, :] = some
            else:
                total[at : at + rows, :] += some


def early_kernel(one, two, three, kv_here, total):
    fresh = set(BLOCKS)
    add_pairs((one, two, three), kv_here, total, 0, fresh)
    rows = total.shape[0] // 8
    for key in fresh:
        at = BLOCKS.index(key) * rows
        total[at : at + rows, :] = jnp.zeros((rows, total.shape[1]), jnp.float32)


def late_kernel(one, two, three, kv_here, early, cosine, sine, out, total):
    total[...] = early[...]
    add_pairs((one, two, three), kv_here, total, 4, set())
    rows = total.shape[0]
    out[:, :HD] = turned(total[:, :HD], cosine[:rows, :], sine[:rows, :])
    out[:, HD:] = total[:, HD:].astype(jnp.bfloat16)


def chosen(spots, positions):
    return jnp.any(spots[:, None] == positions[None, :], axis=1)


def pick(one_hot, rows):
    return jnp.dot(
        one_hot.astype(jnp.bfloat16), rows, preferred_element_type=jnp.float32
    ).astype(jnp.bfloat16)


def shards(tokens, positions, mask_embed, norm_gain, w_query, w_key, w_value, w_out):
    place = lax.axis_index("tensor")
    rows = tokens.shape[0]
    length = rows * PARTS
    relative = jnp.array([m ^ c for c in (0, CORE) for m in BLOCKS], jnp.int32)

    own_spots = place * rows + jnp.arange(rows, dtype=jnp.int32)
    own_masked_0 = chosen(own_spots, positions[0])
    hidden_0 = jnp.where(own_masked_0[:, None], mask_embed[None, :], tokens)
    normed_0 = normalize(hidden_0, norm_gain)
    have = [normed_0[:, first : first + width] for first, width, _ in PIECES]
    key_rows, value_rows = w_key.T, w_value.T
    got, later, key_rows, value_rows = together(
        step_up(have, 0), (positions, place), key_rows, value_rows
    )
    positions, place = later
    have = joined(have, got)

    f32, bf16 = jnp.float32, jnp.bfloat16
    count, columns = positions.shape[1], w_query.shape[1]
    other_key, other_value = swap(key_rows, CORE), swap(value_rows, CORE)
    owners = place ^ relative
    spots = (owners[:, None] * rows + jnp.arange(rows, dtype=jnp.int32)[None, :]).reshape(-1, 1)
    listed = (jnp.arange(count, dtype=jnp.int32) + (place % 2) * (count // 2)) % count
    freq = 500000.0 ** (-(jnp.arange(HD, dtype=f32) % HALF * 2.0 / HD))
    cosine, sine, list_cosine, list_sine, match, flags = call_kernel(
        table_kernel,
        [positions[0][:, None], positions[1][:, None], positions[:1], positions[1:], freq[None], spots, listed[:, None]],
        [((length, HD), f32)] * 2 + [((count, HD), f32)] * 2 + [((length, count), bf16), ((length, HD), f32)],
    )
    (kv_weights,) = call_kernel(
        weight_rows_kernel,
        [key_rows, value_rows, other_key, other_value, place.reshape(1, 1)],
        [((4 * HALF, key_rows.shape[1]), bf16)],
        scalars=1,
    )
    tables = (kv_weights, cosine, sine, list_cosine, list_sine, match, flags)
    got, tables, mask_embed, norm_gain = together(step_up(have, 1), tables, mask_embed, norm_gain)
    kv_weights, cosine, sine, list_cosine, list_sine, match, flags = tables
    have = joined(have, got)

    gain = norm_gain[None, :].astype(f32)
    query_0, base_mask = call_kernel(
        mask_kernel,
        [mask_embed[None, :], gain, w_query, kv_weights, cosine, sine, list_cosine, list_sine],
        [((count, columns), bf16), ((length, columns + 2 * HD), bf16)],
    )
    (early,) = call_kernel(early_kernel, [*have, kv_weights], [((length // 2, 2 * HD), f32)])
    got, query_0, base_mask, early = together(step_up(have, 2), query_0, base_mask, early)

    (pair_own,) = call_kernel(
        late_kernel,
        [*got, kv_weights, early, cosine, sine],
        [((length // 2, 2 * HD), bf16)],
        [pltpu.VMEM((length // 2, 2 * HD), f32)],
    )
    x_own = joined(have, got)
    pair_other, x_own = together(swap(pair_own, CORE), x_own)
    pair = jnp.concatenate([pair_own, pair_other], axis=0)
    x_other = [swap(block, CORE) for block in x_own]
    products = call_projected(
        first_kernel, [query_0, pair, w_out], count, [pltpu.VMEM((count, columns), bf16)], 12
    )
    products, x_other = together(products, x_other)

    def queries_of(x):
        return sum(
            in_order(
                jnp.dot(block, w_query[first : first + width], preferred_element_type=jnp.float32), order, rows
            )
            for block, (first, width, order) in zip(x, PIECES)
        )

    bits = {NEAR: ((place >> 2) ^ (place >> 3)) % 2 == 1, FAR: (place >> 3) % 2 == 1, ZED: (place >> 1) % 2 == 1}
    sides = [bits[order[0]] for _, _, order in PIECES]
    totals = [add(keep, swap(send, CORE)) for keep, send in products]
    keep, send = [], []
    for total, side in zip(totals, sides):
        middle = total.shape[1] // 2
        left, right = total[:, :middle], total[:, middle:]
        keep.append(jnp.where(side, right, left))
        send.append(jnp.where(side, left, right))
    got = [swap(block, order[0]) for block, (_, _, order) in zip(send, PIECES)]

    got, query_own = together(got, queries_of(x_own))
    totals = added(keep, got)
    got = together(*step_up(totals, 1))
    totals = added(totals, got)
    got, query_other = together(step_up(totals, 2), queries_of(x_other))
    totals = added(totals, got)
    states = []
    for (first, width, _), total, side in zip(PIECES, totals, sides):
        row = mask_embed[None, first : first + width]
        middle = width // 2
        states.append(add(jnp.where(side, row[:, middle:], row[:, :middle]), total))
    masked_1, is_list = flags[:, :1] > 0, flags[:, 1:2] > 0
    base_tokens = jnp.concatenate(
        [pair, turn_heads(jnp.concatenate([query_own, query_other], axis=0), cosine[:, :HALF], sine[:, HALF:])], axis=1
    )
    base = jnp.where(masked_1, base_mask, jnp.where(is_list, jnp.zeros_like(base_tokens), base_tokens))
    got, base = together(step_up(states, 0), base)
    raw = []
    for state, block, side in zip(states, got, sides):
        raw.append(
            jnp.where(
                side, jnp.concatenate([block, state], axis=1), jnp.concatenate([state, block], axis=1)
            )
        )
    raw = [(block, swap(block, CORE)) for block in raw]

    operands = [half for both in raw for half in both]
    operands += [gain, list_cosine, list_sine, match, base, w_query, kv_weights, w_out]
    products = call_projected(
        second_kernel,
        operands,
        length,
        [
            pltpu.VMEM((count, CHUNKS[0][1]), bf16),
            pltpu.VMEM((count, columns + 2 * HD), bf16),
            pltpu.VMEM((length, columns + 2 * HD), bf16),
            pltpu.VMEM((length, columns), bf16),
        ],
        16,
    )
    totals = [add(keep, swap(send, CORE)).reshape(2, 2, 2, rows, keep.shape[1]) for keep, send in products]
    keep, incoming = step_down(totals, 0)
    own_match = match[:rows]
    middle = count // 2
    states = jnp.concatenate(
        [pick(own_match[:, :middle], one) + pick(own_match[:, middle:], two) for one, two in raw], axis=1
    )
    hidden_1 = jnp.where(
        masked_1[:rows], mask_embed[None, :], jnp.where(is_list[:rows], states, tokens)
    )
    incoming, hidden_1 = together(incoming, hidden_1)
    keep, incoming = step_down(added(keep, incoming), 1)
    incoming = together(*incoming)
    keep, incoming = step_down(added(keep, incoming), 2)
    incoming = together(*incoming)
    summed_1 = jnp.concatenate(added(keep, incoming), axis=1)
    return (hidden_1.astype(jnp.float32) + summed_1.astype(jnp.float32)).astype(jnp.bfloat16)


def solution(mesh):
    placed = (
        P(("dp", "tensor"), None),
        P("dp", None),
        P(),
        P(),
        P(None, "tensor"),
        P(None, "tensor"),
        P(None, "tensor"),
        P("tensor", None),
    )
    return jax.shard_map(
        shards, mesh=mesh, in_specs=placed, out_specs=P(("dp", "tensor"), None), check_vma=False
    )
```

```python
import jax
import jax.numpy as jnp
from jax import lax
from jax.experimental import pallas as pl
from jax.experimental.pallas import tpu as pltpu
from jax.sharding import PartitionSpec as P

HD = 128
HALF = HD // 2
PARTS = 16
CORE, ZED, NEAR, FAR = 1, 2, 4, 12
LINKS = (NEAR, FAR, ZED)
PIECES = (
    (0, 2816, (NEAR, FAR, ZED)),
    (2816, 2816, (FAR, ZED, NEAR)),
    (5632, 2560, (ZED, NEAR, FAR)),
)
CHUNKS = [(first + i * width // 2, width // 2) for first, width, _ in PIECES for i in range(2)]
FEW = 160
BLOCKS = [a ^ b ^ c for a in (0, NEAR) for b in (0, FAR) for c in (0, ZED)]


def swap(value, mask):
    return lax.ppermute(value, "tensor", [(i, i ^ mask) for i in range(PARTS)])


def normed_kernel(tokens, embed, gain, positions, place, one, two, three):
    rows = tokens.shape[0]
    spots = place[0, 0] * rows + lax.broadcasted_iota(jnp.int32, (rows, 1), 0)
    masked = jnp.max(jnp.where(spots == positions[...], 1.0, 0.0), axis=1, keepdims=True) > 0
    squares = jnp.zeros((rows, HD), jnp.float32)
    for at in range(0, tokens.shape[1], HD):
        some = slice(at, at + HD)
        values = jnp.where(masked, embed[:, some], tokens[:, some]).astype(jnp.float32)
        squares += values * values
    mean = jnp.sum(squares, axis=-1, keepdims=True) * (1.0 / tokens.shape[1])
    scale = lax.rsqrt(mean + 1e-05)
    for out, (first, width, _) in zip((one, two, three), PIECES):
        some = slice(first, first + width)
        values = jnp.where(masked, embed[:, some], tokens[:, some]).astype(jnp.float32)
        out[...] = (values * scale * gain[:, some].astype(jnp.float32)).astype(jnp.bfloat16)


def turn_heads(values, cosine, sine):
    out = []
    for at in range(0, values.shape[1], HD):
        left, right = values[:, at : at + HALF], values[:, at + HALF : at + HD]
        out += [left * cosine - right * sine, right * cosine + left * sine]
    return jnp.concatenate(out, axis=1).astype(jnp.bfloat16)


def few_rows(values, count):
    half = values.shape[0] // 2
    return jnp.concatenate([values[: count // 2], values[half : half + count // 2]], axis=0)


def together(*values):
    return lax.optimization_barrier(values)


def keys_after(order, steps):
    keys = [0]
    for mask in order[:steps]:
        keys = keys + [key ^ mask for key in keys]
    return keys


def step_up(have, step):
    return [swap(block, order[step]) for block, (_, _, order) in zip(have, PIECES)]


def in_order(blocks, order, rows):
    keys = keys_after(order, 3)
    at = [keys.index(m) * rows for m in BLOCKS]
    return jnp.concatenate([blocks[i : i + rows] for i in at], axis=0)


def add(one, two):
    return (one.astype(jnp.float32) + two.astype(jnp.float32)).astype(jnp.bfloat16)


def step_down(totals, step):
    keep, got = [], []
    for total, (_, _, order) in zip(totals, PIECES):
        left = [mask for mask in LINKS if mask not in order[:step]]
        at = left.index(order[step])
        keep.append(lax.index_in_dim(total, 0, at, keepdims=False))
        got.append(swap(lax.index_in_dim(total, 1, at, keepdims=False), order[step]))
    return keep, got


def added(keep, got):
    return [add(one, two) for one, two in zip(keep, got)]


def with_heads(query, key, value, mixed):
    rows, columns = query.shape
    tile = rows // 2
    for h in range(columns // HD):
        for at in range(0, rows, tile):
            scores = lax.dot_general(
                query[at : at + tile, HD * h : HD * (h + 1)],
                key,
                (((1,), (1,)), ((), ())),
                preferred_element_type=jnp.float32,
            ) * HD ** (-0.5)
            weights = jnp.exp(scores - jnp.max(scores, axis=-1, keepdims=True))
            probs = weights * (1.0 / jnp.sum(weights, axis=-1, keepdims=True))
            mixed[at : at + tile, HD * h : HD * (h + 1)] = jnp.dot(
                probs.astype(jnp.bfloat16), value, preferred_element_type=jnp.float32
            ).astype(jnp.bfloat16)


def fetch(source, here, sems, along):
    copies = []
    for i, (first, width) in enumerate(CHUNKS):
        some = pl.ds(first, width)
        where = (some, slice(None)) if along == 0 else (slice(None), some)
        copies.append(pltpu.make_async_copy(source.at[where], here.at[where], sems.at[i]))
        copies[-1].start()
    return copies


def project_out(mixed, out_here, copies, outs):
    half = mixed.shape[0] // 2
    for i, (first, width) in enumerate(CHUNKS):
        copies[i].wait()
        weights = out_here[:, first : first + width]
        at = (i % 2) * width
        for side in range(2):
            outs[2 * (i // 2) + side][:, at : at + width] = jnp.dot(
                mixed[half * side : half * (side + 1), :], weights, preferred_element_type=jnp.float32
            ).astype(jnp.bfloat16)


def first_kernel(query, pair, out_hbm, *rest):
    outs, (mixed, out_here, out_sems) = rest[:6], rest[6:]
    copies = fetch(out_hbm, out_here, out_sems, 1)
    with_heads(query, pair[:, :HD], pair[:, HD:], mixed)
    project_out(mixed, out_here, copies, outs)


def turned(values, cosine, sine):
    return (values * cosine + pltpu.roll(values, HALF, 1) * sine).astype(jnp.bfloat16)


def second_kernel(*refs):
    raw, refs = refs[:6], refs[6:]
    gain, cosine, sine, match, base, kv_here, query_hbm, out_hbm = refs[:8]
    outs, refs = refs[8:14], refs[14:]
    normed, moving, placed, mixed, query_here, out_here, query_sems, out_sems = refs
    arrivals = fetch(query_hbm, query_here, query_sems, 0)
    copies = fetch(out_hbm, out_here, out_sems, 1)
    half = raw[0].shape[0]
    width_all = gain.shape[1]
    scales = []
    for side in range(2):
        squares = jnp.zeros((half, HD), jnp.float32)
        for piece in range(3):
            ref = raw[2 * piece + side]

            def add_squares(i, squares, ref=ref):
                values = ref[:, pl.ds(pl.multiple_of(i * HD, HD), HD)].astype(jnp.float32)
                return squares + values * values

            squares = lax.fori_loop(0, ref.shape[1] // HD, add_squares, squares, unroll=2)
        mean = jnp.sum(squares, axis=-1, keepdims=True) * (1.0 / width_all)
        scales.append(lax.rsqrt(mean + 1e-05))
    queries = jnp.zeros((2 * half, query_here.shape[1]), jnp.float32)
    pairs = jnp.zeros((2 * half, kv_here.shape[0]), jnp.float32)
    for i, (first, width) in enumerate(CHUNKS):
        at = (i % 2) * width
        for side in range(2):
            values = raw[2 * (i // 2) + side][:, at : at + width].astype(jnp.float32)
            normed[half * side : half * (side + 1), :width] = (
                values * scales[side] * gain[:, first : first + width]
            ).astype(jnp.bfloat16)
        some = normed[:, :width]
        arrivals[i].wait()
        queries += jnp.dot(some, query_here[first : first + width, :], preferred_element_type=jnp.float32)
        pairs += dot_rows(some, kv_here[:, first : first + width])
    moving[:, :HD] = turned(pairs[:, :HD], cosine[...], sine[...])
    moving[:, HD : 2 * HD] = pairs[:, HD:].astype(jnp.bfloat16)
    for h in range(queries.shape[1] // HD):
        moving[:, HD * (h + 2) : HD * (h + 3)] = turned(queries[:, HD * h : HD * (h + 1)], cosine[...], sine[...])
    placed[...] = base[...] + jnp.dot(
        match[...], moving[...], preferred_element_type=jnp.float32
    ).astype(jnp.bfloat16)
    with_heads(placed.at[:, 2 * HD :], placed[:, :HD], placed[:, HD : 2 * HD], mixed)
    project_out(mixed, out_here, copies, outs)


def dot_rows(x, weights):
    return lax.dot_general(x, weights, (((1,), (1,)), ((), ())), preferred_element_type=jnp.float32)


def call_kernel(kernel, operands, outs, scratch=(), mib=16, last=()):
    places = [pltpu.VMEM] * (len(operands) - len(last)) + list(last)
    return pl.pallas_call(
        kernel,
        out_shape=[jax.ShapeDtypeStruct(*out) for out in outs],
        in_specs=[pl.BlockSpec(memory_space=place) for place in places],
        out_specs=[pl.BlockSpec(memory_space=pltpu.VMEM)] * len(outs),
        scratch_shapes=list(scratch),
        compiler_params=pltpu.CompilerParams(vmem_limit_bytes=mib * 2**20),
        cost_estimate=pl.CostEstimate(flops=1000000, bytes_accessed=100000, transcendentals=0),
    )(*operands)


def call_projected(kernel, operands, rows, scratch, mib, last):
    outs = [((rows // 2, width), jnp.bfloat16) for _, width, _ in PIECES for _ in range(2)]
    outs = call_kernel(kernel, operands, outs, scratch, mib, last)
    return [(outs[2 * i], outs[2 * i + 1]) for i in range(3)]


def join_kernel(*refs):
    for i in range(3):
        have, got, out = refs[i], refs[3 + i], refs[6 + i]
        rows = have.shape[0]
        out[:rows, :] = have[...]
        out[rows:, :] = got[...]


def joined(have, got):
    outs = [((2 * block.shape[0], block.shape[1]), block.dtype) for block in have]
    return call_kernel(join_kernel, [*have, *got], outs, mib=12)


def weight_rows_kernel(key, value, other_key, other_value, place, out):
    even = place[0, 0] % 2 == 0

    @pl.when(even)
    def _():
        out[:HALF, :] = key[...]
        out[HALF : 2 * HALF, :] = other_key[...]
        out[2 * HALF : 3 * HALF, :] = value[...]
        out[3 * HALF :, :] = other_value[...]

    @pl.when(jnp.logical_not(even))
    def _():
        out[:HALF, :] = other_key[...]
        out[HALF : 2 * HALF, :] = key[...]
        out[2 * HALF : 3 * HALF, :] = other_value[...]
        out[3 * HALF :, :] = value[...]


def table_kernel(one, two, ones_across, twos_across, freq, spots, listed, listed_few, *outs):
    cosine, sine, list_cosine, list_sine, match, match_few, flags = outs
    f32, bf16 = jnp.float32, jnp.bfloat16
    count = one.shape[0]
    stale = jnp.max(jnp.where(two[...] == ones_across[...], 1.0, 0.0), axis=0, keepdims=True)
    fresh = 1.0 - stale
    row = lax.broadcasted_iota(jnp.int32, (count, count), 0)
    column = lax.broadcasted_iota(jnp.int32, (count, count), 1)
    before = jnp.where(row < column, 1.0, 0.0).astype(bf16)

    def ahead(flag):
        wide = jnp.broadcast_to(flag, (16, count)).astype(bf16)
        return jnp.dot(wide, before, preferred_element_type=f32)[:1]

    fresh_count = jnp.sum(fresh, axis=1, keepdims=True)
    rank = jnp.where(fresh > 0, ahead(fresh), fresh_count + ahead(stale))
    spot = jnp.where(listed[...].astype(f32) == rank, 1.0, 0.0)
    list_spots = jnp.sum(spot * ones_across[...].astype(f32), axis=1, keepdims=True)
    here = jnp.where((spots[...] == ones_across[...]) & (fresh > 0), 1.0, 0.0)
    match[...] = dot_rows(here.astype(bf16), spot.astype(bf16)).astype(bf16)
    spot_few = jnp.where(listed_few[...].astype(f32) == rank, 1.0, 0.0)
    match_few[...] = dot_rows(here.astype(bf16), spot_few.astype(bf16)).astype(bf16)
    is_list = jnp.max(here, axis=1, keepdims=True)
    masked_1 = jnp.max(jnp.where(spots[...] == twos_across[...], 1.0, 0.0), axis=1, keepdims=True)
    lane = lax.broadcasted_iota(jnp.int32, (spots.shape[0], HD), 1)
    flags[...] = jnp.where(lane == 0, masked_1, jnp.where(lane == 1, is_list, fresh_count))
    sign = jnp.where(lax.broadcasted_iota(jnp.int32, (1, HD), 1) < HALF, -1.0, 1.0)
    angle = spots[...].astype(f32) * freq[...]
    cosine[...] = jnp.cos(angle)
    sine[...] = jnp.sin(angle) * sign
    angle = list_spots * freq[...]
    list_cosine[...] = jnp.cos(angle)
    list_sine[...] = jnp.sin(angle) * sign


def mask_kernel(embed, gain, query_here, kv_here, cosine, sine, list_cosine, list_sine, query, base):
    values = embed[...].astype(jnp.float32)
    mean = jnp.sum(values * values, axis=-1, keepdims=True) * (1.0 / embed.shape[1])
    row = (values * lax.rsqrt(mean + 1e-05) * gain[...]).astype(jnp.bfloat16)
    row = jnp.broadcast_to(row, (16, row.shape[1]))
    queries = jnp.dot(row, query_here[...], preferred_element_type=jnp.float32)[:1]
    pairs = dot_rows(row, kv_here[...])[:1]
    length = base.shape[0]
    base[:, :HD] = turned(jnp.broadcast_to(pairs[:, :HD], (length, HD)), cosine[...], sine[...])
    base[:, HD : 2 * HD] = jnp.broadcast_to(pairs[:, HD:], (length, HD)).astype(jnp.bfloat16)
    for at in range(0, queries.shape[1], HD):
        some = queries[:, at : at + HD]
        base[:, 2 * HD + at : 3 * HD + at] = turned(jnp.broadcast_to(some, (length, HD)), cosine[...], sine[...])
        query[:, at : at + HD] = turned(
            jnp.broadcast_to(some, (query.shape[0], HD)), list_cosine[...], list_sine[...]
        )


def add_pairs(pieces, kv_here, total, low, fresh):
    rows = total.shape[0] // 8
    for piece, (first, width, order) in zip(pieces, PIECES):
        product = dot_rows(piece[...], kv_here[:, first : first + width])
        for i, key in enumerate(keys_after(order, 3)[low : low + 4]):
            at = BLOCKS.index(key) * rows
            some = product[i * rows : (i + 1) * rows]
            if key in fresh:
                fresh.remove(key)
                total[at : at + rows, :] = some
            else:
                total[at : at + rows, :] += some


def early_kernel(one, two, three, kv_here, total):
    fresh = set(BLOCKS)
    add_pairs((one, two, three), kv_here, total, 0, fresh)
    rows = total.shape[0] // 8
    for key in fresh:
        at = BLOCKS.index(key) * rows
        total[at : at + rows, :] = jnp.zeros((rows, total.shape[1]), jnp.float32)


def late_kernel(one, two, three, kv_here, early, cosine, sine, out, total):
    total[...] = early[...]
    add_pairs((one, two, three), kv_here, total, 4, set())
    rows = total.shape[0]
    out[:, :HD] = turned(total[:, :HD], cosine[:rows, :], sine[:rows, :])
    out[:, HD:] = total[:, HD:].astype(jnp.bfloat16)


def chosen(spots, positions):
    return jnp.any(spots[:, None] == positions[None, :], axis=1)


def pick(one_hot, rows):
    return jnp.dot(
        one_hot.astype(jnp.bfloat16), rows, preferred_element_type=jnp.float32
    ).astype(jnp.bfloat16)


def shards(tokens, positions, mask_embed, norm_gain, w_query, w_key, w_value, w_out):
    place = lax.axis_index("tensor")
    rows = tokens.shape[0]
    length = rows * PARTS
    relative = jnp.array([m ^ c for c in (0, CORE) for m in BLOCKS], jnp.int32)

    have = call_kernel(
        normed_kernel,
        [tokens, mask_embed[None, :], norm_gain[None, :], positions[:1], place.reshape(1, 1)],
        [((rows, width), jnp.bfloat16) for _, width, _ in PIECES],
        last=[pltpu.SMEM],
    )
    key_rows, value_rows = w_key.T, w_value.T
    got, later, key_rows, value_rows = together(
        step_up(have, 0), (positions, place), key_rows, value_rows
    )
    positions, place = later
    have = joined(have, got)

    f32, bf16 = jnp.float32, jnp.bfloat16
    count, columns = positions.shape[1], w_query.shape[1]
    other_key, other_value = swap(key_rows, CORE), swap(value_rows, CORE)
    owners = place ^ relative
    spots = (owners[:, None] * rows + jnp.arange(rows, dtype=jnp.int32)[None, :]).reshape(-1, 1)
    entry = jnp.arange(count // 2, dtype=jnp.int32)
    entry = entry // 16 * 32 + entry % 16
    listed = jnp.concatenate([entry + place % 2 * 16, entry + (1 - place % 2) * 16])[:, None]
    freq = 500000.0 ** (-(jnp.arange(HD, dtype=f32) % HALF * 2.0 / HD))
    cosine, sine, list_cosine, list_sine, match, match_few, flags = call_kernel(
        table_kernel,
        [positions[0][:, None], positions[1][:, None], positions[:1], positions[1:], freq[None], spots, listed, few_rows(listed, FEW)],
        [((length, HD), f32)] * 2 + [((count, HD), f32)] * 2 + [((length, count), bf16), ((length, FEW), bf16), ((length, HD), f32)],
    )
    (kv_weights,) = call_kernel(
        weight_rows_kernel,
        [key_rows, value_rows, other_key, other_value, place.reshape(1, 1)],
        [((4 * HALF, key_rows.shape[1]), bf16)],
        last=[pltpu.SMEM],
    )
    tables = (kv_weights, cosine, sine, list_cosine, list_sine, match, match_few, flags)
    got, tables, mask_embed, norm_gain = together(step_up(have, 1), tables, mask_embed, norm_gain)
    kv_weights, cosine, sine, list_cosine, list_sine, match, match_few, flags = tables
    have = joined(have, got)

    gain = norm_gain[None, :].astype(f32)
    query_0, base_mask = call_kernel(
        mask_kernel,
        [mask_embed[None, :], gain, w_query, kv_weights, cosine, sine, list_cosine, list_sine],
        [((count, columns), bf16), ((length, columns + 2 * HD), bf16)],
    )
    (early,) = call_kernel(early_kernel, [*have, kv_weights], [((length // 2, 2 * HD), f32)])
    got, query_0, base_mask, early = together(step_up(have, 2), query_0, base_mask, early)

    last = got
    (pair_own,) = call_kernel(
        late_kernel,
        [*got, kv_weights, early, cosine, sine],
        [((length // 2, 2 * HD), bf16)],
        [pltpu.VMEM((length // 2, 2 * HD), f32)],
    )
    def rest(count, match):
        x_own = joined(have, last)
        pair_other, x_own = together(swap(pair_own, CORE), x_own)
        pair = jnp.concatenate([pair_own, pair_other], axis=0)
        x_other = [swap(block, CORE) for block in x_own]
        products = call_projected(
            first_kernel,
            [few_rows(query_0, count), pair, w_out],
            count,
            [
                pltpu.VMEM((count, columns), bf16),
                pltpu.VMEM(w_out.shape, bf16),
                pltpu.SemaphoreType.DMA((len(CHUNKS),)),
            ],
            20,
            [pltpu.HBM],
        )
        products, x_own, x_other = together(products, x_own, x_other)

        def queries_of(x):
            return sum(
                in_order(
                    jnp.dot(block, w_query[first : first + width], preferred_element_type=jnp.float32), order, rows
                )
                for block, (first, width, order) in zip(x, PIECES)
            )

        bits = {NEAR: ((place >> 2) ^ (place >> 3)) % 2 == 1, FAR: (place >> 3) % 2 == 1, ZED: (place >> 1) % 2 == 1}
        sides = [bits[order[0]] for _, _, order in PIECES]
        totals = [add(keep, swap(send, CORE)) for keep, send in products]
        keep, send = [], []
        for total, side in zip(totals, sides):
            middle = total.shape[1] // 2
            left, right = total[:, :middle], total[:, middle:]
            keep.append(jnp.where(side, right, left))
            send.append(jnp.where(side, left, right))
        got = [swap(block, order[0]) for block, (_, _, order) in zip(send, PIECES)]

        got, query_own = together(got, queries_of(x_own))
        totals = added(keep, got)
        got = together(*step_up(totals, 1))
        totals = added(totals, got)
        got, query_other = together(step_up(totals, 2), queries_of(x_other))
        totals = added(totals, got)
        states = []
        for (first, width, _), total, side in zip(PIECES, totals, sides):
            row = mask_embed[None, first : first + width]
            middle = width // 2
            states.append(add(jnp.where(side, row[:, middle:], row[:, :middle]), total))
        masked_1, is_list = flags[:, :1] > 0, flags[:, 1:2] > 0
        base_tokens = jnp.concatenate(
            [pair, turn_heads(jnp.concatenate([query_own, query_other], axis=0), cosine[:, :HALF], sine[:, HALF:])], axis=1
        )
        base = jnp.where(masked_1, base_mask, jnp.where(is_list, jnp.zeros_like(base_tokens), base_tokens))
        got, base = together(step_up(states, 0), base)
        raw = []
        for state, block, side in zip(states, got, sides):
            raw.append(
                jnp.where(
                    side, jnp.concatenate([block, state], axis=1), jnp.concatenate([state, block], axis=1)
                )
            )
        raw = [(block, swap(block, CORE)) for block in raw]

        operands = [half for both in raw for half in both]
        operands += [gain, few_rows(list_cosine, count), few_rows(list_sine, count), match, base, kv_weights, w_query, w_out]
        products = call_projected(
            second_kernel,
            operands,
            length,
            [
                pltpu.VMEM((count, CHUNKS[0][1]), bf16),
                pltpu.VMEM((count, columns + 2 * HD), bf16),
                pltpu.VMEM((length, columns + 2 * HD), bf16),
                pltpu.VMEM((length, columns), bf16),
                pltpu.VMEM(w_query.shape, bf16),
                pltpu.VMEM(w_out.shape, bf16),
                pltpu.SemaphoreType.DMA((len(CHUNKS),)),
                pltpu.SemaphoreType.DMA((len(CHUNKS),)),
            ],
            32,
            [pltpu.HBM, pltpu.HBM],
        )
        totals = [add(keep, swap(send, CORE)).reshape(2, 2, 2, rows, keep.shape[1]) for keep, send in products]
        keep, incoming = step_down(totals, 0)
        own_match = match[:rows]
        middle = count // 2
        states = jnp.concatenate(
            [pick(own_match[:, :middle], one) + pick(own_match[:, middle:], two) for one, two in raw], axis=1
        )
        hidden_1 = jnp.where(
            masked_1[:rows], mask_embed[None, :], jnp.where(is_list[:rows], states, tokens)
        )
        incoming, hidden_1 = together(incoming, hidden_1)
        keep, incoming = step_down(added(keep, incoming), 1)
        incoming = together(*incoming)
        keep, incoming = step_down(added(keep, incoming), 2)
        incoming = together(*incoming)
        summed_1 = jnp.concatenate(added(keep, incoming), axis=1)
        return (hidden_1.astype(jnp.float32) + summed_1.astype(jnp.float32)).astype(jnp.bfloat16)

    return lax.cond(flags[0, 2] <= FEW, lambda: rest(FEW, match_few), lambda: rest(count, match))


def solution(mesh):
    placed = (
        P(("dp", "tensor"), None),
        P("dp", None),
        P(),
        P(),
        P(None, "tensor"),
        P(None, "tensor"),
        P(None, "tensor"),
        P("tensor", None),
    )
    return jax.shard_map(
        shards, mesh=mesh, in_specs=placed, out_specs=P(("dp", "tensor"), None), check_vma=False
    )
```

```python
import jax
import jax.numpy as jnp
from jax import lax
from jax.experimental import pallas as pl
from jax.experimental.pallas import tpu as pltpu
from jax.sharding import PartitionSpec as P

HD = 128
HALF = HD // 2
PARTS = 16
CORE, ZED, NEAR, FAR = 1, 2, 4, 12
LINKS = (NEAR, FAR, ZED)
PIECES = (
    (0, 2816, (NEAR, FAR, ZED)),
    (2816, 2816, (FAR, ZED, NEAR)),
    (5632, 2560, (ZED, NEAR, FAR)),
)
CHUNKS = [(first + i * width // 2, width // 2) for first, width, _ in PIECES for i in range(2)]
BLOCKS = [a ^ b ^ c for a in (0, NEAR) for b in (0, FAR) for c in (0, ZED)]


def swap(value, mask):
    return lax.ppermute(value, "tensor", [(i, i ^ mask) for i in range(PARTS)])


def normalize(rows, gain):
    values = rows.astype(jnp.float32)
    scale = lax.rsqrt(jnp.mean(values * values, axis=-1, keepdims=True) + 1e-05)
    return (values * scale * gain.astype(jnp.float32)).astype(jnp.bfloat16)


def turn_heads(values, cosine, sine):
    out = []
    for at in range(0, values.shape[1], HD):
        left, right = values[:, at : at + HALF], values[:, at + HALF : at + HD]
        out += [left * cosine - right * sine, right * cosine + left * sine]
    return jnp.concatenate(out, axis=1).astype(jnp.bfloat16)


def together(*values):
    return lax.optimization_barrier(values)


def keys_after(order, steps):
    keys = [0]
    for mask in order[:steps]:
        keys = keys + [key ^ mask for key in keys]
    return keys


def step_up(have, step):
    return [swap(block, order[step]) for block, (_, _, order) in zip(have, PIECES)]


def in_order(blocks, order, rows):
    keys = keys_after(order, 3)
    at = [keys.index(m) * rows for m in BLOCKS]
    return jnp.concatenate([blocks[i : i + rows] for i in at], axis=0)


def add(one, two):
    return (one.astype(jnp.float32) + two.astype(jnp.float32)).astype(jnp.bfloat16)


def step_down(totals, step):
    keep, got = [], []
    for total, (_, _, order) in zip(totals, PIECES):
        left = [mask for mask in LINKS if mask not in order[:step]]
        at = left.index(order[step])
        keep.append(lax.index_in_dim(total, 0, at, keepdims=False))
        got.append(swap(lax.index_in_dim(total, 1, at, keepdims=False), order[step]))
    return keep, got


def added(keep, got):
    return [add(one, two) for one, two in zip(keep, got)]


def with_heads(query, key, value, mixed):
    rows, columns = query.shape
    tile = rows // 2
    for h in range(columns // HD):
        for at in range(0, rows, tile):
            scores = lax.dot_general(
                query[at : at + tile, HD * h : HD * (h + 1)],
                key,
                (((1,), (1,)), ((), ())),
                preferred_element_type=jnp.float32,
            ) * HD ** (-0.5)
            weights = jnp.exp(scores - jnp.max(scores, axis=-1, keepdims=True))
            probs = weights * (1.0 / jnp.sum(weights, axis=-1, keepdims=True))
            mixed[at : at + tile, HD * h : HD * (h + 1)] = jnp.dot(
                probs.astype(jnp.bfloat16), value, preferred_element_type=jnp.float32
            ).astype(jnp.bfloat16)


def fetch(source, here, sems, along):
    copies = []
    for i, (first, width) in enumerate(CHUNKS):
        some = pl.ds(first, width)
        where = (some, slice(None)) if along == 0 else (slice(None), some)
        copies.append(pltpu.make_async_copy(source.at[where], here.at[where], sems.at[i]))
        copies[-1].start()
    return copies


def project_out(mixed, out_here, copies, outs):
    sides = len(outs) // 3
    for i, (first, width) in enumerate(CHUNKS):
        if copies is not None:
            copies[i].wait()
        weights = out_here[:, first : first + width]
        at = (i % 2) * width
        for side in range(sides):
            out = outs[sides * (i // 2) + side]
            rows = out.shape[0]
            out[:, at : at + width] = jnp.dot(
                mixed[rows * side : rows * (side + 1), :], weights, preferred_element_type=jnp.float32
            ).astype(jnp.bfloat16)


def first_kernel(query, pair, out_here, *rest):
    outs, (mixed,) = rest[:6], rest[6:]
    with_heads(query, pair[:, :HD], pair[:, HD:], mixed)
    project_out(mixed, out_here, None, outs)


def third_kernel(mixed, out_hbm, one, two, three, out_here, sems):
    project_out(mixed, out_here, fetch(out_hbm, out_here, sems, 1), (one, two, three))


def turned(values, cosine, sine):
    return (values * cosine + pltpu.roll(values, HALF, 1) * sine).astype(jnp.bfloat16)


def second_kernel(*refs):
    raw, refs = refs[:12], refs[12:]
    gain, cosine, sine, match, base, kv_here, query_hbm, out_hbm, sides = refs[:9]
    mixed, outs, refs = refs[9], refs[10:13], refs[13:]
    normed, moving, placed, later, query_here, out_here, query_sems, out_sems = refs
    arrivals = fetch(query_hbm, query_here, query_sems, 0)
    copies = fetch(out_hbm, out_here, out_sems, 1)
    half = raw[0].shape[0]
    width_all = gain.shape[1]
    scales = []
    for core in range(2):
        squares = jnp.zeros((half, HD), jnp.float32)
        for piece in range(3):
            for ref in raw[4 * piece + 2 * core : 4 * piece + 2 * core + 2]:

                def add_squares(i, squares, ref=ref):
                    values = ref[:, pl.ds(pl.multiple_of(i * HD, HD), HD)].astype(jnp.float32)
                    return squares + values * values

                squares = lax.fori_loop(0, ref.shape[1] // HD, add_squares, squares)
        mean = jnp.sum(squares, axis=-1, keepdims=True) * (1.0 / width_all)
        scales.append(lax.rsqrt(mean + 1e-05))
    queries = jnp.zeros((2 * half, query_here.shape[1]), jnp.float32)
    pairs = jnp.zeros((2 * half, kv_here.shape[0]), jnp.float32)
    for i, (first, width) in enumerate(CHUNKS):
        here = sides[0, i // 2] == i % 2
        for core in range(2):
            own, came = raw[4 * (i // 2) + 2 * core : 4 * (i // 2) + 2 * core + 2]
            values = jnp.where(here, own[...].astype(jnp.float32), came[...].astype(jnp.float32))
            normed[half * core : half * (core + 1), :width] = (
                values * scales[core] * gain[:, first : first + width]
            ).astype(jnp.bfloat16)
        some = normed[:, :width]
        arrivals[i].wait()
        queries += jnp.dot(some, query_here[first : first + width, :], preferred_element_type=jnp.float32)
        pairs += dot_rows(some, kv_here[:, first : first + width])
    moving[:, :HD] = turned(pairs[:, :HD], cosine[...], sine[...])
    moving[:, HD : 2 * HD] = pairs[:, HD:].astype(jnp.bfloat16)
    for h in range(queries.shape[1] // HD):
        moving[:, HD * (h + 2) : HD * (h + 3)] = turned(queries[:, HD * h : HD * (h + 1)], cosine[...], sine[...])
    placed[...] = base[...] + jnp.dot(
        match[...], moving[...], preferred_element_type=jnp.float32
    ).astype(jnp.bfloat16)
    with_heads(placed.at[:, 2 * HD :], placed[:, :HD], placed[:, HD : 2 * HD], later)
    rows = mixed.shape[0]
    mixed[...] = later[:rows, :]
    project_out(later.at[rows:, :], out_here, copies, outs)


def query_kernel(one, two, three, weights, out, total):
    rows = out.shape[0] // 8
    for i, (piece, (first, width, order)) in enumerate(zip((one, two, three), PIECES)):
        total[...] = jnp.dot(piece[...], weights[first : first + width, :], preferred_element_type=jnp.float32)
        for j, key in enumerate(keys_after(order, 3)):
            at = BLOCKS.index(key) * rows
            some = total[j * rows : (j + 1) * rows, :]
            if i == 0:
                out[at : at + rows, :] = some
            else:
                out[at : at + rows, :] += some


def dot_rows(x, weights):
    return lax.dot_general(x, weights, (((1,), (1,)), ((), ())), preferred_element_type=jnp.float32)


def call_kernel(kernel, operands, outs, scratch=(), mib=16, last=()):
    places = [pltpu.VMEM] * (len(operands) - len(last)) + list(last)
    return pl.pallas_call(
        kernel,
        out_shape=[jax.ShapeDtypeStruct(*out) for out in outs],
        in_specs=[pl.BlockSpec(memory_space=place) for place in places],
        out_specs=[pl.BlockSpec(memory_space=pltpu.VMEM)] * len(outs),
        scratch_shapes=list(scratch),
        compiler_params=pltpu.CompilerParams(vmem_limit_bytes=mib * 2**20),
        cost_estimate=pl.CostEstimate(flops=1000000, bytes_accessed=100000, transcendentals=0),
    )(*operands)


def join_kernel(*refs):
    for i in range(3):
        have, got, out = refs[i], refs[3 + i], refs[6 + i]
        rows = have.shape[0]
        out[:rows, :] = have[...]
        out[rows:, :] = got[...]


def joined(have, got):
    outs = [((2 * block.shape[0], block.shape[1]), block.dtype) for block in have]
    return call_kernel(join_kernel, [*have, *got], outs, mib=12)


def weight_rows_kernel(key, value, other_key, other_value, place, out):
    even = place[0, 0] % 2 == 0

    @pl.when(even)
    def _():
        out[:HALF, :] = key[...]
        out[HALF : 2 * HALF, :] = other_key[...]
        out[2 * HALF : 3 * HALF, :] = value[...]
        out[3 * HALF :, :] = other_value[...]

    @pl.when(jnp.logical_not(even))
    def _():
        out[:HALF, :] = other_key[...]
        out[HALF : 2 * HALF, :] = key[...]
        out[2 * HALF : 3 * HALF, :] = other_value[...]
        out[3 * HALF :, :] = value[...]


def table_kernel(one, two, ones_across, twos_across, freq, spots, listed, cosine, sine, list_cosine, list_sine, match, flags):
    f32, bf16 = jnp.float32, jnp.bfloat16
    count = one.shape[0]
    stale = jnp.max(jnp.where(two[...] == ones_across[...], 1.0, 0.0), axis=0, keepdims=True)
    fresh = 1.0 - stale
    row = lax.broadcasted_iota(jnp.int32, (count, count), 0)
    column = lax.broadcasted_iota(jnp.int32, (count, count), 1)
    before = jnp.where(row < column, 1.0, 0.0).astype(bf16)

    def ahead(flag):
        wide = jnp.broadcast_to(flag, (16, count)).astype(bf16)
        return jnp.dot(wide, before, preferred_element_type=f32)[:1]

    rank = jnp.where(fresh > 0, ahead(fresh), jnp.sum(fresh, axis=1, keepdims=True) + ahead(stale))
    spot = jnp.where(listed[...].astype(f32) == rank, 1.0, 0.0)
    list_spots = jnp.sum(spot * ones_across[...].astype(f32), axis=1, keepdims=True)
    here = jnp.where((spots[...] == ones_across[...]) & (fresh > 0), 1.0, 0.0)
    match[...] = dot_rows(here.astype(bf16), spot.astype(bf16)).astype(bf16)
    is_list = jnp.max(here, axis=1, keepdims=True)
    masked_1 = jnp.max(jnp.where(spots[...] == twos_across[...], 1.0, 0.0), axis=1, keepdims=True)
    lane = lax.broadcasted_iota(jnp.int32, (spots.shape[0], HD), 1)
    flags[...] = jnp.where(lane == 0, masked_1, is_list)
    sign = jnp.where(lax.broadcasted_iota(jnp.int32, (1, HD), 1) < HALF, -1.0, 1.0)
    angle = spots[...].astype(f32) * freq[...]
    cosine[...] = jnp.cos(angle)
    sine[...] = jnp.sin(angle) * sign
    angle = list_spots * freq[...]
    list_cosine[...] = jnp.cos(angle)
    list_sine[...] = jnp.sin(angle) * sign


def mask_kernel(embed, gain, query_here, kv_here, cosine, sine, list_cosine, list_sine, query, base):
    values = embed[...].astype(jnp.float32)
    mean = jnp.sum(values * values, axis=-1, keepdims=True) * (1.0 / embed.shape[1])
    row = (values * lax.rsqrt(mean + 1e-05) * gain[...]).astype(jnp.bfloat16)
    row = jnp.broadcast_to(row, (16, row.shape[1]))
    queries = jnp.dot(row, query_here[...], preferred_element_type=jnp.float32)[:1]
    pairs = dot_rows(row, kv_here[...])[:1]
    length = base.shape[0]
    base[:, :HD] = turned(jnp.broadcast_to(pairs[:, :HD], (length, HD)), cosine[...], sine[...])
    base[:, HD : 2 * HD] = jnp.broadcast_to(pairs[:, HD:], (length, HD)).astype(jnp.bfloat16)
    for at in range(0, queries.shape[1], HD):
        some = queries[:, at : at + HD]
        base[:, 2 * HD + at : 3 * HD + at] = turned(jnp.broadcast_to(some, (length, HD)), cosine[...], sine[...])
        query[:, at : at + HD] = turned(
            jnp.broadcast_to(some, (query.shape[0], HD)), list_cosine[...], list_sine[...]
        )


def add_pairs(pieces, kv_here, total, low, fresh):
    rows = total.shape[0] // 8
    for piece, (first, width, order) in zip(pieces, PIECES):
        product = dot_rows(piece[...], kv_here[:, first : first + width])
        for i, key in enumerate(keys_after(order, 3)[low : low + 4]):
            at = BLOCKS.index(key) * rows
            some = product[i * rows : (i + 1) * rows]
            if key in fresh:
                fresh.remove(key)
                total[at : at + rows, :] = some
            else:
                total[at : at + rows, :] += some


def early_kernel(one, two, three, kv_here, total):
    fresh = set(BLOCKS)
    add_pairs((one, two, three), kv_here, total, 0, fresh)
    rows = total.shape[0] // 8
    for key in fresh:
        at = BLOCKS.index(key) * rows
        total[at : at + rows, :] = jnp.zeros((rows, total.shape[1]), jnp.float32)


def late_kernel(one, two, three, kv_here, early, cosine, sine, out, total):
    total[...] = early[...]
    add_pairs((one, two, three), kv_here, total, 4, set())
    rows = total.shape[0]
    out[:, :HD] = turned(total[:, :HD], cosine[:rows, :], sine[:rows, :])
    out[:, HD:] = total[:, HD:].astype(jnp.bfloat16)


def chosen(spots, positions):
    return jnp.any(spots[:, None] == positions[None, :], axis=1)


def pick(one_hot, rows):
    return jnp.dot(
        one_hot.astype(jnp.bfloat16), rows, preferred_element_type=jnp.float32
    ).astype(jnp.bfloat16)


def shards(tokens, positions, mask_embed, norm_gain, w_query, w_key, w_value, w_out):
    place = lax.axis_index("tensor")
    rows = tokens.shape[0]
    length = rows * PARTS
    relative = jnp.array([m ^ c for c in (0, CORE) for m in BLOCKS], jnp.int32)

    own_spots = place * rows + jnp.arange(rows, dtype=jnp.int32)
    own_masked_0 = chosen(own_spots, positions[0])
    hidden_0 = jnp.where(own_masked_0[:, None], mask_embed[None, :], tokens)
    normed_0 = normalize(hidden_0, norm_gain)
    have = [normed_0[:, first : first + width] for first, width, _ in PIECES]
    key_rows, value_rows = w_key.T, w_value.T
    have, positions, place, key_rows, value_rows = together(have, positions, place, key_rows, value_rows)

    f32, bf16 = jnp.float32, jnp.bfloat16
    count, columns = positions.shape[1], w_query.shape[1]
    owners = place ^ relative
    spots = (owners[:, None] * rows + jnp.arange(rows, dtype=jnp.int32)[None, :]).reshape(-1, 1)
    listed = (jnp.arange(count, dtype=jnp.int32) + (place % 2) * (count // 2)) % count
    freq = 500000.0 ** (-(jnp.arange(HD, dtype=f32) % HALF * 2.0 / HD))
    cosine, sine, list_cosine, list_sine, match, flags = call_kernel(
        table_kernel,
        [positions[0][:, None], positions[1][:, None], positions[:1], positions[1:], freq[None], spots, listed[:, None]],
        [((length, HD), f32)] * 2 + [((count, HD), f32)] * 2 + [((length, count), bf16), ((length, HD), f32)],
    )
    other_rows = swap(key_rows, CORE), swap(value_rows, CORE)
    tables = (cosine, sine, list_cosine, list_sine, match, flags)
    got, tables, other_rows, place = together(step_up(have, 0), tables, other_rows, place)
    cosine, sine, list_cosine, list_sine, match, flags = tables
    have = joined(have, got)

    def head_weights(place):
        (weights,) = call_kernel(
            weight_rows_kernel,
            [key_rows, value_rows, *other_rows, place.reshape(1, 1)],
            [((4 * HALF, key_rows.shape[1]), bf16)],
            last=[pltpu.SMEM],
        )
        return weights

    kv_weights = head_weights(place)
    got, kv_weights, mask_embed, norm_gain = together(step_up(have, 1), kv_weights, mask_embed, norm_gain)
    have = joined(have, got)

    gain = norm_gain[None, :].astype(f32)
    query_0, base_mask = call_kernel(
        mask_kernel,
        [mask_embed[None, :], gain, w_query, kv_weights, cosine, sine, list_cosine, list_sine],
        [((count, columns), bf16), ((length, columns + 2 * HD), bf16)],
    )
    (early,) = call_kernel(early_kernel, [*have, kv_weights], [((length // 2, 2 * HD), f32)])
    got, query_0, base_mask, early = together(step_up(have, 2), query_0, base_mask, early)

    (pair_own,) = call_kernel(
        late_kernel,
        [*got, kv_weights, early, cosine, sine],
        [((length // 2, 2 * HD), bf16)],
        [pltpu.VMEM((length // 2, 2 * HD), f32)],
    )
    x_own = joined(have, got)
    pair_other, x_own = together(swap(pair_own, CORE), x_own)
    pair = jnp.concatenate([pair_own, pair_other], axis=0)
    x_other = [swap(block, CORE) for block in x_own]
    outs = call_kernel(
        first_kernel,
        [query_0, pair, w_out],
        [((count // 2, width), bf16) for _, width, _ in PIECES for _ in range(2)],
        [pltpu.VMEM((count, columns), bf16)],
        12,
    )
    outs, x_other, x_own = together(outs, x_other, x_own)

    def queries_of(x):
        (queries,) = call_kernel(
            query_kernel,
            [*x, w_query],
            [((length // 2, columns), f32)],
            [pltpu.VMEM((length // 2, columns), f32)],
        )
        return queries

    bits = {NEAR: ((place >> 2) ^ (place >> 3)) % 2 == 1, FAR: (place >> 3) % 2 == 1, ZED: (place >> 1) % 2 == 1}
    sides = [bits[order[0]] for _, _, order in PIECES]
    came = [swap(outs[2 * i + 1], CORE) for i in range(3)]
    came, x_own = together(came, x_own)
    totals = [add(outs[2 * i], came[i]) for i in range(3)]
    keep, send = [], []
    for total, side in zip(totals, sides):
        middle = total.shape[1] // 2
        left, right = total[:, :middle], total[:, middle:]
        keep.append(jnp.where(side, right, left))
        send.append(jnp.where(side, left, right))
    got = [swap(block, order[0]) for block, (_, _, order) in zip(send, PIECES)]

    got, query_own, x_other = together(got, queries_of(x_own), x_other)
    totals = added(keep, got)
    got, query_other = together(step_up(totals, 1), queries_of(x_other))
    totals = added(totals, got)
    got, place = together(step_up(totals, 2), place)
    totals = added(totals, got)
    states = []
    for (first, width, _), total, side in zip(PIECES, totals, sides):
        row = mask_embed[None, first : first + width]
        middle = width // 2
        states.append(add(jnp.where(side, row[:, middle:], row[:, :middle]), total))
    masked_1, is_list = flags[:, :1] > 0, flags[:, 1:2] > 0
    base_tokens = jnp.concatenate(
        [pair, turn_heads(jnp.concatenate([query_own, query_other], axis=0), cosine[:, :HALF], sine[:, HALF:])], axis=1
    )
    base = jnp.where(masked_1, base_mask, jnp.where(is_list, jnp.zeros_like(base_tokens), base_tokens))
    kv_weights = head_weights(place)
    got, base, kv_weights, others = together(
        step_up(states, 0), base, kv_weights, [swap(state, CORE) for state in states]
    )
    raw = [
        (state, block, other, swap(block, CORE)) for state, block, other in zip(states, got, others)
    ]

    operands = [some for four in raw for some in four]
    operands += [gain, list_cosine, list_sine, match, base, kv_weights, w_query, w_out]
    operands += [jnp.stack(sides).astype(jnp.int32)[None, :]]
    kept, *send = call_kernel(
        second_kernel,
        operands,
        [((length // 2, columns), bf16)] + [((length // 2, width), bf16) for _, width, _ in PIECES],
        [
            pltpu.VMEM((count, CHUNKS[0][1]), bf16),
            pltpu.VMEM((count, columns + 2 * HD), bf16),
            pltpu.VMEM((length, columns + 2 * HD), bf16),
            pltpu.VMEM((length, columns), bf16),
            pltpu.VMEM(w_query.shape, bf16),
            pltpu.VMEM(w_out.shape, bf16),
            pltpu.SemaphoreType.DMA((len(CHUNKS),)),
            pltpu.SemaphoreType.DMA((len(CHUNKS),)),
        ],
        32,
        [pltpu.HBM, pltpu.HBM, pltpu.SMEM],
    )
    keep = call_kernel(
        third_kernel,
        [kept, w_out],
        [((length // 2, width), bf16) for _, width, _ in PIECES],
        [pltpu.VMEM(w_out.shape, bf16), pltpu.SemaphoreType.DMA((len(CHUNKS),))],
        16,
        [pltpu.HBM],
    )
    totals = [
        add(one, swap(two, CORE)).reshape(2, 2, 2, rows, one.shape[1]) for one, two in zip(keep, send)
    ]
    keep, incoming = step_down(totals, 0)
    own_match = match[:rows]
    middle = count // 2
    picked = []
    for (own, came, other_own, other_came), side in zip(raw, sides):
        here = pick(own_match[:, :middle], own) + pick(own_match[:, middle:], other_own)
        there = pick(own_match[:, :middle], came) + pick(own_match[:, middle:], other_came)
        picked += [jnp.where(side, there, here), jnp.where(side, here, there)]
    states = jnp.concatenate(picked, axis=1)
    hidden_1 = jnp.where(
        masked_1[:rows], mask_embed[None, :], jnp.where(is_list[:rows], states, tokens)
    )
    incoming, hidden_1 = together(incoming, hidden_1)
    keep, incoming = step_down(added(keep, incoming), 1)
    incoming = together(*incoming)
    keep, incoming = step_down(added(keep, incoming), 2)
    incoming = together(*incoming)
    summed_1 = jnp.concatenate(added(keep, incoming), axis=1)
    return (hidden_1.astype(jnp.float32) + summed_1.astype(jnp.float32)).astype(jnp.bfloat16)


def solution(mesh):
    placed = (
        P(("dp", "tensor"), None),
        P("dp", None),
        P(),
        P(),
        P(None, "tensor"),
        P(None, "tensor"),
        P(None, "tensor"),
        P("tensor", None),
    )
    return jax.shard_map(
        shards, mesh=mesh, in_specs=placed, out_specs=P(("dp", "tensor"), None), check_vma=False
    )
```

```python
import jax
import jax.numpy as jnp
from jax import lax
from jax.experimental import pallas as pl
from jax.experimental.pallas import tpu as pltpu
from jax.sharding import PartitionSpec as P

HD = 128
HALF = HD // 2
PARTS = 16
CORE, ZED, NEAR, FAR = 1, 2, 4, 12
LINKS = (NEAR, FAR, ZED)
PIECES = (
    (0, 2816, (NEAR, FAR, ZED)),
    (2816, 2816, (FAR, ZED, NEAR)),
    (5632, 2560, (ZED, NEAR, FAR)),
)
CHUNKS = [(first + i * width // 2, width // 2) for first, width, _ in PIECES for i in range(2)]
GRANT = 20
BLOCKS = [a ^ b ^ c for a in (0, NEAR) for b in (0, FAR) for c in (0, ZED)]


def swap(value, mask):
    return lax.ppermute(value, "tensor", [(i, i ^ mask) for i in range(PARTS)])


def normalize(rows, gain):
    values = rows.astype(jnp.float32)
    scale = lax.rsqrt(jnp.mean(values * values, axis=-1, keepdims=True) + 1e-05)
    return (values * scale * gain.astype(jnp.float32)).astype(jnp.bfloat16)


def turn_heads(values, cosine, sine):
    out = []
    for at in range(0, values.shape[1], HD):
        left, right = values[:, at : at + HALF], values[:, at + HALF : at + HD]
        out += [left * cosine - right * sine, right * cosine + left * sine]
    return jnp.concatenate(out, axis=1).astype(jnp.bfloat16)


def held(weights):
    return pltpu.with_memory_space_constraint(weights, pltpu.HBM)


def together(*values):
    return lax.optimization_barrier(values)


def keys_after(order, steps):
    keys = [0]
    for mask in order[:steps]:
        keys = keys + [key ^ mask for key in keys]
    return keys


def step_up(have, step):
    return [swap(block, order[step]) for block, (_, _, order) in zip(have, PIECES)]


def in_order(blocks, order, rows):
    keys = keys_after(order, 3)
    at = [keys.index(m) * rows for m in BLOCKS]
    return jnp.concatenate([blocks[i : i + rows] for i in at], axis=0)


def add(one, two):
    return (one.astype(jnp.float32) + two.astype(jnp.float32)).astype(jnp.bfloat16)


def step_down(totals, step):
    keep, got = [], []
    for total, (_, _, order) in zip(totals, PIECES):
        left = [mask for mask in LINKS if mask not in order[:step]]
        at = left.index(order[step])
        keep.append(lax.index_in_dim(total, 0, at, keepdims=False))
        got.append(swap(lax.index_in_dim(total, 1, at, keepdims=False), order[step]))
    return keep, got


def added(keep, got):
    return [add(one, two) for one, two in zip(keep, got)]


def with_heads(query, key, value, mixed):
    rows, columns = query.shape
    tile = rows // 2
    for h in range(columns // HD):
        for at in range(0, rows, tile):
            scores = lax.dot_general(
                query[at : at + tile, HD * h : HD * (h + 1)],
                key,
                (((1,), (1,)), ((), ())),
                preferred_element_type=jnp.float32,
            ) * HD ** (-0.5)
            weights = jnp.exp(scores - jnp.max(scores, axis=-1, keepdims=True))
            probs = weights * (1.0 / jnp.sum(weights, axis=-1, keepdims=True))
            mixed[at : at + tile, HD * h : HD * (h + 1)] = jnp.dot(
                probs.astype(jnp.bfloat16), value, preferred_element_type=jnp.float32
            ).astype(jnp.bfloat16)


class Ring:
    def __init__(self, source, here, sems, along):
        self.source, self.here, self.sems, self.along = source, here, sems, along
        for i in range(here.shape[0]):
            self.copy(i).start()

    def slot(self, i):
        width, at = CHUNKS[i][1], i % self.here.shape[0]
        return self.here.at[at, :width, :] if self.along == 0 else self.here.at[at, :, :width]

    def copy(self, i):
        some = pl.ds(*CHUNKS[i])
        source = self.source.at[some, :] if self.along == 0 else self.source.at[:, some]
        return pltpu.make_async_copy(source, self.slot(i), self.sems.at[i % self.here.shape[0]])

    def take(self, i):
        self.copy(i).wait()
        return self.slot(i)[...]

    def done(self, i):
        if i + self.here.shape[0] < len(CHUNKS):
            self.copy(i + self.here.shape[0]).start()


def project_out(mixed, ring, outs):
    half = mixed.shape[0] // 2
    for i, (first, width) in enumerate(CHUNKS):
        weights = ring.take(i)
        at = (i % 2) * width
        for side in range(2):
            outs[2 * (i // 2) + side][:, at : at + width] = jnp.dot(
                mixed[half * side : half * (side + 1), :], weights, preferred_element_type=jnp.float32
            ).astype(jnp.bfloat16)
        ring.done(i)


def first_kernel(query, pair, out_hbm, *rest):
    outs, (mixed, out_here, sems) = rest[:6], rest[6:]
    ring = Ring(out_hbm, out_here, sems, 1)
    with_heads(query, pair[:, :HD], pair[:, HD:], mixed)
    project_out(mixed, ring, outs)


def turned(values, cosine, sine):
    return (values * cosine + pltpu.roll(values, HALF, 1) * sine).astype(jnp.bfloat16)


def second_kernel(*refs):
    raw, refs = refs[:6], refs[6:]
    gain, cosine, sine, match, base, kv_here, query_hbm, out_hbm = refs[:8]
    outs, refs = refs[8:14], refs[14:]
    normed, moving, placed, mixed, query_here, out_here, query_sems, out_sems = refs
    query_ring = Ring(query_hbm, query_here, query_sems, 0)
    out_ring = Ring(out_hbm, out_here, out_sems, 1)
    half = raw[0].shape[0]
    width_all = gain.shape[1]
    scales = []
    for side in range(2):
        squares = jnp.zeros((half, HD), jnp.float32)
        for piece in range(3):
            ref = raw[2 * piece + side]

            def add_squares(i, squares, ref=ref):
                values = ref[:, pl.ds(pl.multiple_of(i * HD, HD), HD)].astype(jnp.float32)
                return squares + values * values

            squares = lax.fori_loop(0, ref.shape[1] // HD, add_squares, squares, unroll=2)
        mean = jnp.sum(squares, axis=-1, keepdims=True) * (1.0 / width_all)
        scales.append(lax.rsqrt(mean + 1e-05))
    queries = jnp.zeros((2 * half, query_hbm.shape[1]), jnp.float32)
    pairs = jnp.zeros((2 * half, kv_here.shape[0]), jnp.float32)
    for i, (first, width) in enumerate(CHUNKS):
        at = (i % 2) * width
        for side in range(2):
            values = raw[2 * (i // 2) + side][:, at : at + width].astype(jnp.float32)
            normed[half * side : half * (side + 1), :width] = (
                values * scales[side] * gain[:, first : first + width]
            ).astype(jnp.bfloat16)
        some = normed[:, :width]
        queries += jnp.dot(some, query_ring.take(i), preferred_element_type=jnp.float32)
        query_ring.done(i)
        pairs += dot_rows(some, kv_here[:, first : first + width])
    moving[:, :HD] = turned(pairs[:, :HD], cosine[...], sine[...])
    moving[:, HD : 2 * HD] = pairs[:, HD:].astype(jnp.bfloat16)
    for h in range(queries.shape[1] // HD):
        moving[:, HD * (h + 2) : HD * (h + 3)] = turned(queries[:, HD * h : HD * (h + 1)], cosine[...], sine[...])
    placed[...] = base[...] + jnp.dot(
        match[...], moving[...], preferred_element_type=jnp.float32
    ).astype(jnp.bfloat16)
    with_heads(placed.at[:, 2 * HD :], placed[:, :HD], placed[:, HD : 2 * HD], mixed)
    project_out(mixed, out_ring, outs)


def dot_rows(x, weights):
    return lax.dot_general(x, weights, (((1,), (1,)), ((), ())), preferred_element_type=jnp.float32)


def query_kernel(one, two, three, weights, out, total):
    rows = out.shape[0] // 8
    for i, (piece, (first, width, order)) in enumerate(zip((one, two, three), PIECES)):
        total[...] = jnp.dot(piece[...], weights[first : first + width, :], preferred_element_type=jnp.float32)
        for j, key in enumerate(keys_after(order, 3)):
            at = BLOCKS.index(key) * rows
            some = total[j * rows : (j + 1) * rows, :]
            if i == 0:
                out[at : at + rows, :] = some
            else:
                out[at : at + rows, :] += some


def dot_rows(x, weights):
    return lax.dot_general(x, weights, (((1,), (1,)), ((), ())), preferred_element_type=jnp.float32)


def call_kernel(kernel, operands, outs, scratch=(), mib=16, last=()):
    places = [pltpu.VMEM] * (len(operands) - len(last)) + list(last)
    return pl.pallas_call(
        kernel,
        out_shape=[jax.ShapeDtypeStruct(*out) for out in outs],
        in_specs=[pl.BlockSpec(memory_space=place) for place in places],
        out_specs=[pl.BlockSpec(memory_space=pltpu.VMEM)] * len(outs),
        scratch_shapes=list(scratch),
        compiler_params=pltpu.CompilerParams(vmem_limit_bytes=mib * 2**20),
        cost_estimate=pl.CostEstimate(flops=1000000, bytes_accessed=100000, transcendentals=0),
    )(*operands)


def join_kernel(*refs):
    for i in range(3):
        have, got, out = refs[i], refs[3 + i], refs[6 + i]
        rows = have.shape[0]
        out[:rows, :] = have[...]
        out[rows:, :] = got[...]


def joined(have, got):
    outs = [((2 * block.shape[0], block.shape[1]), block.dtype) for block in have]
    return call_kernel(join_kernel, [*have, *got], outs, mib=12)


def weight_rows_kernel(key, value, other_key, other_value, place, out):
    even = place[0, 0] % 2 == 0

    @pl.when(even)
    def _():
        out[:HALF, :] = key[...]
        out[HALF : 2 * HALF, :] = other_key[...]
        out[2 * HALF : 3 * HALF, :] = value[...]
        out[3 * HALF :, :] = other_value[...]

    @pl.when(jnp.logical_not(even))
    def _():
        out[:HALF, :] = other_key[...]
        out[HALF : 2 * HALF, :] = key[...]
        out[2 * HALF : 3 * HALF, :] = other_value[...]
        out[3 * HALF :, :] = value[...]


def table_kernel(positions, freq, place, cosine, sine, list_cosine, list_sine, match, flags):
    f32, bf16 = jnp.float32, jnp.bfloat16
    count, length = match.shape[1], match.shape[0]
    rows = length // PARTS
    at = lax.broadcasted_iota(jnp.int32, (length, 1), 0)
    block = at // rows
    offset = (block // 8) * CORE ^ (block // 4 % 2) * NEAR ^ (block // 2 % 2) * FAR ^ (block % 2) * ZED
    spots = (place[0, 0] ^ offset) * rows + at % rows
    listed = (lax.broadcasted_iota(jnp.int32, (count, 1), 0) + place[0, 0] % 2 * (count // 2)) % count
    ones_across, twos_across = positions[:1, :], positions[1:, :]
    row = lax.broadcasted_iota(jnp.int32, (count, count), 0)
    column = lax.broadcasted_iota(jnp.int32, (count, count), 1)
    twos = jnp.sum(jnp.where(row == column, twos_across, 0), axis=1, keepdims=True)
    stale = jnp.max(jnp.where(twos == ones_across, 1.0, 0.0), axis=0, keepdims=True)
    fresh = 1.0 - stale
    before = jnp.where(row < column, 1.0, 0.0).astype(bf16)

    def ahead(flag):
        wide = jnp.broadcast_to(flag, (16, count)).astype(bf16)
        return jnp.dot(wide, before, preferred_element_type=f32)[:1]

    rank = jnp.where(fresh > 0, ahead(fresh), jnp.sum(fresh, axis=1, keepdims=True) + ahead(stale))
    spot = jnp.where(listed.astype(f32) == rank, 1.0, 0.0)
    list_spots = jnp.sum(spot * ones_across.astype(f32), axis=1, keepdims=True)
    here = jnp.where((spots == ones_across) & (fresh > 0), 1.0, 0.0)
    match[...] = dot_rows(here.astype(bf16), spot.astype(bf16)).astype(bf16)
    is_list = jnp.max(here, axis=1, keepdims=True)
    masked_1 = jnp.max(jnp.where(spots == twos_across, 1.0, 0.0), axis=1, keepdims=True)
    lane = lax.broadcasted_iota(jnp.int32, (spots.shape[0], HD), 1)
    flags[...] = jnp.where(lane == 0, masked_1, is_list)
    sign = jnp.where(lax.broadcasted_iota(jnp.int32, (1, HD), 1) < HALF, -1.0, 1.0)
    angle = spots.astype(f32) * freq[...]
    cosine[...] = jnp.cos(angle)
    sine[...] = jnp.sin(angle) * sign
    angle = list_spots * freq[...]
    list_cosine[...] = jnp.cos(angle)
    list_sine[...] = jnp.sin(angle) * sign


def mask_kernel(embed, gain, query_here, kv_here, cosine, sine, list_cosine, list_sine, query, base):
    values = embed[...].astype(jnp.float32)
    mean = jnp.sum(values * values, axis=-1, keepdims=True) * (1.0 / embed.shape[1])
    row = (values * lax.rsqrt(mean + 1e-05) * gain[...]).astype(jnp.bfloat16)
    row = jnp.broadcast_to(row, (16, row.shape[1]))
    queries = jnp.dot(row, query_here[...], preferred_element_type=jnp.float32)[:1]
    pairs = dot_rows(row, kv_here[...])[:1]
    length = base.shape[0]
    base[:, :HD] = turned(jnp.broadcast_to(pairs[:, :HD], (length, HD)), cosine[...], sine[...])
    base[:, HD : 2 * HD] = jnp.broadcast_to(pairs[:, HD:], (length, HD)).astype(jnp.bfloat16)
    for at in range(0, queries.shape[1], HD):
        some = queries[:, at : at + HD]
        base[:, 2 * HD + at : 3 * HD + at] = turned(jnp.broadcast_to(some, (length, HD)), cosine[...], sine[...])
        query[:, at : at + HD] = turned(
            jnp.broadcast_to(some, (query.shape[0], HD)), list_cosine[...], list_sine[...]
        )


def add_pairs(pieces, kv_here, total, low, fresh):
    rows = total.shape[0] // 8
    for piece, (first, width, order) in zip(pieces, PIECES):
        product = dot_rows(piece[...], kv_here[:, first : first + width])
        for i, key in enumerate(keys_after(order, 3)[low : low + 4]):
            at = BLOCKS.index(key) * rows
            some = product[i * rows : (i + 1) * rows]
            if key in fresh:
                fresh.remove(key)
                total[at : at + rows, :] = some
            else:
                total[at : at + rows, :] += some


def early_kernel(one, two, three, kv_here, total):
    fresh = set(BLOCKS)
    add_pairs((one, two, three), kv_here, total, 0, fresh)
    rows = total.shape[0] // 8
    for key in fresh:
        at = BLOCKS.index(key) * rows
        total[at : at + rows, :] = jnp.zeros((rows, total.shape[1]), jnp.float32)


def late_kernel(one, two, three, kv_here, early, cosine, sine, out, total):
    total[...] = early[...]
    add_pairs((one, two, three), kv_here, total, 4, set())
    rows = total.shape[0]
    out[:, :HD] = turned(total[:, :HD], cosine[:rows, :], sine[:rows, :])
    out[:, HD:] = total[:, HD:].astype(jnp.bfloat16)


def chosen(spots, positions):
    return jnp.any(spots[:, None] == positions[None, :], axis=1)


def pick(one_hot, rows):
    return jnp.dot(
        one_hot.astype(jnp.bfloat16), rows, preferred_element_type=jnp.float32
    ).astype(jnp.bfloat16)


def shards(tokens, positions, mask_embed, norm_gain, w_query, w_key, w_value, w_out):
    place = lax.axis_index("tensor")
    rows = tokens.shape[0]
    length = rows * PARTS

    own_spots = place * rows + jnp.arange(rows, dtype=jnp.int32)
    own_masked_0 = chosen(own_spots, positions[0])
    hidden_0 = jnp.where(own_masked_0[:, None], mask_embed[None, :], tokens)
    normed_0 = normalize(hidden_0, norm_gain)
    key_rows, value_rows = w_key.T, w_value.T
    normed_0, positions, place, key_rows, value_rows = together(normed_0, positions, place, key_rows, value_rows)
    have = [normed_0[:, first : first + width] for first, width, _ in PIECES]

    f32, bf16 = jnp.float32, jnp.bfloat16
    count, columns = positions.shape[1], w_query.shape[1]
    freq = 500000.0 ** (-(jnp.arange(HD, dtype=f32) % HALF * 2.0 / HD))
    cosine, sine, list_cosine, list_sine, match, flags = call_kernel(
        table_kernel,
        [positions, freq[None], place.reshape(1, 1)],
        [((length, HD), f32)] * 2 + [((count, HD), f32)] * 2 + [((length, count), bf16), ((length, HD), f32)],
        last=[pltpu.SMEM],
    )
    other_rows = swap(key_rows, CORE), swap(value_rows, CORE)
    tables = (cosine, sine, list_cosine, list_sine, match, flags)
    got, tables, other_rows, place = together(step_up(have, 0), tables, other_rows, place)
    cosine, sine, list_cosine, list_sine, match, flags = tables
    have = joined(have, got)

    def head_weights(place):
        (weights,) = call_kernel(
            weight_rows_kernel,
            [key_rows, value_rows, *other_rows, place.reshape(1, 1)],
            [((4 * HALF, key_rows.shape[1]), bf16)],
            last=[pltpu.SMEM],
        )
        return weights

    kv_weights = head_weights(place)
    got, kv_weights, mask_embed, norm_gain = together(step_up(have, 1), kv_weights, mask_embed, norm_gain)
    have = joined(have, got)

    gain = norm_gain[None, :].astype(f32)
    query_0, base_mask = call_kernel(
        mask_kernel,
        [mask_embed[None, :], gain, w_query, kv_weights, cosine, sine, list_cosine, list_sine],
        [((count, columns), bf16), ((length, columns + 2 * HD), bf16)],
    )
    (early,) = call_kernel(early_kernel, [*have, kv_weights], [((length // 2, 2 * HD), f32)])
    got, query_0, base_mask, early = together(step_up(have, 2), query_0, base_mask, early)

    (pair_own,) = call_kernel(
        late_kernel,
        [*got, kv_weights, early, cosine, sine],
        [((length // 2, 2 * HD), bf16)],
        [pltpu.VMEM((length // 2, 2 * HD), f32)],
    )
    slots, wide = 3, CHUNKS[0][1]
    out_ring = [pltpu.VMEM((slots, columns, wide), bf16), pltpu.SemaphoreType.DMA((slots,))]
    query_ring = [pltpu.VMEM((slots, wide, columns), bf16), pltpu.SemaphoreType.DMA((slots,))]
    x_own = joined(have, got)
    pair_other, x_own = together(swap(pair_own, CORE), x_own)
    pair = jnp.concatenate([pair_own, pair_other], axis=0)
    x_other = [swap(block, CORE) for block in x_own]
    outs = call_kernel(
        first_kernel,
        [query_0, pair, held(w_out)],
        [((count // 2, width), bf16) for _, width, _ in PIECES for _ in range(2)],
        [pltpu.VMEM((count, columns), bf16), *out_ring],
        GRANT,
        [pltpu.HBM],
    )
    outs, x_other, x_own = together(outs, x_other, x_own)

    def queries_of(x):
        (queries,) = call_kernel(
            query_kernel,
            [*x, w_query],
            [((length // 2, columns), f32)],
            [pltpu.VMEM((length // 2, columns), f32)],
        )
        return queries

    bits = {NEAR: ((place >> 2) ^ (place >> 3)) % 2 == 1, FAR: (place >> 3) % 2 == 1, ZED: (place >> 1) % 2 == 1}
    sides = [bits[order[0]] for _, _, order in PIECES]
    came = [swap(outs[2 * i + 1], CORE) for i in range(3)]
    came, x_own = together(came, x_own)
    totals = [add(outs[2 * i], came[i]) for i in range(3)]
    keep, send = [], []
    for total, side in zip(totals, sides):
        middle = total.shape[1] // 2
        left, right = total[:, :middle], total[:, middle:]
        keep.append(jnp.where(side, right, left))
        send.append(jnp.where(side, left, right))
    got = [swap(block, order[0]) for block, (_, _, order) in zip(send, PIECES)]

    got, query_own, x_other = together(got, queries_of(x_own), x_other)
    totals = added(keep, got)
    got, query_other = together(step_up(totals, 1), queries_of(x_other))
    totals = added(totals, got)
    got, place = together(step_up(totals, 2), place)
    totals = added(totals, got)
    states = []
    for (first, width, _), total, side in zip(PIECES, totals, sides):
        row = mask_embed[None, first : first + width]
        middle = width // 2
        states.append(add(jnp.where(side, row[:, middle:], row[:, :middle]), total))
    masked_1, is_list = flags[:, :1] > 0, flags[:, 1:2] > 0
    base_tokens = jnp.concatenate(
        [pair, turn_heads(jnp.concatenate([query_own, query_other], axis=0), cosine[:, :HALF], sine[:, HALF:])], axis=1
    )
    base = jnp.where(masked_1, base_mask, jnp.where(is_list, jnp.zeros_like(base_tokens), base_tokens))
    kv_weights = head_weights(place)
    got, base, kv_weights = together(step_up(states, 0), base, kv_weights)
    raw = []
    for state, block, side in zip(states, got, sides):
        raw.append(
            jnp.where(
                side, jnp.concatenate([block, state], axis=1), jnp.concatenate([state, block], axis=1)
            )
        )
    raw = [(block, swap(block, CORE)) for block in raw]

    operands = [half for both in raw for half in both]
    operands += [gain, list_cosine, list_sine, match, base, kv_weights, held(w_query), held(w_out)]
    outs = call_kernel(
        second_kernel,
        operands,
        [((length // 2, width), bf16) for _, width, _ in PIECES for _ in range(2)],
        [
            pltpu.VMEM((count, CHUNKS[0][1]), bf16),
            pltpu.VMEM((count, columns + 2 * HD), bf16),
            pltpu.VMEM((length, columns + 2 * HD), bf16),
            pltpu.VMEM((length, columns), bf16),
            query_ring[0],
            out_ring[0],
            query_ring[1],
            out_ring[1],
        ],
        GRANT,
        [pltpu.HBM, pltpu.HBM],
    )
    keep, send = outs[::2], outs[1::2]
    totals = [
        add(one, swap(two, CORE)).reshape(2, 2, 2, rows, one.shape[1]) for one, two in zip(keep, send)
    ]
    keep, incoming = step_down(totals, 0)
    own_match = match[:rows]
    middle = count // 2
    states = jnp.concatenate(
        [pick(own_match[:, :middle], one) + pick(own_match[:, middle:], two) for one, two in raw], axis=1
    )
    hidden_1 = jnp.where(
        masked_1[:rows], mask_embed[None, :], jnp.where(is_list[:rows], states, tokens)
    )
    incoming, hidden_1 = together(incoming, hidden_1)
    keep, incoming = step_down(added(keep, incoming), 1)
    incoming = together(*incoming)
    keep, incoming = step_down(added(keep, incoming), 2)
    incoming = together(*incoming)
    summed_1 = jnp.concatenate(added(keep, incoming), axis=1)
    return (hidden_1.astype(jnp.float32) + summed_1.astype(jnp.float32)).astype(jnp.bfloat16)


def solution(mesh):
    placed = (
        P(("dp", "tensor"), None),
        P("dp", None),
        P(),
        P(),
        P(None, "tensor"),
        P(None, "tensor"),
        P(None, "tensor"),
        P("tensor", None),
    )
    return jax.shard_map(
        shards, mesh=mesh, in_specs=placed, out_specs=P(("dp", "tensor"), None), check_vma=False
    )
```

```python
import jax
import jax.numpy as jnp
from jax import lax
from jax.experimental import pallas as pl
from jax.experimental.pallas import tpu as pltpu
from jax.sharding import PartitionSpec as P

HD = 128
HALF = HD // 2
PARTS = 16
CORE, ZED, NEAR, FAR = 1, 2, 4, 12
LINKS = (NEAR, FAR, ZED)
PIECES = (
    (0, 2816, (NEAR, FAR, ZED)),
    (2816, 2816, (FAR, ZED, NEAR)),
    (5632, 2560, (ZED, NEAR, FAR)),
)
CHUNKS = [(first + i * width // 2, width // 2) for first, width, _ in PIECES for i in range(2)]
BLOCKS = [a ^ b ^ c for a in (0, NEAR) for b in (0, FAR) for c in (0, ZED)]


def swap(value, mask):
    return lax.ppermute(value, "tensor", [(i, i ^ mask) for i in range(PARTS)])


def normalize(rows, gain):
    values = rows.astype(jnp.float32)
    scale = lax.rsqrt(jnp.mean(values * values, axis=-1, keepdims=True) + 1e-05)
    return (values * scale * gain.astype(jnp.float32)).astype(jnp.bfloat16)


def turn_heads(values, cosine, sine):
    out = []
    for at in range(0, values.shape[1], HD):
        left, right = values[:, at : at + HALF], values[:, at + HALF : at + HD]
        out += [left * cosine - right * sine, right * cosine + left * sine]
    return jnp.concatenate(out, axis=1).astype(jnp.bfloat16)


def together(*values):
    return lax.optimization_barrier(values)


def keys_after(order, steps):
    keys = [0]
    for mask in order[:steps]:
        keys = keys + [key ^ mask for key in keys]
    return keys


def step_up(have, step):
    return [swap(block, order[step]) for block, (_, _, order) in zip(have, PIECES)]


def in_order(blocks, order, rows):
    keys = keys_after(order, 3)
    at = [keys.index(m) * rows for m in BLOCKS]
    return jnp.concatenate([blocks[i : i + rows] for i in at], axis=0)


def add(one, two):
    return (one.astype(jnp.float32) + two.astype(jnp.float32)).astype(jnp.bfloat16)


def step_down(totals, step):
    keep, got = [], []
    for total, (_, _, order) in zip(totals, PIECES):
        left = [mask for mask in LINKS if mask not in order[:step]]
        at = left.index(order[step])
        keep.append(lax.index_in_dim(total, 0, at, keepdims=False))
        got.append(swap(lax.index_in_dim(total, 1, at, keepdims=False), order[step]))
    return keep, got


def added(keep, got):
    return [add(one, two) for one, two in zip(keep, got)]


def with_heads(query, key, value, mixed):
    rows, columns = query.shape
    tile = rows // 2
    for h in range(columns // HD):
        for at in range(0, rows, tile):
            scores = lax.dot_general(
                query[at : at + tile, HD * h : HD * (h + 1)],
                key,
                (((1,), (1,)), ((), ())),
                preferred_element_type=jnp.float32,
            ) * HD ** (-0.5)
            weights = jnp.exp(scores - jnp.max(scores, axis=-1, keepdims=True))
            probs = weights * (1.0 / jnp.sum(weights, axis=-1, keepdims=True))
            mixed[at : at + tile, HD * h : HD * (h + 1)] = jnp.dot(
                probs.astype(jnp.bfloat16), value, preferred_element_type=jnp.float32
            ).astype(jnp.bfloat16)


def project_out(mixed, out_here, outs):
    half = mixed.shape[0] // 2
    for i, (first, width) in enumerate(CHUNKS):
        weights = out_here[:, first : first + width]
        at = (i % 2) * width
        for side in range(2):
            outs[2 * (i // 2) + side][:, at : at + width] = jnp.dot(
                mixed[half * side : half * (side + 1), :], weights, preferred_element_type=jnp.float32
            ).astype(jnp.bfloat16)


def first_kernel(query, pair, out_here, *rest):
    outs, (mixed,) = rest[:6], rest[6:]
    with_heads(query, pair[:, :HD], pair[:, HD:], mixed)
    project_out(mixed, out_here, outs)


def turned(values, cosine, sine):
    return (values * cosine + pltpu.roll(values, HALF, 1) * sine).astype(jnp.bfloat16)


def second_kernel(*refs):
    raw, refs = refs[:6], refs[6:]
    gain, cosine, sine, match, base, query_here, kv_here, out_here = refs[:8]
    outs, refs = refs[8:14], refs[14:]
    normed, moving, placed, mixed = refs
    half = raw[0].shape[0]
    width_all = gain.shape[1]
    scales = []
    for side in range(2):
        squares = jnp.zeros((half, HD), jnp.float32)
        for piece in range(3):
            ref = raw[2 * piece + side]

            def add_squares(i, squares, ref=ref):
                values = ref[:, pl.ds(pl.multiple_of(i * HD, HD), HD)].astype(jnp.float32)
                return squares + values * values

            squares = lax.fori_loop(0, ref.shape[1] // HD, add_squares, squares, unroll=2)
        mean = jnp.sum(squares, axis=-1, keepdims=True) * (1.0 / width_all)
        scales.append(lax.rsqrt(mean + 1e-05))
    queries = jnp.zeros((2 * half, query_here.shape[1]), jnp.float32)
    pairs = jnp.zeros((2 * half, kv_here.shape[0]), jnp.float32)
    for i, (first, width) in enumerate(CHUNKS):
        at = (i % 2) * width
        for side in range(2):
            values = raw[2 * (i // 2) + side][:, at : at + width].astype(jnp.float32)
            normed[half * side : half * (side + 1), :width] = (
                values * scales[side] * gain[:, first : first + width]
            ).astype(jnp.bfloat16)
        some = normed[:, :width]
        queries += jnp.dot(some, query_here[first : first + width, :], preferred_element_type=jnp.float32)
        pairs += dot_rows(some, kv_here[:, first : first + width])
    moving[:, :HD] = turned(pairs[:, :HD], cosine[...], sine[...])
    moving[:, HD : 2 * HD] = pairs[:, HD:].astype(jnp.bfloat16)
    for h in range(queries.shape[1] // HD):
        moving[:, HD * (h + 2) : HD * (h + 3)] = turned(queries[:, HD * h : HD * (h + 1)], cosine[...], sine[...])
    placed[...] = base[...] + jnp.dot(
        match[...], moving[...], preferred_element_type=jnp.float32
    ).astype(jnp.bfloat16)
    with_heads(placed.at[:, 2 * HD :], placed[:, :HD], placed[:, HD : 2 * HD], mixed)
    project_out(mixed, out_here, outs)


def dot_rows(x, weights):
    return lax.dot_general(x, weights, (((1,), (1,)), ((), ())), preferred_element_type=jnp.float32)


def call_kernel(kernel, operands, outs, scratch=(), mib=16, last=(), moved=100000):
    places = [pltpu.VMEM] * (len(operands) - len(last)) + list(last)
    return pl.pallas_call(
        kernel,
        out_shape=[jax.ShapeDtypeStruct(*out) for out in outs],
        in_specs=[pl.BlockSpec(memory_space=place) for place in places],
        out_specs=[pl.BlockSpec(memory_space=pltpu.VMEM)] * len(outs),
        scratch_shapes=list(scratch),
        compiler_params=pltpu.CompilerParams(vmem_limit_bytes=mib * 2**20),
        cost_estimate=pl.CostEstimate(flops=1000000, bytes_accessed=moved, transcendentals=0),
    )(*operands)


def join_kernel(*refs):
    for i in range(3):
        have, got, out = refs[i], refs[3 + i], refs[6 + i]
        rows = have.shape[0]
        out[:rows, :] = have[...]
        out[rows:, :] = got[...]


def joined(have, got):
    outs = [((2 * block.shape[0], block.shape[1]), block.dtype) for block in have]
    return call_kernel(join_kernel, [*have, *got], outs, mib=12)


def weight_rows_kernel(key, value, other_key, other_value, place, out):
    even = place[0, 0] % 2 == 0

    @pl.when(even)
    def _():
        out[:HALF, :] = key[...]
        out[HALF : 2 * HALF, :] = other_key[...]
        out[2 * HALF : 3 * HALF, :] = value[...]
        out[3 * HALF :, :] = other_value[...]

    @pl.when(jnp.logical_not(even))
    def _():
        out[:HALF, :] = other_key[...]
        out[HALF : 2 * HALF, :] = key[...]
        out[2 * HALF : 3 * HALF, :] = other_value[...]
        out[3 * HALF :, :] = value[...]


def table_kernel(positions, freq, place, cosine, sine, list_cosine, list_sine, match, flags):
    f32, bf16 = jnp.float32, jnp.bfloat16
    count, length = match.shape[1], match.shape[0]
    rows = length // PARTS
    at = lax.broadcasted_iota(jnp.int32, (length, 1), 0)
    block = at // rows
    offset = (block // 8) * CORE ^ (block // 4 % 2) * NEAR ^ (block // 2 % 2) * FAR ^ (block % 2) * ZED
    spots = (place[0, 0] ^ offset) * rows + at % rows
    listed = (lax.broadcasted_iota(jnp.int32, (count, 1), 0) + place[0, 0] % 2 * (count // 2)) % count
    ones_across, twos_across = positions[:1, :], positions[1:, :]
    row = lax.broadcasted_iota(jnp.int32, (count, count), 0)
    column = lax.broadcasted_iota(jnp.int32, (count, count), 1)
    twos = jnp.sum(jnp.where(row == column, twos_across, 0), axis=1, keepdims=True)
    stale = jnp.max(jnp.where(twos == ones_across, 1.0, 0.0), axis=0, keepdims=True)
    fresh = 1.0 - stale
    before = jnp.where(row < column, 1.0, 0.0).astype(bf16)

    def ahead(flag):
        wide = jnp.broadcast_to(flag, (16, count)).astype(bf16)
        return jnp.dot(wide, before, preferred_element_type=f32)[:1]

    rank = jnp.where(fresh > 0, ahead(fresh), jnp.sum(fresh, axis=1, keepdims=True) + ahead(stale))
    spot = jnp.where(listed.astype(f32) == rank, 1.0, 0.0)
    list_spots = jnp.sum(spot * ones_across.astype(f32), axis=1, keepdims=True)
    here = jnp.where((spots == ones_across) & (fresh > 0), 1.0, 0.0)
    match[...] = dot_rows(here.astype(bf16), spot.astype(bf16)).astype(bf16)
    is_list = jnp.max(here, axis=1, keepdims=True)
    masked_1 = jnp.max(jnp.where(spots == twos_across, 1.0, 0.0), axis=1, keepdims=True)
    lane = lax.broadcasted_iota(jnp.int32, (spots.shape[0], HD), 1)
    flags[...] = jnp.where(lane == 0, masked_1, is_list)
    sign = jnp.where(lax.broadcasted_iota(jnp.int32, (1, HD), 1) < HALF, -1.0, 1.0)
    angle = spots.astype(f32) * freq[...]
    cosine[...] = jnp.cos(angle)
    sine[...] = jnp.sin(angle) * sign
    angle = list_spots * freq[...]
    list_cosine[...] = jnp.cos(angle)
    list_sine[...] = jnp.sin(angle) * sign


def mask_kernel(embed, gain, query_here, kv_here, cosine, sine, list_cosine, list_sine, query, base):
    values = embed[...].astype(jnp.float32)
    mean = jnp.sum(values * values, axis=-1, keepdims=True) * (1.0 / embed.shape[1])
    row = (values * lax.rsqrt(mean + 1e-05) * gain[...]).astype(jnp.bfloat16)
    row = jnp.broadcast_to(row, (16, row.shape[1]))
    queries = jnp.dot(row, query_here[...], preferred_element_type=jnp.float32)[:1]
    pairs = dot_rows(row, kv_here[...])[:1]
    length = base.shape[0]
    base[:, :HD] = turned(jnp.broadcast_to(pairs[:, :HD], (length, HD)), cosine[...], sine[...])
    base[:, HD : 2 * HD] = jnp.broadcast_to(pairs[:, HD:], (length, HD)).astype(jnp.bfloat16)
    for at in range(0, queries.shape[1], HD):
        some = queries[:, at : at + HD]
        base[:, 2 * HD + at : 3 * HD + at] = turned(jnp.broadcast_to(some, (length, HD)), cosine[...], sine[...])
        query[:, at : at + HD] = turned(
            jnp.broadcast_to(some, (query.shape[0], HD)), list_cosine[...], list_sine[...]
        )


def add_pairs(pieces, kv_here, total, low, fresh):
    rows = total.shape[0] // 8
    for piece, (first, width, order) in zip(pieces, PIECES):
        product = dot_rows(piece[...], kv_here[:, first : first + width])
        for i, key in enumerate(keys_after(order, 3)[low : low + 4]):
            at = BLOCKS.index(key) * rows
            some = product[i * rows : (i + 1) * rows]
            if key in fresh:
                fresh.remove(key)
                total[at : at + rows, :] = some
            else:
                total[at : at + rows, :] += some


def early_kernel(one, two, three, kv_here, total):
    fresh = set(BLOCKS)
    add_pairs((one, two, three), kv_here, total, 0, fresh)
    rows = total.shape[0] // 8
    for key in fresh:
        at = BLOCKS.index(key) * rows
        total[at : at + rows, :] = jnp.zeros((rows, total.shape[1]), jnp.float32)


def late_kernel(one, two, three, kv_here, early, cosine, sine, out, total):
    total[...] = early[...]
    add_pairs((one, two, three), kv_here, total, 4, set())
    rows = total.shape[0]
    out[:, :HD] = turned(total[:, :HD], cosine[:rows, :], sine[:rows, :])
    out[:, HD:] = total[:, HD:].astype(jnp.bfloat16)


def chosen(spots, positions):
    return jnp.any(spots[:, None] == positions[None, :], axis=1)


def pick(one_hot, rows):
    return jnp.dot(
        one_hot.astype(jnp.bfloat16), rows, preferred_element_type=jnp.float32
    ).astype(jnp.bfloat16)


def shards(tokens, positions, mask_embed, norm_gain, w_query, w_key, w_value, w_out):
    place = lax.axis_index("tensor")
    rows = tokens.shape[0]
    length = rows * PARTS

    own_spots = place * rows + jnp.arange(rows, dtype=jnp.int32)
    own_masked_0 = chosen(own_spots, positions[0])
    hidden_0 = jnp.where(own_masked_0[:, None], mask_embed[None, :], tokens)
    normed_0 = normalize(hidden_0, norm_gain)
    key_rows, value_rows = w_key.T, w_value.T
    normed_0, positions, place, key_rows, value_rows = together(normed_0, positions, place, key_rows, value_rows)
    have = [normed_0[:, first : first + width] for first, width, _ in PIECES]

    f32, bf16 = jnp.float32, jnp.bfloat16
    count, columns = positions.shape[1], w_query.shape[1]
    freq = 500000.0 ** (-(jnp.arange(HD, dtype=f32) % HALF * 2.0 / HD))
    cosine, sine, list_cosine, list_sine, match, flags = call_kernel(
        table_kernel,
        [positions, freq[None], place.reshape(1, 1)],
        [((length, HD), f32)] * 2 + [((count, HD), f32)] * 2 + [((length, count), bf16), ((length, HD), f32)],
        last=[pltpu.SMEM],
    )
    other_rows = swap(key_rows, CORE), swap(value_rows, CORE)
    tables = (cosine, sine, list_cosine, list_sine, match, flags)
    got, tables, other_rows, place = together(step_up(have, 0), tables, other_rows, place)
    cosine, sine, list_cosine, list_sine, match, flags = tables
    have = joined(have, got)

    def head_weights(place, moved):
        (weights,) = call_kernel(
            weight_rows_kernel,
            [key_rows, value_rows, *other_rows, place.reshape(1, 1)],
            [((4 * HALF, key_rows.shape[1]), bf16)],
            last=[pltpu.SMEM],
            moved=moved,
        )
        return weights

    kv_weights = head_weights(place, 100000)
    got, kv_weights, mask_embed, norm_gain = together(step_up(have, 1), kv_weights, mask_embed, norm_gain)
    have = joined(have, got)

    gain = norm_gain[None, :].astype(f32)
    query_0, base_mask = call_kernel(
        mask_kernel,
        [mask_embed[None, :], gain, w_query, kv_weights, cosine, sine, list_cosine, list_sine],
        [((count, columns), bf16), ((length, columns + 2 * HD), bf16)],
    )
    (early,) = call_kernel(early_kernel, [*have, kv_weights], [((length // 2, 2 * HD), f32)])
    got, query_0, base_mask, early = together(step_up(have, 2), query_0, base_mask, early)

    (pair_own,) = call_kernel(
        late_kernel,
        [*got, kv_weights, early, cosine, sine],
        [((length // 2, 2 * HD), bf16)],
        [pltpu.VMEM((length // 2, 2 * HD), f32)],
    )
    x_own = joined(have, got)
    pair_other, x_own = together(swap(pair_own, CORE), x_own)
    pair = jnp.concatenate([pair_own, pair_other], axis=0)
    x_other = [swap(block, CORE) for block in x_own]
    outs = call_kernel(
        first_kernel,
        [query_0, pair, w_out],
        [((count // 2, width), bf16) for _, width, _ in PIECES for _ in range(2)],
        [pltpu.VMEM((count, columns), bf16)],
        12,
    )
    outs, x_other = together(outs, x_other)

    def queries_of(x):
        return sum(
            in_order(
                jnp.dot(block, w_query[first : first + width], preferred_element_type=jnp.float32), order, rows
            )
            for block, (first, width, order) in zip(x, PIECES)
        )

    bits = {NEAR: ((place >> 2) ^ (place >> 3)) % 2 == 1, FAR: (place >> 3) % 2 == 1, ZED: (place >> 1) % 2 == 1}
    sides = [bits[order[0]] for _, _, order in PIECES]
    came = [swap(outs[2 * i + 1], CORE) for i in range(3)]
    came, x_own = together(came, x_own)
    totals = [add(outs[2 * i], came[i]) for i in range(3)]
    keep, send = [], []
    for total, side in zip(totals, sides):
        middle = total.shape[1] // 2
        left, right = total[:, :middle], total[:, middle:]
        keep.append(jnp.where(side, right, left))
        send.append(jnp.where(side, left, right))
    got = [swap(block, order[0]) for block, (_, _, order) in zip(send, PIECES)]

    got, query_own, x_other = together(got, queries_of(x_own), x_other)
    totals = added(keep, got)
    got, query_other = together(step_up(totals, 1), queries_of(x_other))
    totals = added(totals, got)
    masked_1, is_list = flags[:, :1] > 0, flags[:, 1:2] > 0
    base_tokens = jnp.concatenate(
        [pair, turn_heads(jnp.concatenate([query_own, query_other], axis=0), cosine[:, :HALF], sine[:, HALF:])], axis=1
    )
    base = jnp.where(masked_1, base_mask, jnp.where(is_list, jnp.zeros_like(base_tokens), base_tokens))
    got, place, base = together(step_up(totals, 2), place, base)
    totals = added(totals, got)
    states = []
    for (first, width, _), total, side in zip(PIECES, totals, sides):
        row = mask_embed[None, first : first + width]
        middle = width // 2
        states.append(add(jnp.where(side, row[:, middle:], row[:, :middle]), total))
    kv_weights = head_weights(place, 60000000)
    got, kv_weights = together(step_up(states, 0), kv_weights)
    raw = []
    for state, block, side in zip(states, got, sides):
        raw.append(
            jnp.where(
                side, jnp.concatenate([block, state], axis=1), jnp.concatenate([state, block], axis=1)
            )
        )
    raw = [(block, swap(block, CORE)) for block in raw]

    operands = [half for both in raw for half in both]
    operands += [gain, list_cosine, list_sine, match, base, w_query, kv_weights, w_out]
    outs = call_kernel(
        second_kernel,
        operands,
        [((length // 2, width), bf16) for _, width, _ in PIECES for _ in range(2)],
        [
            pltpu.VMEM((count, CHUNKS[0][1]), bf16),
            pltpu.VMEM((count, columns + 2 * HD), bf16),
            pltpu.VMEM((length, columns + 2 * HD), bf16),
            pltpu.VMEM((length, columns), bf16),
        ],
        16,
    )
    keep, send = outs[::2], outs[1::2]
    totals = [
        add(one, swap(two, CORE)).reshape(2, 2, 2, rows, one.shape[1]) for one, two in zip(keep, send)
    ]
    keep, incoming = step_down(totals, 0)
    own_match = match[:rows]
    middle = count // 2
    states = jnp.concatenate(
        [pick(own_match[:, :middle], one) + pick(own_match[:, middle:], two) for one, two in raw], axis=1
    )
    hidden_1 = jnp.where(
        masked_1[:rows], mask_embed[None, :], jnp.where(is_list[:rows], states, tokens)
    )
    incoming, hidden_1 = together(incoming, hidden_1)
    keep, incoming = step_down(added(keep, incoming), 1)
    incoming = together(*incoming)
    keep, incoming = step_down(added(keep, incoming), 2)
    incoming = together(*incoming)
    summed_1 = jnp.concatenate(added(keep, incoming), axis=1)
    return (hidden_1.astype(jnp.float32) + summed_1.astype(jnp.float32)).astype(jnp.bfloat16)


def solution(mesh):
    placed = (
        P(("dp", "tensor"), None),
        P("dp", None),
        P(),
        P(),
        P(None, "tensor"),
        P(None, "tensor"),
        P(None, "tensor"),
        P("tensor", None),
    )
    return jax.shard_map(
        shards, mesh=mesh, in_specs=placed, out_specs=P(("dp", "tensor"), None), check_vma=False
    )
```

```python
import jax
import jax.numpy as jnp
from jax import lax
from jax.experimental import pallas as pl
from jax.experimental.pallas import tpu as pltpu
from jax.sharding import PartitionSpec as P

HD = 128
HALF = HD // 2
PARTS = 16
CORE, ZED, NEAR, FAR = 1, 2, 4, 12
LINKS = (NEAR, FAR, ZED)
PIECES = (
    (0, 2816, (NEAR, FAR, ZED)),
    (2816, 2816, (FAR, ZED, NEAR)),
    (5632, 2560, (ZED, NEAR, FAR)),
)
CHUNKS = [(first + i * width // 2, width // 2) for first, width, _ in PIECES for i in range(2)]
BLOCKS = [a ^ b ^ c for a in (0, NEAR) for b in (0, FAR) for c in (0, ZED)]


def swap(value, mask):
    return lax.ppermute(value, "tensor", [(i, i ^ mask) for i in range(PARTS)])


def normalize(rows, gain):
    values = rows.astype(jnp.float32)
    scale = lax.rsqrt(jnp.mean(values * values, axis=-1, keepdims=True) + 1e-05)
    return (values * scale * gain.astype(jnp.float32)).astype(jnp.bfloat16)


def turn_heads(values, cosine, sine):
    out = []
    for at in range(0, values.shape[1], HD):
        left, right = values[:, at : at + HALF], values[:, at + HALF : at + HD]
        out += [left * cosine - right * sine, right * cosine + left * sine]
    return jnp.concatenate(out, axis=1).astype(jnp.bfloat16)


def together(*values):
    return lax.optimization_barrier(values)


def keys_after(order, steps):
    keys = [0]
    for mask in order[:steps]:
        keys = keys + [key ^ mask for key in keys]
    return keys


def step_up(have, step):
    return [swap(block, order[step]) for block, (_, _, order) in zip(have, PIECES)]


def in_order(blocks, order, rows):
    keys = keys_after(order, 3)
    at = [keys.index(m) * rows for m in BLOCKS]
    return jnp.concatenate([blocks[i : i + rows] for i in at], axis=0)


def add(one, two):
    return (one.astype(jnp.float32) + two.astype(jnp.float32)).astype(jnp.bfloat16)


def step_down(totals, step):
    keep, got = [], []
    for total, (_, _, order) in zip(totals, PIECES):
        left = [mask for mask in LINKS if mask not in order[:step]]
        at = left.index(order[step])
        keep.append(lax.index_in_dim(total, 0, at, keepdims=False))
        got.append(swap(lax.index_in_dim(total, 1, at, keepdims=False), order[step]))
    return keep, got


def added(keep, got):
    return [add(one, two) for one, two in zip(keep, got)]


def with_heads(query, key, value, mixed):
    rows, columns = query.shape
    tile = rows // 2
    for h in range(columns // HD):
        for at in range(0, rows, tile):
            scores = lax.dot_general(
                query[at : at + tile, HD * h : HD * (h + 1)],
                key,
                (((1,), (1,)), ((), ())),
                preferred_element_type=jnp.float32,
            ) * HD ** (-0.5)
            weights = jnp.exp(scores - jnp.max(scores, axis=-1, keepdims=True))
            probs = weights * (1.0 / jnp.sum(weights, axis=-1, keepdims=True))
            mixed[at : at + tile, HD * h : HD * (h + 1)] = jnp.dot(
                probs.astype(jnp.bfloat16), value, preferred_element_type=jnp.float32
            ).astype(jnp.bfloat16)


def project_out(mixed, out_here, outs):
    half = mixed.shape[0] // 2
    for i, (first, width) in enumerate(CHUNKS):
        weights = out_here[:, first : first + width]
        at = (i % 2) * width
        for side in range(2):
            outs[2 * (i // 2) + side][:, at : at + width] = jnp.dot(
                mixed[half * side : half * (side + 1), :], weights, preferred_element_type=jnp.float32
            ).astype(jnp.bfloat16)


def first_kernel(query, pair_own, pair_other, out_here, *rest):
    outs, (mixed, pair) = rest[:6], rest[6:]
    half = pair_own.shape[0]
    pair[:half, :] = pair_own[...]
    pair[half:, :] = pair_other[...]
    with_heads(query, pair[:, :HD], pair[:, HD:], mixed)
    project_out(mixed, out_here, outs)


def turned(values, cosine, sine):
    return (values * cosine + pltpu.roll(values, HALF, 1) * sine).astype(jnp.bfloat16)


def second_kernel(*refs):
    raw, refs = refs[:6], refs[6:]
    gain, cosine, sine, match, base, query_here, kv_here, out_here = refs[:8]
    outs, refs = refs[8:14], refs[14:]
    normed, moving, placed, mixed = refs
    half = raw[0].shape[0]
    width_all = gain.shape[1]
    scales = []
    for side in range(2):
        squares = jnp.zeros((half, HD), jnp.float32)
        for piece in range(3):
            ref = raw[2 * piece + side]

            def add_squares(i, squares, ref=ref):
                values = ref[:, pl.ds(pl.multiple_of(i * HD, HD), HD)].astype(jnp.float32)
                return squares + values * values

            squares = lax.fori_loop(0, ref.shape[1] // HD, add_squares, squares, unroll=2)
        mean = jnp.sum(squares, axis=-1, keepdims=True) * (1.0 / width_all)
        scales.append(lax.rsqrt(mean + 1e-05))
    queries = jnp.zeros((2 * half, query_here.shape[1]), jnp.float32)
    pairs = jnp.zeros((2 * half, kv_here.shape[0]), jnp.float32)
    for i, (first, width) in enumerate(CHUNKS):
        at = (i % 2) * width
        for side in range(2):
            values = raw[2 * (i // 2) + side][:, at : at + width].astype(jnp.float32)
            normed[half * side : half * (side + 1), :width] = (
                values * scales[side] * gain[:, first : first + width]
            ).astype(jnp.bfloat16)
        some = normed[:, :width]
        queries += jnp.dot(some, query_here[first : first + width, :], preferred_element_type=jnp.float32)
        pairs += dot_rows(some, kv_here[:, first : first + width])
    moving[:, :HD] = turned(pairs[:, :HD], cosine[...], sine[...])
    moving[:, HD : 2 * HD] = pairs[:, HD:].astype(jnp.bfloat16)
    for h in range(queries.shape[1] // HD):
        moving[:, HD * (h + 2) : HD * (h + 3)] = turned(queries[:, HD * h : HD * (h + 1)], cosine[...], sine[...])
    placed[...] = base[...] + jnp.dot(
        match[...], moving[...], preferred_element_type=jnp.float32
    ).astype(jnp.bfloat16)
    with_heads(placed.at[:, 2 * HD :], placed[:, :HD], placed[:, HD : 2 * HD], mixed)
    project_out(mixed, out_here, outs)


def dot_rows(x, weights):
    return lax.dot_general(x, weights, (((1,), (1,)), ((), ())), preferred_element_type=jnp.float32)


def query_kernel(one, two, three, weights, out, total):
    rows = out.shape[0] // 8
    for i, (piece, (first, width, order)) in enumerate(zip((one, two, three), PIECES)):
        total[...] = jnp.dot(piece[...], weights[first : first + width, :], preferred_element_type=jnp.float32)
        for j, key in enumerate(keys_after(order, 3)):
            at = BLOCKS.index(key) * rows
            some = total[j * rows : (j + 1) * rows, :]
            if i == 0:
                out[at : at + rows, :] = some
            else:
                out[at : at + rows, :] += some


def dot_rows(x, weights):
    return lax.dot_general(x, weights, (((1,), (1,)), ((), ())), preferred_element_type=jnp.float32)


def base_kernel(pair_own, pair_other, query_own, query_other, cosine, sine, masked, flags, base):
    half = pair_own.shape[0]
    for core, (pair, query) in enumerate(((pair_own, query_own), (pair_other, query_other))):
        some = slice(half * core, half * (core + 1))
        is_masked, is_list = flags[some, :1] > 0, flags[some, 1:2] > 0
        for at in range(0, base.shape[1], HD):
            if at < 2 * HD:
                values = pair[:, at : at + HD]
            else:
                values = turned(query[:, at - 2 * HD : at - HD], cosine[some, :], sine[some, :])
            values = jnp.where(is_list, 0.0, values.astype(jnp.float32))
            mask_values = masked[some, at : at + HD].astype(jnp.float32)
            base[some, at : at + HD] = jnp.where(is_masked, mask_values, values).astype(jnp.bfloat16)


def call_kernel(kernel, operands, outs, scratch=(), mib=16, last=(), moved=100000):
    places = [pltpu.VMEM] * (len(operands) - len(last)) + list(last)
    return pl.pallas_call(
        kernel,
        out_shape=[jax.ShapeDtypeStruct(*out) for out in outs],
        in_specs=[pl.BlockSpec(memory_space=place) for place in places],
        out_specs=[pl.BlockSpec(memory_space=pltpu.VMEM)] * len(outs),
        scratch_shapes=list(scratch),
        compiler_params=pltpu.CompilerParams(vmem_limit_bytes=mib * 2**20),
        cost_estimate=pl.CostEstimate(flops=1000000, bytes_accessed=moved, transcendentals=0),
    )(*operands)


def join_kernel(*refs):
    for i in range(3):
        have, got, out = refs[i], refs[3 + i], refs[6 + i]
        rows = have.shape[0]
        out[:rows, :] = have[...]
        out[rows:, :] = got[...]


def joined(have, got):
    outs = [((2 * block.shape[0], block.shape[1]), block.dtype) for block in have]
    return call_kernel(join_kernel, [*have, *got], outs, mib=12)


def weight_rows_kernel(key, value, other_key, other_value, place, out):
    even = place[0, 0] % 2 == 0

    @pl.when(even)
    def _():
        out[:HALF, :] = key[...]
        out[HALF : 2 * HALF, :] = other_key[...]
        out[2 * HALF : 3 * HALF, :] = value[...]
        out[3 * HALF :, :] = other_value[...]

    @pl.when(jnp.logical_not(even))
    def _():
        out[:HALF, :] = other_key[...]
        out[HALF : 2 * HALF, :] = key[...]
        out[2 * HALF : 3 * HALF, :] = other_value[...]
        out[3 * HALF :, :] = value[...]


def table_kernel(positions, freq, place, cosine, sine, list_cosine, list_sine, match, flags):
    f32, bf16 = jnp.float32, jnp.bfloat16
    count, length = match.shape[1], match.shape[0]
    rows = length // PARTS
    at = lax.broadcasted_iota(jnp.int32, (length, 1), 0)
    block = at // rows
    offset = (block // 8) * CORE ^ (block // 4 % 2) * NEAR ^ (block // 2 % 2) * FAR ^ (block % 2) * ZED
    spots = (place[0, 0] ^ offset) * rows + at % rows
    listed = (lax.broadcasted_iota(jnp.int32, (count, 1), 0) + place[0, 0] % 2 * (count // 2)) % count
    ones_across, twos_across = positions[:1, :], positions[1:, :]
    row = lax.broadcasted_iota(jnp.int32, (count, count), 0)
    column = lax.broadcasted_iota(jnp.int32, (count, count), 1)
    twos = jnp.sum(jnp.where(row == column, twos_across, 0), axis=1, keepdims=True)
    stale = jnp.max(jnp.where(twos == ones_across, 1.0, 0.0), axis=0, keepdims=True)
    fresh = 1.0 - stale
    before = jnp.where(row < column, 1.0, 0.0).astype(bf16)

    def ahead(flag):
        wide = jnp.broadcast_to(flag, (16, count)).astype(bf16)
        return jnp.dot(wide, before, preferred_element_type=f32)[:1]

    rank = jnp.where(fresh > 0, ahead(fresh), jnp.sum(fresh, axis=1, keepdims=True) + ahead(stale))
    spot = jnp.where(listed.astype(f32) == rank, 1.0, 0.0)
    list_spots = jnp.sum(spot * ones_across.astype(f32), axis=1, keepdims=True)
    here = jnp.where((spots == ones_across) & (fresh > 0), 1.0, 0.0)
    match[...] = dot_rows(here.astype(bf16), spot.astype(bf16)).astype(bf16)
    is_list = jnp.max(here, axis=1, keepdims=True)
    masked_1 = jnp.max(jnp.where(spots == twos_across, 1.0, 0.0), axis=1, keepdims=True)
    lane = lax.broadcasted_iota(jnp.int32, (spots.shape[0], HD), 1)
    flags[...] = jnp.where(lane == 0, masked_1, is_list)
    sign = jnp.where(lax.broadcasted_iota(jnp.int32, (1, HD), 1) < HALF, -1.0, 1.0)
    angle = spots.astype(f32) * freq[...]
    cosine[...] = jnp.cos(angle)
    sine[...] = jnp.sin(angle) * sign
    angle = list_spots * freq[...]
    list_cosine[...] = jnp.cos(angle)
    list_sine[...] = jnp.sin(angle) * sign


def mask_kernel(embed, gain, query_here, kv_here, cosine, sine, list_cosine, list_sine, query, base):
    values = embed[...].astype(jnp.float32)
    mean = jnp.sum(values * values, axis=-1, keepdims=True) * (1.0 / embed.shape[1])
    row = (values * lax.rsqrt(mean + 1e-05) * gain[...]).astype(jnp.bfloat16)
    row = jnp.broadcast_to(row, (16, row.shape[1]))
    queries = jnp.dot(row, query_here[...], preferred_element_type=jnp.float32)[:1]
    pairs = dot_rows(row, kv_here[...])[:1]
    length = base.shape[0]
    base[:, :HD] = turned(jnp.broadcast_to(pairs[:, :HD], (length, HD)), cosine[...], sine[...])
    base[:, HD : 2 * HD] = jnp.broadcast_to(pairs[:, HD:], (length, HD)).astype(jnp.bfloat16)
    for at in range(0, queries.shape[1], HD):
        some = queries[:, at : at + HD]
        base[:, 2 * HD + at : 3 * HD + at] = turned(jnp.broadcast_to(some, (length, HD)), cosine[...], sine[...])
        query[:, at : at + HD] = turned(
            jnp.broadcast_to(some, (query.shape[0], HD)), list_cosine[...], list_sine[...]
        )


def add_pairs(pieces, kv_here, total, low, fresh):
    rows = total.shape[0] // 8
    for piece, (first, width, order) in zip(pieces, PIECES):
        product = dot_rows(piece[...], kv_here[:, first : first + width])
        for i, key in enumerate(keys_after(order, 3)[low : low + 4]):
            at = BLOCKS.index(key) * rows
            some = product[i * rows : (i + 1) * rows]
            if key in fresh:
                fresh.remove(key)
                total[at : at + rows, :] = some
            else:
                total[at : at + rows, :] += some


def early_kernel(one, two, three, kv_here, total):
    fresh = set(BLOCKS)
    add_pairs((one, two, three), kv_here, total, 0, fresh)
    rows = total.shape[0] // 8
    for key in fresh:
        at = BLOCKS.index(key) * rows
        total[at : at + rows, :] = jnp.zeros((rows, total.shape[1]), jnp.float32)


def late_kernel(one, two, three, kv_here, early, cosine, sine, out, total):
    total[...] = early[...]
    add_pairs((one, two, three), kv_here, total, 4, set())
    rows = total.shape[0]
    out[:, :HD] = turned(total[:, :HD], cosine[:rows, :], sine[:rows, :])
    out[:, HD:] = total[:, HD:].astype(jnp.bfloat16)


def chosen(spots, positions):
    return jnp.any(spots[:, None] == positions[None, :], axis=1)


def pick(one_hot, rows):
    return jnp.dot(
        one_hot.astype(jnp.bfloat16), rows, preferred_element_type=jnp.float32
    ).astype(jnp.bfloat16)


def shards(tokens, positions, mask_embed, norm_gain, w_query, w_key, w_value, w_out):
    place = lax.axis_index("tensor")
    rows = tokens.shape[0]
    length = rows * PARTS

    own_spots = place * rows + jnp.arange(rows, dtype=jnp.int32)
    own_masked_0 = chosen(own_spots, positions[0])
    hidden_0 = jnp.where(own_masked_0[:, None], mask_embed[None, :], tokens)
    normed_0 = normalize(hidden_0, norm_gain)
    key_rows, value_rows = w_key.T, w_value.T
    bits = {NEAR: (place >> 2 ^ place >> 3) & 1 == 1, FAR: place >> 3 & 1 == 1, ZED: place >> 1 & 1 == 1}
    sides = [bits[order[0]] for _, _, order in PIECES]
    normed_0, positions, place, sides, key_rows, value_rows = together(
        normed_0, positions, place, sides, key_rows, value_rows
    )
    have = [normed_0[:, first : first + width] for first, width, _ in PIECES]

    f32, bf16 = jnp.float32, jnp.bfloat16
    count, columns = positions.shape[1], w_query.shape[1]
    freq = 500000.0 ** (-(jnp.arange(HD, dtype=f32) % HALF * 2.0 / HD))
    cosine, sine, list_cosine, list_sine, match, flags = call_kernel(
        table_kernel,
        [positions, freq[None], place.reshape(1, 1)],
        [((length, HD), f32)] * 2 + [((count, HD), f32)] * 2 + [((length, count), bf16), ((length, HD), f32)],
        last=[pltpu.SMEM],
    )
    other_rows = swap(key_rows, CORE), swap(value_rows, CORE)
    tables = (cosine, sine, list_cosine, list_sine, match, flags)
    got, tables, other_rows, place = together(step_up(have, 0), tables, other_rows, place)
    cosine, sine, list_cosine, list_sine, match, flags = tables
    have = joined(have, got)

    def head_weights(place, moved):
        (weights,) = call_kernel(
            weight_rows_kernel,
            [key_rows, value_rows, *other_rows, place.reshape(1, 1)],
            [((4 * HALF, key_rows.shape[1]), bf16)],
            last=[pltpu.SMEM],
            moved=moved,
        )
        return weights

    kv_weights = head_weights(place, 100000)
    got, kv_weights, mask_embed, norm_gain = together(step_up(have, 1), kv_weights, mask_embed, norm_gain)
    have = joined(have, got)

    gain = norm_gain[None, :].astype(f32)
    query_0, base_mask = call_kernel(
        mask_kernel,
        [mask_embed[None, :], gain, w_query, kv_weights, cosine, sine, list_cosine, list_sine],
        [((count, columns), bf16), ((length, columns + 2 * HD), bf16)],
    )
    (early,) = call_kernel(early_kernel, [*have, kv_weights], [((length // 2, 2 * HD), f32)])
    got, query_0, base_mask, early = together(step_up(have, 2), query_0, base_mask, early)

    (pair_own,) = call_kernel(
        late_kernel,
        [*got, kv_weights, early, cosine, sine],
        [((length // 2, 2 * HD), bf16)],
        [pltpu.VMEM((length // 2, 2 * HD), f32)],
    )
    x_own = joined(have, got)
    pair_other, x_own = together(swap(pair_own, CORE), x_own)
    x_other = [swap(block, CORE) for block in x_own]
    outs = call_kernel(
        first_kernel,
        [query_0, pair_own, pair_other, w_out],
        [((count // 2, width), bf16) for _, width, _ in PIECES for _ in range(2)],
        [pltpu.VMEM((count, columns), bf16), pltpu.VMEM((length, 2 * HD), bf16)],
        12,
    )
    outs, x_other = together(outs, x_other)

    def queries_of(x):
        (queries,) = call_kernel(
            query_kernel,
            [*x, w_query],
            [((length // 2, columns), f32)],
            [pltpu.VMEM((length // 2, columns), f32)],
        )
        return queries

    came = [swap(outs[2 * i + 1], CORE) for i in range(3)]
    came, x_own = together(came, x_own)
    totals = [add(outs[2 * i], came[i]) for i in range(3)]
    keep, send = [], []
    for total, side in zip(totals, sides):
        middle = total.shape[1] // 2
        left, right = total[:, :middle], total[:, middle:]
        keep.append(jnp.where(side, right, left))
        send.append(jnp.where(side, left, right))
    got = [swap(block, order[0]) for block, (_, _, order) in zip(send, PIECES)]

    got, query_own, x_other = together(got, queries_of(x_own), x_other)
    totals = added(keep, got)
    got, query_other = together(step_up(totals, 1), queries_of(x_other))
    totals = added(totals, got)
    masked_1, is_list = flags[:, :1] > 0, flags[:, 1:2] > 0
    (base,) = call_kernel(
        base_kernel,
        [pair_own, pair_other, query_own, query_other, cosine, sine, base_mask, flags],
        [((length, columns + 2 * HD), bf16)],
    )
    got, place, base = together(step_up(totals, 2), place, base)
    totals = added(totals, got)
    states = []
    for (first, width, _), total, side in zip(PIECES, totals, sides):
        row = mask_embed[None, first : first + width]
        middle = width // 2
        states.append(add(jnp.where(side, row[:, middle:], row[:, :middle]), total))
    kv_weights = head_weights(place, 60000000)
    got, kv_weights = together(step_up(states, 0), kv_weights)
    raw = []
    for state, block, side in zip(states, got, sides):
        raw.append(
            jnp.where(
                side, jnp.concatenate([block, state], axis=1), jnp.concatenate([state, block], axis=1)
            )
        )
    raw = [(block, swap(block, CORE)) for block in raw]

    operands = [half for both in raw for half in both]
    operands += [gain, list_cosine, list_sine, match, base, w_query, kv_weights, w_out]
    outs = call_kernel(
        second_kernel,
        operands,
        [((length // 2, width), bf16) for _, width, _ in PIECES for _ in range(2)],
        [
            pltpu.VMEM((count, CHUNKS[0][1]), bf16),
            pltpu.VMEM((count, columns + 2 * HD), bf16),
            pltpu.VMEM((length, columns + 2 * HD), bf16),
            pltpu.VMEM((length, columns), bf16),
        ],
        16,
    )
    keep, send = outs[::2], outs[1::2]
    totals = [
        add(one, swap(two, CORE)).reshape(2, 2, 2, rows, one.shape[1]) for one, two in zip(keep, send)
    ]
    keep, incoming = step_down(totals, 0)
    own_match = match[:rows]
    middle = count // 2
    states = jnp.concatenate(
        [pick(own_match[:, :middle], one) + pick(own_match[:, middle:], two) for one, two in raw], axis=1
    )
    hidden_1 = jnp.where(
        masked_1[:rows], mask_embed[None, :], jnp.where(is_list[:rows], states, tokens)
    )
    incoming, hidden_1 = together(incoming, hidden_1)
    keep, incoming = step_down(added(keep, incoming), 1)
    incoming = together(*incoming)
    keep, incoming = step_down(added(keep, incoming), 2)
    incoming = together(*incoming)
    summed_1 = jnp.concatenate(added(keep, incoming), axis=1)
    return (hidden_1.astype(jnp.float32) + summed_1.astype(jnp.float32)).astype(jnp.bfloat16)


def solution(mesh):
    placed = (
        P(("dp", "tensor"), None),
        P("dp", None),
        P(),
        P(),
        P(None, "tensor"),
        P(None, "tensor"),
        P(None, "tensor"),
        P("tensor", None),
    )
    return jax.shard_map(
        shards, mesh=mesh, in_specs=placed, out_specs=P(("dp", "tensor"), None), check_vma=False
    )
```

```python
import functools

import jax
import jax.numpy as jnp
from jax import lax
from jax.experimental import pallas as pl
from jax.experimental.pallas import tpu as pltpu
from jax.sharding import PartitionSpec as P

HD = 128
HALF = HD // 2
PARTS = 16
CORE, ZED, NEAR, FAR = 1, 2, 4, 12
LINKS = (NEAR, FAR, ZED)
PIECES = (
    (0, 2816, (NEAR, FAR, ZED)),
    (2816, 2816, (FAR, ZED, NEAR)),
    (5632, 2560, (ZED, NEAR, FAR)),
)
CHUNKS = [(first + i * width // 2, width // 2) for first, width, _ in PIECES for i in range(2)]
FEW = 160
BLOCKS = [a ^ b ^ c for a in (0, NEAR) for b in (0, FAR) for c in (0, ZED)]


def swap(value, mask):
    return lax.ppermute(value, "tensor", [(i, i ^ mask) for i in range(PARTS)])


def normalize(rows, gain):
    values = rows.astype(jnp.float32)
    scale = lax.rsqrt(jnp.mean(values * values, axis=-1, keepdims=True) + 1e-05)
    return (values * scale * gain.astype(jnp.float32)).astype(jnp.bfloat16)


def turn_heads(values, cosine, sine):
    out = []
    for at in range(0, values.shape[1], HD):
        left, right = values[:, at : at + HALF], values[:, at + HALF : at + HD]
        out += [left * cosine - right * sine, right * cosine + left * sine]
    return jnp.concatenate(out, axis=1).astype(jnp.bfloat16)


def together(*values):
    return lax.optimization_barrier(values)


def keys_after(order, steps):
    keys = [0]
    for mask in order[:steps]:
        keys = keys + [key ^ mask for key in keys]
    return keys


def step_up(have, step):
    return [swap(block, order[step]) for block, (_, _, order) in zip(have, PIECES)]


def in_order(blocks, order, rows):
    keys = keys_after(order, 3)
    at = [keys.index(m) * rows for m in BLOCKS]
    return jnp.concatenate([blocks[i : i + rows] for i in at], axis=0)


def add(one, two):
    return (one.astype(jnp.float32) + two.astype(jnp.float32)).astype(jnp.bfloat16)


def step_down(totals, step):
    keep, got = [], []
    for total, (_, _, order) in zip(totals, PIECES):
        left = [mask for mask in LINKS if mask not in order[:step]]
        at = left.index(order[step])
        keep.append(lax.index_in_dim(total, 0, at, keepdims=False))
        got.append(swap(lax.index_in_dim(total, 1, at, keepdims=False), order[step]))
    return keep, got


def added(keep, got):
    return [add(one, two) for one, two in zip(keep, got)]


def with_heads(query, key, value, mixed):
    rows, columns = query.shape
    tile = rows // 2
    for h in range(columns // HD):
        for at in range(0, rows, tile):
            scores = lax.dot_general(
                query[at : at + tile, HD * h : HD * (h + 1)],
                key,
                (((1,), (1,)), ((), ())),
                preferred_element_type=jnp.float32,
            ) * HD ** (-0.5)
            weights = jnp.exp(scores - jnp.max(scores, axis=-1, keepdims=True))
            probs = weights * (1.0 / jnp.sum(weights, axis=-1, keepdims=True))
            mixed[at : at + tile, HD * h : HD * (h + 1)] = jnp.dot(
                probs.astype(jnp.bfloat16), value, preferred_element_type=jnp.float32
            ).astype(jnp.bfloat16)


def project_out(mixed, out_here, outs):
    half = mixed.shape[0] // 2
    for i, (first, width) in enumerate(CHUNKS):
        weights = out_here[:, first : first + width]
        at = (i % 2) * width
        for side in range(2):
            outs[2 * (i // 2) + side][:, at : at + width] = jnp.dot(
                mixed[half * side : half * (side + 1), :], weights, preferred_element_type=jnp.float32
            ).astype(jnp.bfloat16)


def first_kernel(query, pair_own, pair_other, out_here, *rest):
    outs, (mixed, pair) = rest[:6], rest[6:]
    half = pair_own.shape[0]
    pair[:half, :] = pair_own[...]
    pair[half:, :] = pair_other[...]
    with_heads(query, pair[:, :HD], pair[:, HD:], mixed)
    project_out(mixed, out_here, outs)


def turned(values, cosine, sine):
    return (values * cosine + pltpu.roll(values, HALF, 1) * sine).astype(jnp.bfloat16)


def second_kernel(*refs):
    raw, refs = refs[:6], refs[6:]
    gain, cosine, sine, match, base, query_here, kv_here, out_here = refs[:8]
    outs, refs = refs[8:14], refs[14:]
    normed, moving, placed, mixed = refs
    half = raw[0].shape[0]
    width_all = gain.shape[1]
    scales = []
    for side in range(2):
        squares = jnp.zeros((half, HD), jnp.float32)
        for piece in range(3):
            ref = raw[2 * piece + side]

            def add_squares(i, squares, ref=ref):
                values = ref[:, pl.ds(pl.multiple_of(i * HD, HD), HD)].astype(jnp.float32)
                return squares + values * values

            squares = lax.fori_loop(0, ref.shape[1] // HD, add_squares, squares, unroll=2)
        mean = jnp.sum(squares, axis=-1, keepdims=True) * (1.0 / width_all)
        scales.append(lax.rsqrt(mean + 1e-05))
    queries = jnp.zeros((2 * half, query_here.shape[1]), jnp.float32)
    pairs = jnp.zeros((2 * half, kv_here.shape[0]), jnp.float32)
    for i, (first, width) in enumerate(CHUNKS):
        at = (i % 2) * width
        for side in range(2):
            values = raw[2 * (i // 2) + side][:, at : at + width].astype(jnp.float32)
            normed[half * side : half * (side + 1), :width] = (
                values * scales[side] * gain[:, first : first + width]
            ).astype(jnp.bfloat16)
        some = normed[:, :width]
        queries += jnp.dot(some, query_here[first : first + width, :], preferred_element_type=jnp.float32)
        pairs += dot_rows(some, kv_here[:, first : first + width])
    moving[:, :HD] = turned(pairs[:, :HD], cosine[...], sine[...])
    moving[:, HD : 2 * HD] = pairs[:, HD:].astype(jnp.bfloat16)
    for h in range(queries.shape[1] // HD):
        moving[:, HD * (h + 2) : HD * (h + 3)] = turned(queries[:, HD * h : HD * (h + 1)], cosine[...], sine[...])
    placed[...] = base[...] + jnp.dot(
        match[...], moving[...], preferred_element_type=jnp.float32
    ).astype(jnp.bfloat16)
    with_heads(placed.at[:, 2 * HD :], placed[:, :HD], placed[:, HD : 2 * HD], mixed)
    project_out(mixed, out_here, outs)


def dot_rows(x, weights):
    return lax.dot_general(x, weights, (((1,), (1,)), ((), ())), preferred_element_type=jnp.float32)


def query_kernel(one, two, three, weights, out, total):
    rows = out.shape[0] // 8
    for i, (piece, (first, width, order)) in enumerate(zip((one, two, three), PIECES)):
        total[...] = jnp.dot(piece[...], weights[first : first + width, :], preferred_element_type=jnp.float32)
        for j, key in enumerate(keys_after(order, 3)):
            at = BLOCKS.index(key) * rows
            some = total[j * rows : (j + 1) * rows, :]
            if i == 0:
                out[at : at + rows, :] = some
            else:
                out[at : at + rows, :] += some


def dot_rows(x, weights):
    return lax.dot_general(x, weights, (((1,), (1,)), ((), ())), preferred_element_type=jnp.float32)


def base_kernel(pair_own, pair_other, query_own, query_other, cosine, sine, masked, flags, base):
    half = pair_own.shape[0]
    for core, (pair, query) in enumerate(((pair_own, query_own), (pair_other, query_other))):
        some = slice(half * core, half * (core + 1))
        is_masked, is_list = flags[some, :1] > 0, flags[some, 1:2] > 0
        for at in range(0, base.shape[1], HD):
            if at < 2 * HD:
                values = pair[:, at : at + HD]
            else:
                values = turned(query[:, at - 2 * HD : at - HD], cosine[some, :], sine[some, :])
            values = jnp.where(is_list, 0.0, values.astype(jnp.float32))
            mask_values = masked[some, at : at + HD].astype(jnp.float32)
            base[some, at : at + HD] = jnp.where(is_masked, mask_values, values).astype(jnp.bfloat16)


def call_kernel(kernel, operands, outs, scratch=(), mib=16, last=(), moved=100000, least=0):
    places = [pltpu.VMEM] * (len(operands) - len(last)) + list(last)
    return pl.pallas_call(
        kernel,
        out_shape=[jax.ShapeDtypeStruct(*out) for out in outs],
        in_specs=[pl.BlockSpec(memory_space=place) for place in places],
        out_specs=[pl.BlockSpec(memory_space=pltpu.VMEM)] * len(outs),
        scratch_shapes=list(scratch),
        compiler_params=pltpu.CompilerParams(vmem_limit_bytes=max(mib, least) * 2**20),
        cost_estimate=pl.CostEstimate(flops=1000000, bytes_accessed=moved, transcendentals=0),
    )(*operands)


def join_kernel(*refs):
    for i in range(3):
        have, got, out = refs[i], refs[3 + i], refs[6 + i]
        rows = have.shape[0]
        out[:rows, :] = have[...]
        out[rows:, :] = got[...]


def joined(have, got):
    outs = [((2 * block.shape[0], block.shape[1]), block.dtype) for block in have]
    return call_kernel(join_kernel, [*have, *got], outs, mib=12)


def weight_rows_kernel(key, value, other_key, other_value, place, out):
    even = place[0, 0] % 2 == 0

    @pl.when(even)
    def _():
        out[:HALF, :] = key[...]
        out[HALF : 2 * HALF, :] = other_key[...]
        out[2 * HALF : 3 * HALF, :] = value[...]
        out[3 * HALF :, :] = other_value[...]

    @pl.when(jnp.logical_not(even))
    def _():
        out[:HALF, :] = other_key[...]
        out[HALF : 2 * HALF, :] = key[...]
        out[2 * HALF : 3 * HALF, :] = other_value[...]
        out[3 * HALF :, :] = value[...]


def table_kernel(positions, freq, place, cosine, sine, list_cosine, list_sine, match, flags, needed):
    f32, bf16 = jnp.float32, jnp.bfloat16
    count, length, chosen = match.shape[1], match.shape[0], positions.shape[1]
    rows = length // PARTS
    at = lax.broadcasted_iota(jnp.int32, (length, 1), 0)
    block = at // rows
    offset = (block // 8) * CORE ^ (block // 4 % 2) * NEAR ^ (block // 2 % 2) * FAR ^ (block % 2) * ZED
    spots = (place[0, 0] ^ offset) * rows + at % rows
    listed = (lax.broadcasted_iota(jnp.int32, (count, 1), 0) + place[0, 0] % 2 * (count // 2)) % count
    ones_across, twos_across = positions[:1, :], positions[1:, :]
    row = lax.broadcasted_iota(jnp.int32, (chosen, chosen), 0)
    column = lax.broadcasted_iota(jnp.int32, (chosen, chosen), 1)
    twos = jnp.sum(jnp.where(row == column, twos_across, 0), axis=1, keepdims=True)
    stale = jnp.max(jnp.where(twos == ones_across, 1.0, 0.0), axis=0, keepdims=True)
    fresh = 1.0 - stale
    before = jnp.where(row < column, 1.0, 0.0).astype(bf16)

    def ahead(flag):
        wide = jnp.broadcast_to(flag, (16, chosen)).astype(bf16)
        return jnp.dot(wide, before, preferred_element_type=f32)[:1]

    fresh_count = jnp.sum(fresh, axis=1, keepdims=True)
    rank = jnp.where(fresh > 0, ahead(fresh), fresh_count + ahead(stale))
    needed[...] = jnp.broadcast_to(fresh_count, needed.shape)
    spot = jnp.where(listed.astype(f32) == rank, 1.0, 0.0)
    list_spots = jnp.sum(spot * ones_across.astype(f32), axis=1, keepdims=True)
    here = jnp.where((spots == ones_across) & (fresh > 0), 1.0, 0.0)
    match[...] = dot_rows(here.astype(bf16), spot.astype(bf16)).astype(bf16)
    is_list = jnp.max(here, axis=1, keepdims=True)
    masked_1 = jnp.max(jnp.where(spots == twos_across, 1.0, 0.0), axis=1, keepdims=True)
    lane = lax.broadcasted_iota(jnp.int32, (spots.shape[0], HD), 1)
    flags[...] = jnp.where(lane == 0, masked_1, is_list)
    sign = jnp.where(lax.broadcasted_iota(jnp.int32, (1, HD), 1) < HALF, -1.0, 1.0)
    angle = spots.astype(f32) * freq[...]
    cosine[...] = jnp.cos(angle)
    sine[...] = jnp.sin(angle) * sign
    angle = list_spots * freq[...]
    list_cosine[...] = jnp.cos(angle)
    list_sine[...] = jnp.sin(angle) * sign


def mask_kernel(embed, gain, query_here, kv_here, cosine, sine, list_cosine, list_sine, query, base):
    values = embed[...].astype(jnp.float32)
    mean = jnp.sum(values * values, axis=-1, keepdims=True) * (1.0 / embed.shape[1])
    row = (values * lax.rsqrt(mean + 1e-05) * gain[...]).astype(jnp.bfloat16)
    row = jnp.broadcast_to(row, (16, row.shape[1]))
    queries = jnp.dot(row, query_here[...], preferred_element_type=jnp.float32)[:1]
    pairs = dot_rows(row, kv_here[...])[:1]
    length = base.shape[0]
    base[:, :HD] = turned(jnp.broadcast_to(pairs[:, :HD], (length, HD)), cosine[...], sine[...])
    base[:, HD : 2 * HD] = jnp.broadcast_to(pairs[:, HD:], (length, HD)).astype(jnp.bfloat16)
    for at in range(0, queries.shape[1], HD):
        some = queries[:, at : at + HD]
        base[:, 2 * HD + at : 3 * HD + at] = turned(jnp.broadcast_to(some, (length, HD)), cosine[...], sine[...])
        query[:, at : at + HD] = turned(
            jnp.broadcast_to(some, (query.shape[0], HD)), list_cosine[...], list_sine[...]
        )


def add_pairs(pieces, kv_here, total, low, fresh):
    rows = total.shape[0] // 8
    for piece, (first, width, order) in zip(pieces, PIECES):
        product = dot_rows(piece[...], kv_here[:, first : first + width])
        for i, key in enumerate(keys_after(order, 3)[low : low + 4]):
            at = BLOCKS.index(key) * rows
            some = product[i * rows : (i + 1) * rows]
            if key in fresh:
                fresh.remove(key)
                total[at : at + rows, :] = some
            else:
                total[at : at + rows, :] += some


def early_kernel(one, two, three, kv_here, total):
    fresh = set(BLOCKS)
    add_pairs((one, two, three), kv_here, total, 0, fresh)
    rows = total.shape[0] // 8
    for key in fresh:
        at = BLOCKS.index(key) * rows
        total[at : at + rows, :] = jnp.zeros((rows, total.shape[1]), jnp.float32)


def late_kernel(one, two, three, kv_here, early, cosine, sine, out, total):
    total[...] = early[...]
    add_pairs((one, two, three), kv_here, total, 4, set())
    rows = total.shape[0]
    out[:, :HD] = turned(total[:, :HD], cosine[:rows, :], sine[:rows, :])
    out[:, HD:] = total[:, HD:].astype(jnp.bfloat16)


def chosen(spots, positions):
    return jnp.any(spots[:, None] == positions[None, :], axis=1)


def pick(one_hot, rows):
    return jnp.dot(
        one_hot.astype(jnp.bfloat16), rows, preferred_element_type=jnp.float32
    ).astype(jnp.bfloat16)


def steps(count, tokens, positions, mask_embed, norm_gain, w_query, w_key, w_value, w_out):
    place = lax.axis_index("tensor")
    run_kernel = functools.partial(call_kernel, least=0 if count <= FEW else 52)
    rows = tokens.shape[0]
    length = rows * PARTS

    own_spots = place * rows + jnp.arange(rows, dtype=jnp.int32)
    own_masked_0 = chosen(own_spots, positions[0])
    hidden_0 = jnp.where(own_masked_0[:, None], mask_embed[None, :], tokens)
    normed_0 = normalize(hidden_0, norm_gain)
    key_rows, value_rows = w_key.T, w_value.T
    bits = {NEAR: (place >> 2 ^ place >> 3) & 1 == 1, FAR: place >> 3 & 1 == 1, ZED: place >> 1 & 1 == 1}
    sides = [bits[order[0]] for _, _, order in PIECES]
    normed_0, positions, place, sides, key_rows, value_rows = together(
        normed_0, positions, place, sides, key_rows, value_rows
    )
    have = [normed_0[:, first : first + width] for first, width, _ in PIECES]

    f32, bf16 = jnp.float32, jnp.bfloat16
    columns = w_query.shape[1]
    freq = 500000.0 ** (-(jnp.arange(HD, dtype=f32) % HALF * 2.0 / HD))
    cosine, sine, list_cosine, list_sine, match, flags, needed = run_kernel(
        table_kernel,
        [positions, freq[None], place.reshape(1, 1)],
        [((length, HD), f32)] * 2 + [((count, HD), f32)] * 2 + [((length, count), bf16), ((length, HD), f32), ((8, HD), f32)],
        last=[pltpu.SMEM],
    )
    other_rows = swap(key_rows, CORE), swap(value_rows, CORE)
    tables = (cosine, sine, list_cosine, list_sine, match, flags)
    got, tables, other_rows, place = together(step_up(have, 0), tables, other_rows, place)
    cosine, sine, list_cosine, list_sine, match, flags = tables
    have = joined(have, got)

    def head_weights(place, moved):
        (weights,) = run_kernel(
            weight_rows_kernel,
            [key_rows, value_rows, *other_rows, place.reshape(1, 1)],
            [((4 * HALF, key_rows.shape[1]), bf16)],
            last=[pltpu.SMEM],
            moved=moved,
        )
        return weights

    kv_weights = head_weights(place, 100000)
    got, kv_weights, mask_embed, norm_gain = together(step_up(have, 1), kv_weights, mask_embed, norm_gain)
    have = joined(have, got)

    gain = norm_gain[None, :].astype(f32)
    query_0, base_mask = run_kernel(
        mask_kernel,
        [mask_embed[None, :], gain, w_query, kv_weights, cosine, sine, list_cosine, list_sine],
        [((count, columns), bf16), ((length, columns + 2 * HD), bf16)],
    )
    (early,) = run_kernel(early_kernel, [*have, kv_weights], [((length // 2, 2 * HD), f32)])
    got, query_0, base_mask, early = together(step_up(have, 2), query_0, base_mask, early)

    (pair_own,) = run_kernel(
        late_kernel,
        [*got, kv_weights, early, cosine, sine],
        [((length // 2, 2 * HD), bf16)],
        [pltpu.VMEM((length // 2, 2 * HD), f32)],
    )
    x_own = joined(have, got)
    pair_other, x_own = together(swap(pair_own, CORE), x_own)
    x_other = [swap(block, CORE) for block in x_own]
    outs = run_kernel(
        first_kernel,
        [query_0, pair_own, pair_other, w_out],
        [((count // 2, width), bf16) for _, width, _ in PIECES for _ in range(2)],
        [pltpu.VMEM((count, columns), bf16), pltpu.VMEM((length, 2 * HD), bf16)],
        12,
    )
    outs, x_other = together(outs, x_other)

    def queries_of(x):
        (queries,) = run_kernel(
            query_kernel,
            [*x, w_query],
            [((length // 2, columns), f32)],
            [pltpu.VMEM((length // 2, columns), f32)],
        )
        return queries

    came = [swap(outs[2 * i + 1], CORE) for i in range(3)]
    came, x_own = together(came, x_own)
    totals = [add(outs[2 * i], came[i]) for i in range(3)]
    keep, send = [], []
    for total, side in zip(totals, sides):
        middle = total.shape[1] // 2
        left, right = total[:, :middle], total[:, middle:]
        keep.append(jnp.where(side, right, left))
        send.append(jnp.where(side, left, right))
    got = [swap(block, order[0]) for block, (_, _, order) in zip(send, PIECES)]

    got, query_own, x_other = together(got, queries_of(x_own), x_other)
    totals = added(keep, got)
    got, query_other = together(step_up(totals, 1), queries_of(x_other))
    totals = added(totals, got)
    masked_1, is_list = flags[:, :1] > 0, flags[:, 1:2] > 0
    (base,) = run_kernel(
        base_kernel,
        [pair_own, pair_other, query_own, query_other, cosine, sine, base_mask, flags],
        [((length, columns + 2 * HD), bf16)],
    )
    got, place, base = together(step_up(totals, 2), place, base)
    totals = added(totals, got)
    states = []
    for (first, width, _), total, side in zip(PIECES, totals, sides):
        row = mask_embed[None, first : first + width]
        middle = width // 2
        states.append(add(jnp.where(side, row[:, middle:], row[:, :middle]), total))
    kv_weights = head_weights(place, 60000000)
    got, kv_weights = together(step_up(states, 0), kv_weights)
    raw = []
    for state, block, side in zip(states, got, sides):
        raw.append(
            jnp.where(
                side, jnp.concatenate([block, state], axis=1), jnp.concatenate([state, block], axis=1)
            )
        )
    raw = [(block, swap(block, CORE)) for block in raw]

    operands = [half for both in raw for half in both]
    operands += [gain, list_cosine, list_sine, match, base, w_query, kv_weights, w_out]
    outs = run_kernel(
        second_kernel,
        operands,
        [((length // 2, width), bf16) for _, width, _ in PIECES for _ in range(2)],
        [
            pltpu.VMEM((count, CHUNKS[0][1]), bf16),
            pltpu.VMEM((count, columns + 2 * HD), bf16),
            pltpu.VMEM((length, columns + 2 * HD), bf16),
            pltpu.VMEM((length, columns), bf16),
        ],
        26,
    )
    keep, send = outs[::2], outs[1::2]
    totals = [
        add(one, swap(two, CORE)).reshape(2, 2, 2, rows, one.shape[1]) for one, two in zip(keep, send)
    ]
    keep, incoming = step_down(totals, 0)
    own_match = match[:rows]
    middle = count // 2
    states = jnp.concatenate(
        [pick(own_match[:, :middle], one) + pick(own_match[:, middle:], two) for one, two in raw], axis=1
    )
    hidden_1 = jnp.where(
        masked_1[:rows], mask_embed[None, :], jnp.where(is_list[:rows], states, tokens)
    )
    incoming, hidden_1 = together(incoming, hidden_1)
    keep, incoming = step_down(added(keep, incoming), 1)
    incoming = together(*incoming)
    keep, incoming = step_down(added(keep, incoming), 2)
    incoming = together(*incoming)
    summed_1 = jnp.concatenate(added(keep, incoming), axis=1)
    return (hidden_1.astype(jnp.float32) + summed_1.astype(jnp.float32)).astype(jnp.bfloat16), needed


def shards(*args):
    positions = args[1]
    result, needed = together(*steps(FEW, *args))
    return lax.cond(
        needed[0, 0] <= FEW, lambda: result, lambda: steps(positions.shape[1], *args)[0]
    )


def solution(mesh):
    placed = (
        P(("dp", "tensor"), None),
        P("dp", None),
        P(),
        P(),
        P(None, "tensor"),
        P(None, "tensor"),
        P(None, "tensor"),
        P("tensor", None),
    )
    return jax.shard_map(
        shards, mesh=mesh, in_specs=placed, out_specs=P(("dp", "tensor"), None), check_vma=False
    )
```

```python
import functools

import jax
import jax.numpy as jnp
from jax import lax
from jax.experimental import pallas as pl
from jax.experimental.pallas import tpu as pltpu
from jax.sharding import PartitionSpec as P

HD = 128
HALF = HD // 2
PARTS = 16
CORE, ZED, NEAR, FAR = 1, 2, 4, 12
LINKS = (NEAR, FAR, ZED)
PIECES = (
    (0, 2816, (NEAR, FAR, ZED)),
    (2816, 2816, (FAR, ZED, NEAR)),
    (5632, 2560, (ZED, NEAR, FAR)),
)
CHUNKS = [(first + i * width // 2, width // 2) for first, width, _ in PIECES for i in range(2)]
FEW = 160
BLOCKS = [a ^ b ^ c for a in (0, NEAR) for b in (0, FAR) for c in (0, ZED)]


def swap(value, mask):
    return lax.ppermute(value, "tensor", [(i, i ^ mask) for i in range(PARTS)])


def normalize(rows, gain):
    values = rows.astype(jnp.float32)
    scale = lax.rsqrt(jnp.mean(values * values, axis=-1, keepdims=True) + 1e-05)
    return (values * scale * gain.astype(jnp.float32)).astype(jnp.bfloat16)


def turn_heads(values, cosine, sine):
    out = []
    for at in range(0, values.shape[1], HD):
        left, right = values[:, at : at + HALF], values[:, at + HALF : at + HD]
        out += [left * cosine - right * sine, right * cosine + left * sine]
    return jnp.concatenate(out, axis=1).astype(jnp.bfloat16)


def together(*values):
    return lax.optimization_barrier(values)


def keys_after(order, steps):
    keys = [0]
    for mask in order[:steps]:
        keys = keys + [key ^ mask for key in keys]
    return keys


def step_up(have, step):
    return [swap(block, order[step]) for block, (_, _, order) in zip(have, PIECES)]


def in_order(blocks, order, rows):
    keys = keys_after(order, 3)
    at = [keys.index(m) * rows for m in BLOCKS]
    return jnp.concatenate([blocks[i : i + rows] for i in at], axis=0)


def add(one, two):
    return (one.astype(jnp.float32) + two.astype(jnp.float32)).astype(jnp.bfloat16)


def step_down(totals, step):
    keep, got = [], []
    for total, (_, _, order) in zip(totals, PIECES):
        left = [mask for mask in LINKS if mask not in order[:step]]
        at = left.index(order[step])
        keep.append(lax.index_in_dim(total, 0, at, keepdims=False))
        got.append(swap(lax.index_in_dim(total, 1, at, keepdims=False), order[step]))
    return keep, got


def added(keep, got):
    return [add(one, two) for one, two in zip(keep, got)]


def with_heads(query, key, value, mixed):
    rows, columns = query.shape
    tile = rows // 2
    for h in range(columns // HD):
        for at in range(0, rows, tile):
            scores = lax.dot_general(
                query[at : at + tile, HD * h : HD * (h + 1)],
                key,
                (((1,), (1,)), ((), ())),
                preferred_element_type=jnp.float32,
            ) * HD ** (-0.5)
            weights = jnp.exp(scores - jnp.max(scores, axis=-1, keepdims=True))
            probs = weights * (1.0 / jnp.sum(weights, axis=-1, keepdims=True))
            mixed[at : at + tile, HD * h : HD * (h + 1)] = jnp.dot(
                probs.astype(jnp.bfloat16), value, preferred_element_type=jnp.float32
            ).astype(jnp.bfloat16)


def project_out(mixed, out_here, outs):
    half = mixed.shape[0] // 2
    for i, (first, width) in enumerate(CHUNKS):
        weights = out_here[:, first : first + width]
        at = (i % 2) * width
        for side in range(2):
            outs[2 * (i // 2) + side][:, at : at + width] = jnp.dot(
                mixed[half * side : half * (side + 1), :], weights, preferred_element_type=jnp.float32
            ).astype(jnp.bfloat16)


def first_kernel(query, pair_own, pair_other, out_here, *rest):
    outs, (mixed, pair) = rest[:6], rest[6:]
    half = pair_own.shape[0]
    pair[:half, :] = pair_own[...]
    pair[half:, :] = pair_other[...]
    with_heads(query, pair[:, :HD], pair[:, HD:], mixed)
    project_out(mixed, out_here, outs)


def turned(values, cosine, sine):
    return (values * cosine + pltpu.roll(values, HALF, 1) * sine).astype(jnp.bfloat16)


def second_kernel(*refs):
    raw, refs = refs[:6], refs[6:]
    gain, cosine, sine, match, base, query_here, kv_here, out_here = refs[:8]
    outs, refs = refs[8:14], refs[14:]
    normed, moving, placed, mixed = refs
    half = raw[0].shape[0]
    width_all = gain.shape[1]
    scales = []
    for side in range(2):
        squares = jnp.zeros((half, HD), jnp.float32)
        for piece in range(3):
            ref = raw[2 * piece + side]

            def add_squares(i, squares, ref=ref):
                values = ref[:, pl.ds(pl.multiple_of(i * HD, HD), HD)].astype(jnp.float32)
                return squares + values * values

            squares = lax.fori_loop(0, ref.shape[1] // HD, add_squares, squares, unroll=2)
        mean = jnp.sum(squares, axis=-1, keepdims=True) * (1.0 / width_all)
        scales.append(lax.rsqrt(mean + 1e-05))
    queries = jnp.zeros((2 * half, query_here.shape[1]), jnp.float32)
    pairs = jnp.zeros((2 * half, kv_here.shape[0]), jnp.float32)
    for i, (first, width) in enumerate(CHUNKS):
        at = (i % 2) * width
        for side in range(2):
            values = raw[2 * (i // 2) + side][:, at : at + width].astype(jnp.float32)
            normed[half * side : half * (side + 1), :width] = (
                values * scales[side] * gain[:, first : first + width]
            ).astype(jnp.bfloat16)
        some = normed[:, :width]
        queries += jnp.dot(some, query_here[first : first + width, :], preferred_element_type=jnp.float32)
        pairs += dot_rows(some, kv_here[:, first : first + width])
    moving[:, :HD] = turned(pairs[:, :HD], cosine[...], sine[...])
    moving[:, HD : 2 * HD] = pairs[:, HD:].astype(jnp.bfloat16)
    for h in range(queries.shape[1] // HD):
        moving[:, HD * (h + 2) : HD * (h + 3)] = turned(queries[:, HD * h : HD * (h + 1)], cosine[...], sine[...])
    placed[...] = base[...] + jnp.dot(
        match[...], moving[...], preferred_element_type=jnp.float32
    ).astype(jnp.bfloat16)
    with_heads(placed.at[:, 2 * HD :], placed[:, :HD], placed[:, HD : 2 * HD], mixed)
    project_out(mixed, out_here, outs)


def dot_rows(x, weights):
    return lax.dot_general(x, weights, (((1,), (1,)), ((), ())), preferred_element_type=jnp.float32)


def query_kernel(one, two, three, weights, out, total):
    rows = out.shape[0] // 8
    for i, (piece, (first, width, order)) in enumerate(zip((one, two, three), PIECES)):
        total[...] = jnp.dot(piece[...], weights[first : first + width, :], preferred_element_type=jnp.float32)
        for j, key in enumerate(keys_after(order, 3)):
            at = BLOCKS.index(key) * rows
            some = total[j * rows : (j + 1) * rows, :]
            if i == 0:
                out[at : at + rows, :] = some
            else:
                out[at : at + rows, :] += some


def dot_rows(x, weights):
    return lax.dot_general(x, weights, (((1,), (1,)), ((), ())), preferred_element_type=jnp.float32)


def base_kernel(pair_own, pair_other, query_own, query_other, cosine, sine, masked, flags, base):
    half = pair_own.shape[0]
    for core, (pair, query) in enumerate(((pair_own, query_own), (pair_other, query_other))):
        some = slice(half * core, half * (core + 1))
        is_masked, is_list = flags[some, :1] > 0, flags[some, 1:2] > 0
        for at in range(0, base.shape[1], HD):
            if at < 2 * HD:
                values = pair[:, at : at + HD]
            else:
                values = turned(query[:, at - 2 * HD : at - HD], cosine[some, :], sine[some, :])
            values = jnp.where(is_list, 0.0, values.astype(jnp.float32))
            mask_values = masked[some, at : at + HD].astype(jnp.float32)
            base[some, at : at + HD] = jnp.where(is_masked, mask_values, values).astype(jnp.bfloat16)


def call_kernel(kernel, operands, outs, scratch=(), mib=16, last=(), moved=100000, least=0):
    places = [pltpu.VMEM] * (len(operands) - len(last)) + list(last)
    return pl.pallas_call(
        kernel,
        out_shape=[jax.ShapeDtypeStruct(*out) for out in outs],
        in_specs=[pl.BlockSpec(memory_space=place) for place in places],
        out_specs=[pl.BlockSpec(memory_space=pltpu.VMEM)] * len(outs),
        scratch_shapes=list(scratch),
        compiler_params=pltpu.CompilerParams(vmem_limit_bytes=max(mib, least) * 2**20),
        cost_estimate=pl.CostEstimate(flops=1000000, bytes_accessed=moved, transcendentals=0),
    )(*operands)


def load_kernel(source, out, sem):
    copy = pltpu.make_async_copy(source, out, sem)
    copy.start()
    copy.wait()


def join_kernel(*refs):
    for i in range(3):
        have, got, out = refs[i], refs[3 + i], refs[6 + i]
        rows = have.shape[0]
        out[:rows, :] = have[...]
        out[rows:, :] = got[...]


def joined(have, got):
    outs = [((2 * block.shape[0], block.shape[1]), block.dtype) for block in have]
    return call_kernel(join_kernel, [*have, *got], outs, mib=12)


def weight_rows_kernel(key, value, other_key, other_value, place, out):
    even = place[0, 0] % 2 == 0

    @pl.when(even)
    def _():
        out[:HALF, :] = key[...]
        out[HALF : 2 * HALF, :] = other_key[...]
        out[2 * HALF : 3 * HALF, :] = value[...]
        out[3 * HALF :, :] = other_value[...]

    @pl.when(jnp.logical_not(even))
    def _():
        out[:HALF, :] = other_key[...]
        out[HALF : 2 * HALF, :] = key[...]
        out[2 * HALF : 3 * HALF, :] = other_value[...]
        out[3 * HALF :, :] = value[...]


def table_kernel(positions, freq, place, cosine, sine, list_cosine, list_sine, match, flags, needed):
    f32, bf16 = jnp.float32, jnp.bfloat16
    count, length, chosen = match.shape[1], match.shape[0], positions.shape[1]
    rows = length // PARTS
    at = lax.broadcasted_iota(jnp.int32, (length, 1), 0)
    block = at // rows
    offset = (block // 8) * CORE ^ (block // 4 % 2) * NEAR ^ (block // 2 % 2) * FAR ^ (block % 2) * ZED
    spots = (place[0, 0] ^ offset) * rows + at % rows
    listed = (lax.broadcasted_iota(jnp.int32, (count, 1), 0) + place[0, 0] % 2 * (count // 2)) % count
    ones_across, twos_across = positions[:1, :], positions[1:, :]
    row = lax.broadcasted_iota(jnp.int32, (chosen, chosen), 0)
    column = lax.broadcasted_iota(jnp.int32, (chosen, chosen), 1)
    twos = jnp.sum(jnp.where(row == column, twos_across, 0), axis=1, keepdims=True)
    stale = jnp.max(jnp.where(twos == ones_across, 1.0, 0.0), axis=0, keepdims=True)
    fresh = 1.0 - stale
    before = jnp.where(row < column, 1.0, 0.0).astype(bf16)

    def ahead(flag):
        wide = jnp.broadcast_to(flag, (16, chosen)).astype(bf16)
        return jnp.dot(wide, before, preferred_element_type=f32)[:1]

    fresh_count = jnp.sum(fresh, axis=1, keepdims=True)
    rank = jnp.where(fresh > 0, ahead(fresh), fresh_count + ahead(stale))
    needed[...] = jnp.broadcast_to(fresh_count, needed.shape)
    spot = jnp.where(listed.astype(f32) == rank, 1.0, 0.0)
    list_spots = jnp.sum(spot * ones_across.astype(f32), axis=1, keepdims=True)
    here = jnp.where((spots == ones_across) & (fresh > 0), 1.0, 0.0)
    match[...] = dot_rows(here.astype(bf16), spot.astype(bf16)).astype(bf16)
    is_list = jnp.max(here, axis=1, keepdims=True)
    masked_1 = jnp.max(jnp.where(spots == twos_across, 1.0, 0.0), axis=1, keepdims=True)
    lane = lax.broadcasted_iota(jnp.int32, (spots.shape[0], HD), 1)
    flags[...] = jnp.where(lane == 0, masked_1, is_list)
    sign = jnp.where(lax.broadcasted_iota(jnp.int32, (1, HD), 1) < HALF, -1.0, 1.0)
    angle = spots.astype(f32) * freq[...]
    cosine[...] = jnp.cos(angle)
    sine[...] = jnp.sin(angle) * sign
    angle = list_spots * freq[...]
    list_cosine[...] = jnp.cos(angle)
    list_sine[...] = jnp.sin(angle) * sign


def mask_kernel(embed, gain, query_here, kv_here, cosine, sine, list_cosine, list_sine, query, base):
    values = embed[...].astype(jnp.float32)
    mean = jnp.sum(values * values, axis=-1, keepdims=True) * (1.0 / embed.shape[1])
    row = (values * lax.rsqrt(mean + 1e-05) * gain[...]).astype(jnp.bfloat16)
    row = jnp.broadcast_to(row, (16, row.shape[1]))
    queries = jnp.dot(row, query_here[...], preferred_element_type=jnp.float32)[:1]
    pairs = dot_rows(row, kv_here[...])[:1]
    length = base.shape[0]
    base[:, :HD] = turned(jnp.broadcast_to(pairs[:, :HD], (length, HD)), cosine[...], sine[...])
    base[:, HD : 2 * HD] = jnp.broadcast_to(pairs[:, HD:], (length, HD)).astype(jnp.bfloat16)
    for at in range(0, queries.shape[1], HD):
        some = queries[:, at : at + HD]
        base[:, 2 * HD + at : 3 * HD + at] = turned(jnp.broadcast_to(some, (length, HD)), cosine[...], sine[...])
        query[:, at : at + HD] = turned(
            jnp.broadcast_to(some, (query.shape[0], HD)), list_cosine[...], list_sine[...]
        )


def add_pairs(pieces, kv_here, total, low, fresh):
    rows = total.shape[0] // 8
    for piece, (first, width, order) in zip(pieces, PIECES):
        product = dot_rows(piece[...], kv_here[:, first : first + width])
        for i, key in enumerate(keys_after(order, 3)[low : low + 4]):
            at = BLOCKS.index(key) * rows
            some = product[i * rows : (i + 1) * rows]
            if key in fresh:
                fresh.remove(key)
                total[at : at + rows, :] = some
            else:
                total[at : at + rows, :] += some


def early_kernel(one, two, three, kv_here, total):
    fresh = set(BLOCKS)
    add_pairs((one, two, three), kv_here, total, 0, fresh)
    rows = total.shape[0] // 8
    for key in fresh:
        at = BLOCKS.index(key) * rows
        total[at : at + rows, :] = jnp.zeros((rows, total.shape[1]), jnp.float32)


def late_kernel(one, two, three, kv_here, early, cosine, sine, out, total):
    total[...] = early[...]
    add_pairs((one, two, three), kv_here, total, 4, set())
    rows = total.shape[0]
    out[:, :HD] = turned(total[:, :HD], cosine[:rows, :], sine[:rows, :])
    out[:, HD:] = total[:, HD:].astype(jnp.bfloat16)


def chosen(spots, positions):
    return jnp.any(spots[:, None] == positions[None, :], axis=1)


def pick(one_hot, rows):
    return jnp.dot(
        one_hot.astype(jnp.bfloat16), rows, preferred_element_type=jnp.float32
    ).astype(jnp.bfloat16)


def steps(count, tokens, positions, mask_embed, norm_gain, w_query, w_key, w_value, w_out):
    place = lax.axis_index("tensor")
    run_kernel = functools.partial(call_kernel, least=0 if count <= FEW else 52)
    rows = tokens.shape[0]
    length = rows * PARTS

    own_spots = place * rows + jnp.arange(rows, dtype=jnp.int32)
    own_masked_0 = chosen(own_spots, positions[0])
    hidden_0 = jnp.where(own_masked_0[:, None], mask_embed[None, :], tokens)
    normed_0 = normalize(hidden_0, norm_gain)
    key_rows, value_rows = w_key.T, w_value.T
    bits = {NEAR: (place >> 2 ^ place >> 3) & 1 == 1, FAR: place >> 3 & 1 == 1, ZED: place >> 1 & 1 == 1}
    sides = [bits[order[0]] for _, _, order in PIECES]
    normed_0, positions, place, sides, key_rows, value_rows = together(
        normed_0, positions, place, sides, key_rows, value_rows
    )
    have = [normed_0[:, first : first + width] for first, width, _ in PIECES]

    f32, bf16 = jnp.float32, jnp.bfloat16
    columns = w_query.shape[1]
    freq = 500000.0 ** (-(jnp.arange(HD, dtype=f32) % HALF * 2.0 / HD))
    cosine, sine, list_cosine, list_sine, match, flags, needed = run_kernel(
        table_kernel,
        [positions, freq[None], place.reshape(1, 1)],
        [((length, HD), f32)] * 2 + [((count, HD), f32)] * 2 + [((length, count), bf16), ((length, HD), f32), ((8, HD), f32)],
        last=[pltpu.SMEM],
    )
    other_rows = swap(key_rows, CORE), swap(value_rows, CORE)
    tables = (cosine, sine, list_cosine, list_sine, match, flags)
    got, tables, other_rows, place = together(step_up(have, 0), tables, other_rows, place)
    cosine, sine, list_cosine, list_sine, match, flags = tables
    have = joined(have, got)

    def head_weights(place, moved):
        (weights,) = run_kernel(
            weight_rows_kernel,
            [key_rows, value_rows, *other_rows, place.reshape(1, 1)],
            [((4 * HALF, key_rows.shape[1]), bf16)],
            last=[pltpu.SMEM],
            moved=moved,
        )
        return weights

    kv_weights = head_weights(place, 100000)
    def load(weights):
        if count > FEW:
            return weights
        return run_kernel(
            load_kernel, [weights], [(weights.shape, weights.dtype)], [pltpu.SemaphoreType.DMA], 1, [pl.ANY]
        )[0]

    w_query = load(w_query)
    got, kv_weights, mask_embed, norm_gain, w_query, w_out = together(
        step_up(have, 1), kv_weights, mask_embed, norm_gain, w_query, w_out
    )
    have = joined(have, got)

    gain = norm_gain[None, :].astype(f32)
    query_0, base_mask = run_kernel(
        mask_kernel,
        [mask_embed[None, :], gain, w_query, kv_weights, cosine, sine, list_cosine, list_sine],
        [((count, columns), bf16), ((length, columns + 2 * HD), bf16)],
    )
    (early,) = run_kernel(early_kernel, [*have, kv_weights], [((length // 2, 2 * HD), f32)])
    w_out = load(w_out)
    got, query_0, base_mask, early, w_out = together(step_up(have, 2), query_0, base_mask, early, w_out)

    (pair_own,) = run_kernel(
        late_kernel,
        [*got, kv_weights, early, cosine, sine],
        [((length // 2, 2 * HD), bf16)],
        [pltpu.VMEM((length // 2, 2 * HD), f32)],
    )
    x_own = joined(have, got)
    pair_other, x_own = together(swap(pair_own, CORE), x_own)
    x_other = [swap(block, CORE) for block in x_own]
    outs = run_kernel(
        first_kernel,
        [query_0, pair_own, pair_other, w_out],
        [((count // 2, width), bf16) for _, width, _ in PIECES for _ in range(2)],
        [pltpu.VMEM((count, columns), bf16), pltpu.VMEM((length, 2 * HD), bf16)],
        12,
    )
    outs, x_other = together(outs, x_other)

    def queries_of(x):
        (queries,) = run_kernel(
            query_kernel,
            [*x, w_query],
            [((length // 2, columns), f32)],
            [pltpu.VMEM((length // 2, columns), f32)],
        )
        return queries

    came = [swap(outs[2 * i + 1], CORE) for i in range(3)]
    came, x_own = together(came, x_own)
    totals = [add(outs[2 * i], came[i]) for i in range(3)]
    keep, send = [], []
    for total, side in zip(totals, sides):
        middle = total.shape[1] // 2
        left, right = total[:, :middle], total[:, middle:]
        keep.append(jnp.where(side, right, left))
        send.append(jnp.where(side, left, right))
    got = [swap(block, order[0]) for block, (_, _, order) in zip(send, PIECES)]

    got, query_own, x_other = together(got, queries_of(x_own), x_other)
    totals = added(keep, got)
    got, query_other = together(step_up(totals, 1), queries_of(x_other))
    totals = added(totals, got)
    masked_1, is_list = flags[:, :1] > 0, flags[:, 1:2] > 0
    (base,) = run_kernel(
        base_kernel,
        [pair_own, pair_other, query_own, query_other, cosine, sine, base_mask, flags],
        [((length, columns + 2 * HD), bf16)],
    )
    got, place, base = together(step_up(totals, 2), place, base)
    totals = added(totals, got)
    states = []
    for (first, width, _), total, side in zip(PIECES, totals, sides):
        row = mask_embed[None, first : first + width]
        middle = width // 2
        states.append(add(jnp.where(side, row[:, middle:], row[:, :middle]), total))
    kv_weights = head_weights(place, 100000)
    got, kv_weights = together(step_up(states, 0), kv_weights)
    raw = []
    for state, block, side in zip(states, got, sides):
        raw.append(
            jnp.where(
                side, jnp.concatenate([block, state], axis=1), jnp.concatenate([state, block], axis=1)
            )
        )
    raw = [(block, swap(block, CORE)) for block in raw]

    operands = [half for both in raw for half in both]
    operands += [gain, list_cosine, list_sine, match, base, w_query, kv_weights, w_out]
    outs = run_kernel(
        second_kernel,
        operands,
        [((length // 2, width), bf16) for _, width, _ in PIECES for _ in range(2)],
        [
            pltpu.VMEM((count, CHUNKS[0][1]), bf16),
            pltpu.VMEM((count, columns + 2 * HD), bf16),
            pltpu.VMEM((length, columns + 2 * HD), bf16),
            pltpu.VMEM((length, columns), bf16),
        ],
        26,
    )
    keep, send = outs[::2], outs[1::2]
    totals = [
        add(one, swap(two, CORE)).reshape(2, 2, 2, rows, one.shape[1]) for one, two in zip(keep, send)
    ]
    keep, incoming = step_down(totals, 0)
    own_match = match[:rows]
    middle = count // 2
    states = jnp.concatenate(
        [pick(own_match[:, :middle], one) + pick(own_match[:, middle:], two) for one, two in raw], axis=1
    )
    hidden_1 = jnp.where(
        masked_1[:rows], mask_embed[None, :], jnp.where(is_list[:rows], states, tokens)
    )
    incoming, hidden_1 = together(incoming, hidden_1)
    keep, incoming = step_down(added(keep, incoming), 1)
    incoming = together(*incoming)
    keep, incoming = step_down(added(keep, incoming), 2)
    incoming = together(*incoming)
    summed_1 = jnp.concatenate(added(keep, incoming), axis=1)
    return (hidden_1.astype(jnp.float32) + summed_1.astype(jnp.float32)).astype(jnp.bfloat16), needed


def shards(*args):
    positions = args[1]
    result, needed = together(*steps(FEW, *args))
    return lax.cond(
        needed[0, 0] <= FEW, lambda: result, lambda: steps(positions.shape[1], *args)[0]
    )


def solution(mesh):
    placed = (
        P(("dp", "tensor"), None),
        P("dp", None),
        P(),
        P(),
        P(None, "tensor"),
        P(None, "tensor"),
        P(None, "tensor"),
        P("tensor", None),
    )
    return jax.shard_map(
        shards, mesh=mesh, in_specs=placed, out_specs=P(("dp", "tensor"), None), check_vma=False
    )
```

```python
import functools

import jax
import jax.numpy as jnp
from jax import lax
from jax.experimental import pallas as pl
from jax.experimental.pallas import tpu as pltpu
from jax.sharding import PartitionSpec as P

HD = 128
HALF = HD // 2
PARTS = 16
CORE, ZED, NEAR, FAR = 1, 2, 4, 12
LINKS = (NEAR, FAR, ZED)
PIECES = (
    (0, 2816, (NEAR, FAR, ZED)),
    (2816, 2816, (FAR, ZED, NEAR)),
    (5632, 2560, (ZED, NEAR, FAR)),
)
CHUNKS = [(first + i * width // 2, width // 2) for first, width, _ in PIECES for i in range(2)]
FEW = 160
BLOCKS = [a ^ b ^ c for a in (0, NEAR) for b in (0, FAR) for c in (0, ZED)]


def swap(value, mask):
    return lax.ppermute(value, "tensor", [(i, i ^ mask) for i in range(PARTS)])


def normalize(rows, gain):
    values = rows.astype(jnp.float32)
    scale = lax.rsqrt(jnp.mean(values * values, axis=-1, keepdims=True) + 1e-05)
    return (values * scale * gain.astype(jnp.float32)).astype(jnp.bfloat16)


def turn_heads(values, cosine, sine):
    out = []
    for at in range(0, values.shape[1], HD):
        left, right = values[:, at : at + HALF], values[:, at + HALF : at + HD]
        out += [left * cosine - right * sine, right * cosine + left * sine]
    return jnp.concatenate(out, axis=1).astype(jnp.bfloat16)


def together(*values):
    return lax.optimization_barrier(values)


def keys_after(order, steps):
    keys = [0]
    for mask in order[:steps]:
        keys = keys + [key ^ mask for key in keys]
    return keys


def step_up(have, step):
    return [swap(block, order[step]) for block, (_, _, order) in zip(have, PIECES)]


def in_order(blocks, order, rows):
    keys = keys_after(order, 3)
    at = [keys.index(m) * rows for m in BLOCKS]
    return jnp.concatenate([blocks[i : i + rows] for i in at], axis=0)


def add(one, two):
    return (one.astype(jnp.float32) + two.astype(jnp.float32)).astype(jnp.bfloat16)


def step_down(totals, step):
    keep, got = [], []
    for total, (_, _, order) in zip(totals, PIECES):
        left = [mask for mask in LINKS if mask not in order[:step]]
        at = left.index(order[step])
        keep.append(lax.index_in_dim(total, 0, at, keepdims=False))
        got.append(swap(lax.index_in_dim(total, 1, at, keepdims=False), order[step]))
    return keep, got


def added(keep, got):
    return [add(one, two) for one, two in zip(keep, got)]


def with_heads(query, key, value, mixed):
    rows, columns = query.shape
    tile = rows
    for h in range(columns // HD):
        for at in range(0, rows, tile):
            scores = lax.dot_general(
                query[at : at + tile, HD * h : HD * (h + 1)],
                key,
                (((1,), (1,)), ((), ())),
                preferred_element_type=jnp.float32,
            ) * HD ** (-0.5)
            weights = jnp.exp(scores - jnp.max(scores, axis=-1, keepdims=True))
            probs = weights * (1.0 / jnp.sum(weights, axis=-1, keepdims=True))
            mixed[at : at + tile, HD * h : HD * (h + 1)] = jnp.dot(
                probs.astype(jnp.bfloat16), value, preferred_element_type=jnp.float32
            ).astype(jnp.bfloat16)


def project_out(mixed, out_here, outs):
    half = mixed.shape[0] // 2
    for i, (first, width) in enumerate(CHUNKS):
        weights = out_here[:, first : first + width]
        at = (i % 2) * width
        product = jnp.dot(mixed[...], weights, preferred_element_type=jnp.float32).astype(jnp.bfloat16)
        for side in range(2):
            outs[2 * (i // 2) + side][:, at : at + width] = product[half * side : half * (side + 1)]


def first_kernel(query, pair_own, pair_other, out_here, *rest):
    outs, (mixed, pair) = rest[:6], rest[6:]
    half = pair_own.shape[0]
    pair[:half, :] = pair_own[...]
    pair[half:, :] = pair_other[...]
    with_heads(query, pair[:, :HD], pair[:, HD:], mixed)
    project_out(mixed, out_here, outs)


def turned(values, cosine, sine):
    return (values * cosine + pltpu.roll(values, HALF, 1) * sine).astype(jnp.bfloat16)


def second_kernel(*refs):
    raw, refs = refs[:6], refs[6:]
    gain, cosine, sine, match, base, query_here, kv_here, out_here = refs[:8]
    outs, refs = refs[8:14], refs[14:]
    normed, moving, placed, mixed = refs
    half = raw[0].shape[0]
    width_all = gain.shape[1]
    scales = []
    for side in range(2):
        squares = jnp.zeros((half, HD), jnp.float32)
        for piece in range(3):
            ref = raw[2 * piece + side]

            def add_squares(i, squares, ref=ref):
                values = ref[:, pl.ds(pl.multiple_of(i * HD, HD), HD)].astype(jnp.float32)
                return squares + values * values

            squares = lax.fori_loop(0, ref.shape[1] // HD, add_squares, squares, unroll=ref.shape[1] // HD // 2)
        mean = jnp.sum(squares, axis=-1, keepdims=True) * (1.0 / width_all)
        scales.append(lax.rsqrt(mean + 1e-05))
    queries = jnp.zeros((2 * half, query_here.shape[1]), jnp.float32)
    pairs = jnp.zeros((2 * half, kv_here.shape[0]), jnp.float32)
    for i, (first, width) in enumerate(CHUNKS):
        at = (i % 2) * width
        for side in range(2):
            values = raw[2 * (i // 2) + side][:, at : at + width].astype(jnp.float32)
            normed[half * side : half * (side + 1), :width] = (
                values * scales[side] * gain[:, first : first + width]
            ).astype(jnp.bfloat16)
        some = normed[:, :width]
        queries += jnp.dot(some, query_here[first : first + width, :], preferred_element_type=jnp.float32)
        pairs += dot_rows(some, kv_here[:, first : first + width])
    moving[:, :HD] = turned(pairs[:, :HD], cosine[...], sine[...])
    moving[:, HD : 2 * HD] = pairs[:, HD:].astype(jnp.bfloat16)
    for h in range(queries.shape[1] // HD):
        moving[:, HD * (h + 2) : HD * (h + 3)] = turned(queries[:, HD * h : HD * (h + 1)], cosine[...], sine[...])
    placed[...] = base[...] + jnp.dot(
        match[...], moving[...], preferred_element_type=jnp.float32
    ).astype(jnp.bfloat16)
    with_heads(placed.at[:, 2 * HD :], placed[:, :HD], placed[:, HD : 2 * HD], mixed)
    project_out(mixed, out_here, outs)


def dot_rows(x, weights):
    return lax.dot_general(x, weights, (((1,), (1,)), ((), ())), preferred_element_type=jnp.float32)


def query_kernel(one, two, three, weights, out, total):
    rows = out.shape[0] // 8
    for i, (piece, (first, width, order)) in enumerate(zip((one, two, three), PIECES)):
        total[...] = jnp.dot(piece[...], weights[first : first + width, :], preferred_element_type=jnp.float32)
        for j, key in enumerate(keys_after(order, 3)):
            at = BLOCKS.index(key) * rows
            some = total[j * rows : (j + 1) * rows, :]
            if i == 0:
                out[at : at + rows, :] = some
            else:
                out[at : at + rows, :] += some


def dot_rows(x, weights):
    return lax.dot_general(x, weights, (((1,), (1,)), ((), ())), preferred_element_type=jnp.float32)


def base_kernel(pair_own, pair_other, query_own, query_other, cosine, sine, masked, flags, base):
    half = pair_own.shape[0]
    for core, (pair, query) in enumerate(((pair_own, query_own), (pair_other, query_other))):
        some = slice(half * core, half * (core + 1))
        is_masked, is_list = flags[some, :1] > 0, flags[some, 1:2] > 0
        for at in range(0, base.shape[1], HD):
            if at < 2 * HD:
                values = pair[:, at : at + HD]
            else:
                values = turned(query[:, at - 2 * HD : at - HD], cosine[some, :], sine[some, :])
            values = jnp.where(is_list, 0.0, values.astype(jnp.float32))
            mask_values = masked[some, at : at + HD].astype(jnp.float32)
            base[some, at : at + HD] = jnp.where(is_masked, mask_values, values).astype(jnp.bfloat16)


def call_kernel(kernel, operands, outs, scratch=(), mib=16, last=(), moved=100000, least=0):
    places = [pltpu.VMEM] * (len(operands) - len(last)) + list(last)
    return pl.pallas_call(
        kernel,
        out_shape=[jax.ShapeDtypeStruct(*out) for out in outs],
        in_specs=[pl.BlockSpec(memory_space=place) for place in places],
        out_specs=[pl.BlockSpec(memory_space=pltpu.VMEM)] * len(outs),
        scratch_shapes=list(scratch),
        compiler_params=pltpu.CompilerParams(vmem_limit_bytes=max(mib, least) * 2**20),
        cost_estimate=pl.CostEstimate(flops=1000000, bytes_accessed=moved, transcendentals=0),
    )(*operands)


def load_kernel(source, out, sem):
    copy = pltpu.make_async_copy(source, out, sem)
    copy.start()
    copy.wait()


def join_kernel(*refs):
    for i in range(3):
        have, got, out = refs[i], refs[3 + i], refs[6 + i]
        rows = have.shape[0]
        out[:rows, :] = have[...]
        out[rows:, :] = got[...]


def joined(have, got):
    outs = [((2 * block.shape[0], block.shape[1]), block.dtype) for block in have]
    return call_kernel(join_kernel, [*have, *got], outs, mib=12)


def weight_rows_kernel(key, value, other_key, other_value, place, out):
    even = place[0, 0] % 2 == 0

    @pl.when(even)
    def _():
        out[:HALF, :] = key[...]
        out[HALF : 2 * HALF, :] = other_key[...]
        out[2 * HALF : 3 * HALF, :] = value[...]
        out[3 * HALF :, :] = other_value[...]

    @pl.when(jnp.logical_not(even))
    def _():
        out[:HALF, :] = other_key[...]
        out[HALF : 2 * HALF, :] = key[...]
        out[2 * HALF : 3 * HALF, :] = other_value[...]
        out[3 * HALF :, :] = value[...]


def table_kernel(positions, freq, place, cosine, sine, list_cosine, list_sine, match, flags, needed):
    f32, bf16 = jnp.float32, jnp.bfloat16
    count, length, chosen = match.shape[1], match.shape[0], positions.shape[1]
    rows = length // PARTS
    at = lax.broadcasted_iota(jnp.int32, (length, 1), 0)
    block = at // rows
    offset = (block // 8) * CORE ^ (block // 4 % 2) * NEAR ^ (block // 2 % 2) * FAR ^ (block % 2) * ZED
    spots = (place[0, 0] ^ offset) * rows + at % rows
    listed = (lax.broadcasted_iota(jnp.int32, (count, 1), 0) + place[0, 0] % 2 * (count // 2)) % count
    ones_across, twos_across = positions[:1, :], positions[1:, :]
    row = lax.broadcasted_iota(jnp.int32, (chosen, chosen), 0)
    column = lax.broadcasted_iota(jnp.int32, (chosen, chosen), 1)
    twos = jnp.sum(jnp.where(row == column, twos_across, 0), axis=1, keepdims=True)
    stale = jnp.max(jnp.where(twos == ones_across, 1.0, 0.0), axis=0, keepdims=True)
    fresh = 1.0 - stale
    before = jnp.where(row < column, 1.0, 0.0).astype(bf16)

    def ahead(flag):
        wide = jnp.broadcast_to(flag, (16, chosen)).astype(bf16)
        return jnp.dot(wide, before, preferred_element_type=f32)[:1]

    fresh_count = jnp.sum(fresh, axis=1, keepdims=True)
    rank = jnp.where(fresh > 0, ahead(fresh), fresh_count + ahead(stale))
    needed[...] = jnp.broadcast_to(fresh_count, needed.shape)
    spot = jnp.where(listed.astype(f32) == rank, 1.0, 0.0)
    list_spots = jnp.sum(spot * ones_across.astype(f32), axis=1, keepdims=True)
    here = jnp.where((spots == ones_across) & (fresh > 0), 1.0, 0.0)
    match[...] = dot_rows(here.astype(bf16), spot.astype(bf16)).astype(bf16)
    is_list = jnp.max(here, axis=1, keepdims=True)
    masked_1 = jnp.max(jnp.where(spots == twos_across, 1.0, 0.0), axis=1, keepdims=True)
    lane = lax.broadcasted_iota(jnp.int32, (spots.shape[0], HD), 1)
    flags[...] = jnp.where(lane == 0, masked_1, is_list)
    sign = jnp.where(lax.broadcasted_iota(jnp.int32, (1, HD), 1) < HALF, -1.0, 1.0)
    angle = spots.astype(f32) * freq[...]
    cosine[...] = jnp.cos(angle)
    sine[...] = jnp.sin(angle) * sign
    angle = list_spots * freq[...]
    list_cosine[...] = jnp.cos(angle)
    list_sine[...] = jnp.sin(angle) * sign


def mask_kernel(embed, gain, query_here, kv_here, cosine, sine, list_cosine, list_sine, query, base):
    values = embed[...].astype(jnp.float32)
    mean = jnp.sum(values * values, axis=-1, keepdims=True) * (1.0 / embed.shape[1])
    row = (values * lax.rsqrt(mean + 1e-05) * gain[...]).astype(jnp.bfloat16)
    row = jnp.broadcast_to(row, (16, row.shape[1]))
    queries = jnp.dot(row, query_here[...], preferred_element_type=jnp.float32)[:1]
    pairs = dot_rows(row, kv_here[...])[:1]
    length = base.shape[0]
    base[:, :HD] = turned(jnp.broadcast_to(pairs[:, :HD], (length, HD)), cosine[...], sine[...])
    base[:, HD : 2 * HD] = jnp.broadcast_to(pairs[:, HD:], (length, HD)).astype(jnp.bfloat16)
    for at in range(0, queries.shape[1], HD):
        some = queries[:, at : at + HD]
        base[:, 2 * HD + at : 3 * HD + at] = turned(jnp.broadcast_to(some, (length, HD)), cosine[...], sine[...])
        query[:, at : at + HD] = turned(
            jnp.broadcast_to(some, (query.shape[0], HD)), list_cosine[...], list_sine[...]
        )


def add_pairs(pieces, kv_here, total, low, fresh):
    rows = total.shape[0] // 8
    for piece, (first, width, order) in zip(pieces, PIECES):
        product = dot_rows(piece[...], kv_here[:, first : first + width])
        for i, key in enumerate(keys_after(order, 3)[low : low + 4]):
            at = BLOCKS.index(key) * rows
            some = product[i * rows : (i + 1) * rows]
            if key in fresh:
                fresh.remove(key)
                total[at : at + rows, :] = some
            else:
                total[at : at + rows, :] += some


def early_kernel(one, two, three, kv_here, total):
    fresh = set(BLOCKS)
    add_pairs((one, two, three), kv_here, total, 0, fresh)
    rows = total.shape[0] // 8
    for key in fresh:
        at = BLOCKS.index(key) * rows
        total[at : at + rows, :] = jnp.zeros((rows, total.shape[1]), jnp.float32)


def late_kernel(one, two, three, kv_here, early, cosine, sine, out, total):
    total[...] = early[...]
    add_pairs((one, two, three), kv_here, total, 4, set())
    rows = total.shape[0]
    out[:, :HD] = turned(total[:, :HD], cosine[:rows, :], sine[:rows, :])
    out[:, HD:] = total[:, HD:].astype(jnp.bfloat16)


def chosen(spots, positions):
    return jnp.any(spots[:, None] == positions[None, :], axis=1)


def pick(one_hot, rows):
    return jnp.dot(
        one_hot.astype(jnp.bfloat16), rows, preferred_element_type=jnp.float32
    ).astype(jnp.bfloat16)


def steps(count, tokens, positions, mask_embed, norm_gain, w_query, w_key, w_value, w_out):
    place = lax.axis_index("tensor")
    run_kernel = functools.partial(call_kernel, least=0 if count <= FEW else 52)
    rows = tokens.shape[0]
    length = rows * PARTS

    own_spots = place * rows + jnp.arange(rows, dtype=jnp.int32)
    own_masked_0 = chosen(own_spots, positions[0])
    hidden_0 = jnp.where(own_masked_0[:, None], mask_embed[None, :], tokens)
    normed_0 = normalize(hidden_0, norm_gain)
    key_rows, value_rows = w_key.T, w_value.T
    bits = {NEAR: (place >> 2 ^ place >> 3) & 1 == 1, FAR: place >> 3 & 1 == 1, ZED: place >> 1 & 1 == 1}
    sides = [bits[order[0]] for _, _, order in PIECES]
    normed_0, positions, place, sides, key_rows, value_rows = together(
        normed_0, positions, place, sides, key_rows, value_rows
    )
    have = [normed_0[:, first : first + width] for first, width, _ in PIECES]

    f32, bf16 = jnp.float32, jnp.bfloat16
    columns = w_query.shape[1]
    freq = 500000.0 ** (-(jnp.arange(HD, dtype=f32) % HALF * 2.0 / HD))
    cosine, sine, list_cosine, list_sine, match, flags, needed = run_kernel(
        table_kernel,
        [positions, freq[None], place.reshape(1, 1)],
        [((length, HD), f32)] * 2 + [((count, HD), f32)] * 2 + [((length, count), bf16), ((length, HD), f32), ((8, HD), f32)],
        last=[pltpu.SMEM],
    )
    other_rows = swap(key_rows, CORE), swap(value_rows, CORE)
    tables = (cosine, sine, list_cosine, list_sine, match, flags)
    got, tables, other_rows, place = together(step_up(have, 0), tables, other_rows, place)
    cosine, sine, list_cosine, list_sine, match, flags = tables
    have = joined(have, got)

    def head_weights(place, moved):
        (weights,) = run_kernel(
            weight_rows_kernel,
            [key_rows, value_rows, *other_rows, place.reshape(1, 1)],
            [((4 * HALF, key_rows.shape[1]), bf16)],
            last=[pltpu.SMEM],
            moved=moved,
        )
        return weights

    kv_weights = head_weights(place, 100000)
    def load(weights):
        if count > FEW:
            return weights
        return run_kernel(
            load_kernel, [weights], [(weights.shape, weights.dtype)], [pltpu.SemaphoreType.DMA], 1, [pl.ANY]
        )[0]

    w_query = load(w_query)
    got, kv_weights, mask_embed, norm_gain, w_query, w_out = together(
        step_up(have, 1), kv_weights, mask_embed, norm_gain, w_query, w_out
    )
    have = joined(have, got)

    gain = norm_gain[None, :].astype(f32)
    query_0, base_mask = run_kernel(
        mask_kernel,
        [mask_embed[None, :], gain, w_query, kv_weights, cosine, sine, list_cosine, list_sine],
        [((count, columns), bf16), ((length, columns + 2 * HD), bf16)],
    )
    (early,) = run_kernel(early_kernel, [*have, kv_weights], [((length // 2, 2 * HD), f32)])
    w_out = load(w_out)
    got, query_0, base_mask, early, w_out = together(step_up(have, 2), query_0, base_mask, early, w_out)

    (pair_own,) = run_kernel(
        late_kernel,
        [*got, kv_weights, early, cosine, sine],
        [((length // 2, 2 * HD), bf16)],
        [pltpu.VMEM((length // 2, 2 * HD), f32)],
    )
    x_own = joined(have, got)
    pair_other, x_own = together(swap(pair_own, CORE), x_own)
    x_other = [swap(block, CORE) for block in x_own]
    outs = run_kernel(
        first_kernel,
        [query_0, pair_own, pair_other, w_out],
        [((count // 2, width), bf16) for _, width, _ in PIECES for _ in range(2)],
        [pltpu.VMEM((count, columns), bf16), pltpu.VMEM((length, 2 * HD), bf16)],
        12,
    )
    outs, x_other = together(outs, x_other)

    def queries_of(x):
        (queries,) = run_kernel(
            query_kernel,
            [*x, w_query],
            [((length // 2, columns), f32)],
            [pltpu.VMEM((length // 2, columns), f32)],
        )
        return queries

    came = [swap(outs[2 * i + 1], CORE) for i in range(3)]
    came, x_own = together(came, x_own)
    totals = [add(outs[2 * i], came[i]) for i in range(3)]
    keep, send = [], []
    for total, side in zip(totals, sides):
        middle = total.shape[1] // 2
        left, right = total[:, :middle], total[:, middle:]
        keep.append(jnp.where(side, right, left))
        send.append(jnp.where(side, left, right))
    got = [swap(block, order[0]) for block, (_, _, order) in zip(send, PIECES)]

    got, query_own, x_other = together(got, queries_of(x_own), x_other)
    totals = added(keep, got)
    got, query_other = together(step_up(totals, 1), queries_of(x_other))
    totals = added(totals, got)
    masked_1, is_list = flags[:, :1] > 0, flags[:, 1:2] > 0
    (base,) = run_kernel(
        base_kernel,
        [pair_own, pair_other, query_own, query_other, cosine, sine, base_mask, flags],
        [((length, columns + 2 * HD), bf16)],
    )
    got, place, base = together(step_up(totals, 2), place, base)
    totals = added(totals, got)
    states = []
    for (first, width, _), total, side in zip(PIECES, totals, sides):
        row = mask_embed[None, first : first + width]
        middle = width // 2
        states.append(add(jnp.where(side, row[:, middle:], row[:, :middle]), total))
    kv_weights = head_weights(place, 100000)
    got, kv_weights = together(step_up(states, 0), kv_weights)
    raw = []
    for state, block, side in zip(states, got, sides):
        raw.append(
            jnp.where(
                side, jnp.concatenate([block, state], axis=1), jnp.concatenate([state, block], axis=1)
            )
        )
    raw = [(block, swap(block, CORE)) for block in raw]

    operands = [half for both in raw for half in both]
    operands += [gain, list_cosine, list_sine, match, base, w_query, kv_weights, w_out]
    outs = run_kernel(
        second_kernel,
        operands,
        [((length // 2, width), bf16) for _, width, _ in PIECES for _ in range(2)],
        [
            pltpu.VMEM((count, CHUNKS[0][1]), bf16),
            pltpu.VMEM((count, columns + 2 * HD), bf16),
            pltpu.VMEM((length, columns + 2 * HD), bf16),
            pltpu.VMEM((length, columns), bf16),
        ],
        26,
    )
    keep, send = outs[::2], outs[1::2]
    totals = [
        add(one, swap(two, CORE)).reshape(2, 2, 2, rows, one.shape[1]) for one, two in zip(keep, send)
    ]
    keep, incoming = step_down(totals, 0)
    own_match = match[:rows]
    middle = count // 2
    states = jnp.concatenate(
        [pick(own_match[:, :middle], one) + pick(own_match[:, middle:], two) for one, two in raw], axis=1
    )
    hidden_1 = jnp.where(
        masked_1[:rows], mask_embed[None, :], jnp.where(is_list[:rows], states, tokens)
    )
    incoming, hidden_1 = together(incoming, hidden_1)
    keep, incoming = step_down(added(keep, incoming), 1)
    incoming = together(*incoming)
    keep, incoming = step_down(added(keep, incoming), 2)
    incoming = together(*incoming)
    summed_1 = jnp.concatenate(added(keep, incoming), axis=1)
    return (hidden_1.astype(jnp.float32) + summed_1.astype(jnp.float32)).astype(jnp.bfloat16), needed


def shards(*args):
    positions = args[1]
    result, needed = together(*steps(FEW, *args))
    return lax.cond(
        needed[0, 0] <= FEW, lambda: result, lambda: steps(positions.shape[1], *args)[0]
    )


def solution(mesh):
    placed = (
        P(("dp", "tensor"), None),
        P("dp", None),
        P(),
        P(),
        P(None, "tensor"),
        P(None, "tensor"),
        P(None, "tensor"),
        P("tensor", None),
    )
    return jax.shard_map(
        shards, mesh=mesh, in_specs=placed, out_specs=P(("dp", "tensor"), None), check_vma=False
    )
```

```python
import functools

import jax
import jax.numpy as jnp
from jax import lax
from jax.experimental import pallas as pl
from jax.experimental.pallas import tpu as pltpu
from jax.sharding import PartitionSpec as P

HD = 128
HALF = HD // 2
PARTS = 16
CORE, ZED, NEAR, FAR = 1, 2, 4, 12
LINKS = (NEAR, FAR, ZED)
PIECES = (
    (0, 2816, (NEAR, FAR, ZED)),
    (2816, 2816, (FAR, ZED, NEAR)),
    (5632, 2560, (ZED, NEAR, FAR)),
)
CHUNKS = [(first + i * width // 2, width // 2) for first, width, _ in PIECES for i in range(2)]
FEW = 160
BLOCKS = [a ^ b ^ c for a in (0, NEAR) for b in (0, FAR) for c in (0, ZED)]


def swap(value, mask):
    return lax.ppermute(value, "tensor", [(i, i ^ mask) for i in range(PARTS)])


def normalize(rows, gain):
    values = rows.astype(jnp.float32)
    scale = lax.rsqrt(jnp.mean(values * values, axis=-1, keepdims=True) + 1e-05)
    return (values * scale * gain.astype(jnp.float32)).astype(jnp.bfloat16)


def turn_heads(values, cosine, sine):
    out = []
    for at in range(0, values.shape[1], HD):
        left, right = values[:, at : at + HALF], values[:, at + HALF : at + HD]
        out += [left * cosine - right * sine, right * cosine + left * sine]
    return jnp.concatenate(out, axis=1).astype(jnp.bfloat16)


def together(*values):
    return lax.optimization_barrier(values)


def keys_after(order, steps):
    keys = [0]
    for mask in order[:steps]:
        keys = keys + [key ^ mask for key in keys]
    return keys


def step_up(have, step):
    return [swap(block, order[step]) for block, (_, _, order) in zip(have, PIECES)]


def in_order(blocks, order, rows):
    keys = keys_after(order, 3)
    at = [keys.index(m) * rows for m in BLOCKS]
    return jnp.concatenate([blocks[i : i + rows] for i in at], axis=0)


def add(one, two):
    return (one.astype(jnp.float32) + two.astype(jnp.float32)).astype(jnp.bfloat16)


def step_down(totals, step):
    keep, got = [], []
    for total, (_, _, order) in zip(totals, PIECES):
        left = [mask for mask in LINKS if mask not in order[:step]]
        at = left.index(order[step])
        keep.append(lax.index_in_dim(total, 0, at, keepdims=False))
        got.append(swap(lax.index_in_dim(total, 1, at, keepdims=False), order[step]))
    return keep, got


def added(keep, got):
    return [add(one, two) for one, two in zip(keep, got)]


def with_heads(query, key, value, mixed):
    rows, columns = query.shape
    tile = rows
    for h in range(columns // HD):
        for at in range(0, rows, tile):
            scores = lax.dot_general(
                query[at : at + tile, HD * h : HD * (h + 1)],
                key,
                (((1,), (1,)), ((), ())),
                preferred_element_type=jnp.float32,
            ) * HD ** (-0.5)
            weights = jnp.exp(scores - jnp.max(scores, axis=-1, keepdims=True))
            probs = weights * (1.0 / jnp.sum(weights, axis=-1, keepdims=True))
            mixed[at : at + tile, HD * h : HD * (h + 1)] = jnp.dot(
                probs.astype(jnp.bfloat16), value, preferred_element_type=jnp.float32
            ).astype(jnp.bfloat16)


def project_out(mixed, out_here, outs):
    half = mixed.shape[0] // 2
    for i, (first, width) in enumerate(CHUNKS):
        weights = out_here[:, first : first + width]
        at = (i % 2) * width
        product = jnp.dot(mixed[...], weights, preferred_element_type=jnp.float32).astype(jnp.bfloat16)
        for side in range(2):
            outs[2 * (i // 2) + side][:, at : at + width] = product[half * side : half * (side + 1)]


def first_kernel(query, pair_own, pair_other, out_here, *rest):
    outs, (mixed, pair) = rest[:6], rest[6:]
    half = pair_own.shape[0]
    pair[:half, :] = pair_own[...]
    pair[half:, :] = pair_other[...]
    with_heads(query, pair[:, :HD], pair[:, HD:], mixed)
    project_out(mixed, out_here, outs)


def turned(values, cosine, sine):
    return (values * cosine + pltpu.roll(values, HALF, 1) * sine).astype(jnp.bfloat16)


def second_kernel(*refs):
    raw, refs = refs[:6], refs[6:]
    gain, cosine, sine, match, base, query_here, kv_here, out_here = refs[:8]
    outs, refs = refs[8:14], refs[14:]
    normed, moving, placed, mixed = refs
    half = raw[0].shape[0]
    width_all = gain.shape[1]
    scales = []
    for side in range(2):
        squares = jnp.zeros((half, HD), jnp.float32)
        for piece in range(3):
            ref = raw[2 * piece + side]

            def add_squares(i, squares, ref=ref):
                values = ref[:, pl.ds(pl.multiple_of(i * HD, HD), HD)].astype(jnp.float32)
                return squares + values * values

            squares = lax.fori_loop(0, ref.shape[1] // HD, add_squares, squares, unroll=ref.shape[1] // HD // 2)
        mean = jnp.sum(squares, axis=-1, keepdims=True) * (1.0 / width_all)
        scales.append(lax.rsqrt(mean + 1e-05))
    queries = jnp.zeros((2 * half, query_here.shape[1]), jnp.float32)
    pairs = jnp.zeros((2 * half, kv_here.shape[1]), jnp.float32)
    for i, (first, width) in enumerate(CHUNKS):
        at = (i % 2) * width
        for side in range(2):
            values = raw[2 * (i // 2) + side][:, at : at + width].astype(jnp.float32)
            normed[half * side : half * (side + 1), :width] = (
                values * scales[side] * gain[:, first : first + width]
            ).astype(jnp.bfloat16)
        some = normed[:, :width]
        queries += jnp.dot(some, query_here[first : first + width, :], preferred_element_type=jnp.float32)
        pairs += jnp.dot(some, kv_here[first : first + width, :], preferred_element_type=jnp.float32)
    moving[:, :HD] = turned(pairs[:, :HD], cosine[...], sine[...])
    moving[:, HD : 2 * HD] = pairs[:, HD:].astype(jnp.bfloat16)
    for h in range(queries.shape[1] // HD):
        moving[:, HD * (h + 2) : HD * (h + 3)] = turned(queries[:, HD * h : HD * (h + 1)], cosine[...], sine[...])
    placed[...] = base[...] + jnp.dot(
        match[...], moving[...], preferred_element_type=jnp.float32
    ).astype(jnp.bfloat16)
    with_heads(placed.at[:, 2 * HD :], placed[:, :HD], placed[:, HD : 2 * HD], mixed)
    project_out(mixed, out_here, outs)


def dot_rows(x, weights):
    return lax.dot_general(x, weights, (((1,), (1,)), ((), ())), preferred_element_type=jnp.float32)


def query_kernel(one, two, three, weights, out, total):
    rows = out.shape[0] // 8
    for i, (piece, (first, width, order)) in enumerate(zip((one, two, three), PIECES)):
        total[...] = jnp.dot(piece[...], weights[first : first + width, :], preferred_element_type=jnp.float32)
        for j, key in enumerate(keys_after(order, 3)):
            at = BLOCKS.index(key) * rows
            some = total[j * rows : (j + 1) * rows, :]
            if i == 0:
                out[at : at + rows, :] = some
            else:
                out[at : at + rows, :] += some


def dot_rows(x, weights):
    return lax.dot_general(x, weights, (((1,), (1,)), ((), ())), preferred_element_type=jnp.float32)


def base_kernel(pair_own, pair_other, query_own, query_other, cosine, sine, masked, flags, base):
    half = pair_own.shape[0]
    for core, (pair, query) in enumerate(((pair_own, query_own), (pair_other, query_other))):
        some = slice(half * core, half * (core + 1))
        is_masked, is_list = flags[some, :1] > 0, flags[some, 1:2] > 0
        for at in range(0, base.shape[1], HD):
            if at < 2 * HD:
                values = pair[:, at : at + HD]
            else:
                values = turned(query[:, at - 2 * HD : at - HD], cosine[some, :], sine[some, :])
            values = jnp.where(is_list, 0.0, values.astype(jnp.float32))
            mask_values = masked[some, at : at + HD].astype(jnp.float32)
            base[some, at : at + HD] = jnp.where(is_masked, mask_values, values).astype(jnp.bfloat16)


def call_kernel(kernel, operands, outs, scratch=(), mib=16, last=(), moved=100000, least=0):
    places = [pltpu.VMEM] * (len(operands) - len(last)) + list(last)
    return pl.pallas_call(
        kernel,
        out_shape=[jax.ShapeDtypeStruct(*out) for out in outs],
        in_specs=[pl.BlockSpec(memory_space=place) for place in places],
        out_specs=[pl.BlockSpec(memory_space=pltpu.VMEM)] * len(outs),
        scratch_shapes=list(scratch),
        compiler_params=pltpu.CompilerParams(vmem_limit_bytes=max(mib, least) * 2**20),
        cost_estimate=pl.CostEstimate(flops=1000000, bytes_accessed=moved, transcendentals=0),
    )(*operands)


def load_kernel(source, out, sem):
    copy = pltpu.make_async_copy(source, out, sem)
    copy.start()
    copy.wait()


def join_kernel(*refs):
    for i in range(3):
        have, got, out = refs[i], refs[3 + i], refs[6 + i]
        rows = have.shape[0]
        out[:rows, :] = have[...]
        out[rows:, :] = got[...]


def joined(have, got):
    outs = [((2 * block.shape[0], block.shape[1]), block.dtype) for block in have]
    return call_kernel(join_kernel, [*have, *got], outs, mib=12)


def weight_rows_kernel(key, value, other_key, other_value, place, turned_out, out):
    even = place[0, 0] % 2 == 0

    @pl.when(even)
    def _():
        out[:HALF, :] = key[...]
        out[HALF : 2 * HALF, :] = other_key[...]
        out[2 * HALF : 3 * HALF, :] = value[...]
        out[3 * HALF :, :] = other_value[...]

    @pl.when(jnp.logical_not(even))
    def _():
        out[:HALF, :] = other_key[...]
        out[HALF : 2 * HALF, :] = key[...]
        out[2 * HALF : 3 * HALF, :] = other_value[...]
        out[3 * HALF :, :] = value[...]

    width = 1024
    for at in range(0, turned_out.shape[0], width):
        turned_out[at : at + width, :] = out[:, at : at + width].T


def table_kernel(positions, freq, place, cosine, sine, list_cosine, list_sine, match, flags, needed):
    f32, bf16 = jnp.float32, jnp.bfloat16
    count, length, chosen = match.shape[1], match.shape[0], positions.shape[1]
    rows = length // PARTS
    at = lax.broadcasted_iota(jnp.int32, (length, 1), 0)
    block = at // rows
    offset = (block // 8) * CORE ^ (block // 4 % 2) * NEAR ^ (block // 2 % 2) * FAR ^ (block % 2) * ZED
    spots = (place[0, 0] ^ offset) * rows + at % rows
    listed = (lax.broadcasted_iota(jnp.int32, (count, 1), 0) + place[0, 0] % 2 * (count // 2)) % count
    ones_across, twos_across = positions[:1, :], positions[1:, :]
    row = lax.broadcasted_iota(jnp.int32, (chosen, chosen), 0)
    column = lax.broadcasted_iota(jnp.int32, (chosen, chosen), 1)
    twos = jnp.sum(jnp.where(row == column, twos_across, 0), axis=1, keepdims=True)
    stale = jnp.max(jnp.where(twos == ones_across, 1.0, 0.0), axis=0, keepdims=True)
    fresh = 1.0 - stale
    before = jnp.where(row < column, 1.0, 0.0).astype(bf16)

    def ahead(flag):
        wide = jnp.broadcast_to(flag, (16, chosen)).astype(bf16)
        return jnp.dot(wide, before, preferred_element_type=f32)[:1]

    fresh_count = jnp.sum(fresh, axis=1, keepdims=True)
    rank = jnp.where(fresh > 0, ahead(fresh), fresh_count + ahead(stale))
    needed[...] = jnp.broadcast_to(fresh_count, needed.shape)
    spot = jnp.where(listed.astype(f32) == rank, 1.0, 0.0)
    list_spots = jnp.sum(spot * ones_across.astype(f32), axis=1, keepdims=True)
    here = jnp.where((spots == ones_across) & (fresh > 0), 1.0, 0.0)
    match[...] = dot_rows(here.astype(bf16), spot.astype(bf16)).astype(bf16)
    is_list = jnp.max(here, axis=1, keepdims=True)
    masked_1 = jnp.max(jnp.where(spots == twos_across, 1.0, 0.0), axis=1, keepdims=True)
    lane = lax.broadcasted_iota(jnp.int32, (spots.shape[0], HD), 1)
    flags[...] = jnp.where(lane == 0, masked_1, is_list)
    sign = jnp.where(lax.broadcasted_iota(jnp.int32, (1, HD), 1) < HALF, -1.0, 1.0)
    angle = spots.astype(f32) * freq[...]
    cosine[...] = jnp.cos(angle)
    sine[...] = jnp.sin(angle) * sign
    angle = list_spots * freq[...]
    list_cosine[...] = jnp.cos(angle)
    list_sine[...] = jnp.sin(angle) * sign


def mask_kernel(embed, gain, query_here, kv_here, cosine, sine, list_cosine, list_sine, query, base):
    values = embed[...].astype(jnp.float32)
    mean = jnp.sum(values * values, axis=-1, keepdims=True) * (1.0 / embed.shape[1])
    row = (values * lax.rsqrt(mean + 1e-05) * gain[...]).astype(jnp.bfloat16)
    row = jnp.broadcast_to(row, (16, row.shape[1]))
    queries = jnp.dot(row, query_here[...], preferred_element_type=jnp.float32)[:1]
    pairs = jnp.dot(row, kv_here[...], preferred_element_type=jnp.float32)[:1]
    length = base.shape[0]
    base[:, :HD] = turned(jnp.broadcast_to(pairs[:, :HD], (length, HD)), cosine[...], sine[...])
    base[:, HD : 2 * HD] = jnp.broadcast_to(pairs[:, HD:], (length, HD)).astype(jnp.bfloat16)
    for at in range(0, queries.shape[1], HD):
        some = queries[:, at : at + HD]
        base[:, 2 * HD + at : 3 * HD + at] = turned(jnp.broadcast_to(some, (length, HD)), cosine[...], sine[...])
        query[:, at : at + HD] = turned(
            jnp.broadcast_to(some, (query.shape[0], HD)), list_cosine[...], list_sine[...]
        )


def add_pairs(pieces, kv_here, total, low, fresh):
    rows = total.shape[0] // 8
    for piece, (first, width, order) in zip(pieces, PIECES):
        product = jnp.dot(piece[...], kv_here[first : first + width, :], preferred_element_type=jnp.float32)
        for i, key in enumerate(keys_after(order, 3)[low : low + 4]):
            at = BLOCKS.index(key) * rows
            some = product[i * rows : (i + 1) * rows]
            if key in fresh:
                fresh.remove(key)
                total[at : at + rows, :] = some
            else:
                total[at : at + rows, :] += some


def early_kernel(one, two, three, kv_here, total):
    fresh = set(BLOCKS)
    add_pairs((one, two, three), kv_here, total, 0, fresh)
    rows = total.shape[0] // 8
    for key in fresh:
        at = BLOCKS.index(key) * rows
        total[at : at + rows, :] = jnp.zeros((rows, total.shape[1]), jnp.float32)


def late_kernel(one, two, three, kv_here, early, cosine, sine, out, total):
    total[...] = early[...]
    add_pairs((one, two, three), kv_here, total, 4, set())
    rows = total.shape[0]
    out[:, :HD] = turned(total[:, :HD], cosine[:rows, :], sine[:rows, :])
    out[:, HD:] = total[:, HD:].astype(jnp.bfloat16)


def chosen(spots, positions):
    return jnp.any(spots[:, None] == positions[None, :], axis=1)


def pick(one_hot, rows):
    return jnp.dot(
        one_hot.astype(jnp.bfloat16), rows, preferred_element_type=jnp.float32
    ).astype(jnp.bfloat16)


def steps(count, tokens, positions, mask_embed, norm_gain, w_query, w_key, w_value, w_out):
    place = lax.axis_index("tensor")
    run_kernel = functools.partial(call_kernel, least=0 if count <= FEW else 52)
    rows = tokens.shape[0]
    length = rows * PARTS

    own_spots = place * rows + jnp.arange(rows, dtype=jnp.int32)
    own_masked_0 = chosen(own_spots, positions[0])
    hidden_0 = jnp.where(own_masked_0[:, None], mask_embed[None, :], tokens)
    normed_0 = normalize(hidden_0, norm_gain)
    key_rows, value_rows = w_key.T, w_value.T
    bits = {NEAR: (place >> 2 ^ place >> 3) & 1 == 1, FAR: place >> 3 & 1 == 1, ZED: place >> 1 & 1 == 1}
    sides = [bits[order[0]] for _, _, order in PIECES]
    normed_0, positions, place, sides, key_rows, value_rows = together(
        normed_0, positions, place, sides, key_rows, value_rows
    )
    have = [normed_0[:, first : first + width] for first, width, _ in PIECES]

    f32, bf16 = jnp.float32, jnp.bfloat16
    columns = w_query.shape[1]
    freq = 500000.0 ** (-(jnp.arange(HD, dtype=f32) % HALF * 2.0 / HD))
    cosine, sine, list_cosine, list_sine, match, flags, needed = run_kernel(
        table_kernel,
        [positions, freq[None], place.reshape(1, 1)],
        [((length, HD), f32)] * 2 + [((count, HD), f32)] * 2 + [((length, count), bf16), ((length, HD), f32), ((8, HD), f32)],
        last=[pltpu.SMEM],
    )
    other_rows = swap(key_rows, CORE), swap(value_rows, CORE)
    tables = (cosine, sine, list_cosine, list_sine, match, flags)
    got, tables, other_rows, place = together(step_up(have, 0), tables, other_rows, place)
    cosine, sine, list_cosine, list_sine, match, flags = tables
    have = joined(have, got)

    def head_weights(place, moved):
        (weights,) = run_kernel(
            weight_rows_kernel,
            [key_rows, value_rows, *other_rows, place.reshape(1, 1)],
            [((key_rows.shape[1], 4 * HALF), bf16)],
            [pltpu.VMEM((4 * HALF, key_rows.shape[1]), bf16)],
            last=[pltpu.SMEM],
            moved=moved,
        )
        return weights

    kv_weights = head_weights(place, 100000)
    def load(weights):
        if count > FEW:
            return weights
        return run_kernel(
            load_kernel, [weights], [(weights.shape, weights.dtype)], [pltpu.SemaphoreType.DMA], 1, [pl.ANY]
        )[0]

    w_query = load(w_query)
    got, kv_weights, mask_embed, norm_gain, w_query, w_out = together(
        step_up(have, 1), kv_weights, mask_embed, norm_gain, w_query, w_out
    )
    have = joined(have, got)

    gain = norm_gain[None, :].astype(f32)
    query_0, base_mask = run_kernel(
        mask_kernel,
        [mask_embed[None, :], gain, w_query, kv_weights, cosine, sine, list_cosine, list_sine],
        [((count, columns), bf16), ((length, columns + 2 * HD), bf16)],
    )
    (early,) = run_kernel(early_kernel, [*have, kv_weights], [((length // 2, 2 * HD), f32)])
    w_out = load(w_out)
    got, query_0, base_mask, early, w_out = together(step_up(have, 2), query_0, base_mask, early, w_out)

    (pair_own,) = run_kernel(
        late_kernel,
        [*got, kv_weights, early, cosine, sine],
        [((length // 2, 2 * HD), bf16)],
        [pltpu.VMEM((length // 2, 2 * HD), f32)],
    )
    x_own = joined(have, got)
    pair_other, x_own = together(swap(pair_own, CORE), x_own)
    x_other = [swap(block, CORE) for block in x_own]
    outs = run_kernel(
        first_kernel,
        [query_0, pair_own, pair_other, w_out],
        [((count // 2, width), bf16) for _, width, _ in PIECES for _ in range(2)],
        [pltpu.VMEM((count, columns), bf16), pltpu.VMEM((length, 2 * HD), bf16)],
        12,
    )
    outs, x_other = together(outs, x_other)

    def queries_of(x):
        (queries,) = run_kernel(
            query_kernel,
            [*x, w_query],
            [((length // 2, columns), f32)],
            [pltpu.VMEM((length // 2, columns), f32)],
        )
        return queries

    came = [swap(outs[2 * i + 1], CORE) for i in range(3)]
    came, x_own = together(came, x_own)
    totals = [add(outs[2 * i], came[i]) for i in range(3)]
    keep, send = [], []
    for total, side in zip(totals, sides):
        middle = total.shape[1] // 2
        left, right = total[:, :middle], total[:, middle:]
        keep.append(jnp.where(side, right, left))
        send.append(jnp.where(side, left, right))
    got = [swap(block, order[0]) for block, (_, _, order) in zip(send, PIECES)]

    got, query_own, x_other = together(got, queries_of(x_own), x_other)
    totals = added(keep, got)
    got, query_other = together(step_up(totals, 1), queries_of(x_other))
    totals = added(totals, got)
    masked_1, is_list = flags[:, :1] > 0, flags[:, 1:2] > 0
    (base,) = run_kernel(
        base_kernel,
        [pair_own, pair_other, query_own, query_other, cosine, sine, base_mask, flags],
        [((length, columns + 2 * HD), bf16)],
    )
    got, place, base = together(step_up(totals, 2), place, base)
    totals = added(totals, got)
    states = []
    for (first, width, _), total, side in zip(PIECES, totals, sides):
        row = mask_embed[None, first : first + width]
        middle = width // 2
        states.append(add(jnp.where(side, row[:, middle:], row[:, :middle]), total))
    kv_weights = head_weights(place, 100000)
    got, kv_weights = together(step_up(states, 0), kv_weights)
    raw = []
    for state, block, side in zip(states, got, sides):
        raw.append(
            jnp.where(
                side, jnp.concatenate([block, state], axis=1), jnp.concatenate([state, block], axis=1)
            )
        )
    raw = [(block, swap(block, CORE)) for block in raw]

    operands = [half for both in raw for half in both]
    operands += [gain, list_cosine, list_sine, match, base, w_query, kv_weights, w_out]
    outs = run_kernel(
        second_kernel,
        operands,
        [((length // 2, width), bf16) for _, width, _ in PIECES for _ in range(2)],
        [
            pltpu.VMEM((count, CHUNKS[0][1]), bf16),
            pltpu.VMEM((count, columns + 2 * HD), bf16),
            pltpu.VMEM((length, columns + 2 * HD), bf16),
            pltpu.VMEM((length, columns), bf16),
        ],
        26,
    )
    keep, send = outs[::2], outs[1::2]
    totals = [
        add(one, swap(two, CORE)).reshape(2, 2, 2, rows, one.shape[1]) for one, two in zip(keep, send)
    ]
    keep, incoming = step_down(totals, 0)
    own_match = match[:rows]
    middle = count // 2
    states = jnp.concatenate(
        [pick(own_match[:, :middle], one) + pick(own_match[:, middle:], two) for one, two in raw], axis=1
    )
    hidden_1 = jnp.where(
        masked_1[:rows], mask_embed[None, :], jnp.where(is_list[:rows], states, tokens)
    )
    incoming, hidden_1 = together(incoming, hidden_1)
    keep, incoming = step_down(added(keep, incoming), 1)
    incoming = together(*incoming)
    keep, incoming = step_down(added(keep, incoming), 2)
    incoming = together(*incoming)
    summed_1 = jnp.concatenate(added(keep, incoming), axis=1)
    return (hidden_1.astype(jnp.float32) + summed_1.astype(jnp.float32)).astype(jnp.bfloat16), needed


def shards(*args):
    positions = args[1]
    result, needed = together(*steps(FEW, *args))
    return lax.cond(
        needed[0, 0] <= FEW, lambda: result, lambda: steps(positions.shape[1], *args)[0]
    )


def solution(mesh):
    placed = (
        P(("dp", "tensor"), None),
        P("dp", None),
        P(),
        P(),
        P(None, "tensor"),
        P(None, "tensor"),
        P(None, "tensor"),
        P("tensor", None),
    )
    return jax.shard_map(
        shards, mesh=mesh, in_specs=placed, out_specs=P(("dp", "tensor"), None), check_vma=False
    )
```

```python
import functools

import jax
import jax.numpy as jnp
from jax import lax
from jax.experimental import pallas as pl
from jax.experimental.pallas import tpu as pltpu
from jax.sharding import PartitionSpec as P

HD = 128
HALF = HD // 2
PARTS = 16
CORE, ZED, NEAR, FAR = 1, 2, 4, 12
LINKS = (NEAR, FAR, ZED)
PIECES = (
    (0, 2816, (NEAR, FAR, ZED)),
    (2816, 2816, (FAR, ZED, NEAR)),
    (5632, 2560, (ZED, NEAR, FAR)),
)
CHUNKS = [(first + i * width // 2, width // 2) for first, width, _ in PIECES for i in range(2)]
FEW = 160
BLOCKS = [a ^ b ^ c for a in (0, NEAR) for b in (0, FAR) for c in (0, ZED)]


def swap(value, mask):
    return lax.ppermute(value, "tensor", [(i, i ^ mask) for i in range(PARTS)])


def normalize(rows, gain):
    values = rows.astype(jnp.float32)
    scale = lax.rsqrt(jnp.mean(values * values, axis=-1, keepdims=True) + 1e-05)
    return (values * scale * gain.astype(jnp.float32)).astype(jnp.bfloat16)


def turn_heads(values, cosine, sine):
    out = []
    for at in range(0, values.shape[1], HD):
        left, right = values[:, at : at + HALF], values[:, at + HALF : at + HD]
        out += [left * cosine - right * sine, right * cosine + left * sine]
    return jnp.concatenate(out, axis=1).astype(jnp.bfloat16)


def together(*values):
    return lax.optimization_barrier(values)


def keys_after(order, steps):
    keys = [0]
    for mask in order[:steps]:
        keys = keys + [key ^ mask for key in keys]
    return keys


def step_up(have, step):
    return [swap(block, order[step]) for block, (_, _, order) in zip(have, PIECES)]


def in_order(blocks, order, rows):
    keys = keys_after(order, 3)
    at = [keys.index(m) * rows for m in BLOCKS]
    return jnp.concatenate([blocks[i : i + rows] for i in at], axis=0)


def add(one, two):
    return (one.astype(jnp.float32) + two.astype(jnp.float32)).astype(jnp.bfloat16)


def step_down(totals, step):
    keep, got = [], []
    for total, (_, _, order) in zip(totals, PIECES):
        left = [mask for mask in LINKS if mask not in order[:step]]
        at = left.index(order[step])
        keep.append(lax.index_in_dim(total, 0, at, keepdims=False))
        got.append(swap(lax.index_in_dim(total, 1, at, keepdims=False), order[step]))
    return keep, got


def added(keep, got):
    return [add(one, two) for one, two in zip(keep, got)]


def with_heads(query, key, value, mixed):
    rows, columns = query.shape
    tile = rows
    for h in range(columns // HD):
        for at in range(0, rows, tile):
            scores = lax.dot_general(
                query[at : at + tile, HD * h : HD * (h + 1)],
                key,
                (((1,), (1,)), ((), ())),
                preferred_element_type=jnp.float32,
            ) * HD ** (-0.5)
            weights = jnp.exp(scores - jnp.max(scores, axis=-1, keepdims=True))
            probs = weights * (1.0 / jnp.sum(weights, axis=-1, keepdims=True))
            mixed[at : at + tile, HD * h : HD * (h + 1)] = jnp.dot(
                probs.astype(jnp.bfloat16), value, preferred_element_type=jnp.float32
            ).astype(jnp.bfloat16)


def project_out(mixed, out_here, outs):
    half = mixed.shape[0] // 2
    for i, (first, width) in enumerate(CHUNKS):
        weights = out_here[:, first : first + width]
        at = (i % 2) * width
        product = jnp.dot(mixed[...], weights, preferred_element_type=jnp.float32).astype(jnp.bfloat16)
        for side in range(2):
            outs[2 * (i // 2) + side][:, at : at + width] = product[half * side : half * (side + 1)]


def first_kernel(query, pair_own, pair_other, out_here, *rest):
    outs, (mixed, pair) = rest[:6], rest[6:]
    half = pair_own.shape[0]
    pair[:half, :] = pair_own[...]
    pair[half:, :] = pair_other[...]
    with_heads(query, pair[:, :HD], pair[:, HD:], mixed)
    project_out(mixed, out_here, outs)


def turned(values, cosine, sine):
    return (values * cosine + pltpu.roll(values, HALF, 1) * sine).astype(jnp.bfloat16)


def second_kernel(*refs):
    raw, refs = refs[:6], refs[6:]
    gain, cosine, sine, match, base, query_here, kv_here, out_here = refs[:8]
    outs, refs = refs[8:14], refs[14:]
    normed, moving, placed, mixed = refs
    half = raw[0].shape[0]
    width_all = gain.shape[1]
    scales = []
    for side in range(2):
        squares = jnp.zeros((half, HD), jnp.float32)
        for piece in range(3):
            ref = raw[2 * piece + side]

            def add_squares(i, squares, ref=ref):
                values = ref[:, pl.ds(pl.multiple_of(i * HD, HD), HD)].astype(jnp.float32)
                return squares + values * values

            squares = lax.fori_loop(0, ref.shape[1] // HD, add_squares, squares, unroll=ref.shape[1] // HD // 2)
        mean = jnp.sum(squares, axis=-1, keepdims=True) * (1.0 / width_all)
        scales.append(lax.rsqrt(mean + 1e-05))
    queries = jnp.zeros((2 * half, query_here.shape[1]), jnp.float32)
    pairs = jnp.zeros((2 * half, kv_here.shape[1]), jnp.float32)
    for i, (first, width) in enumerate(CHUNKS):
        at = (i % 2) * width
        for side in range(2):
            values = raw[2 * (i // 2) + side][:, at : at + width].astype(jnp.float32)
            normed[half * side : half * (side + 1), :width] = (
                values * scales[side] * gain[:, first : first + width]
            ).astype(jnp.bfloat16)
        some = normed[:, :width]
        queries += jnp.dot(some, query_here[first : first + width, :], preferred_element_type=jnp.float32)
        pairs += jnp.dot(some, kv_here[first : first + width, :], preferred_element_type=jnp.float32)
    moving[:, :HD] = turned(pairs[:, :HD], cosine[...], sine[...])
    moving[:, HD : 2 * HD] = pairs[:, HD:].astype(jnp.bfloat16)
    for h in range(queries.shape[1] // HD):
        moving[:, HD * (h + 2) : HD * (h + 3)] = turned(queries[:, HD * h : HD * (h + 1)], cosine[...], sine[...])
    placed[...] = base[...] + jnp.dot(
        match[...], moving[...], preferred_element_type=jnp.float32
    ).astype(jnp.bfloat16)
    with_heads(placed.at[:, 2 * HD :], placed[:, :HD], placed[:, HD : 2 * HD], mixed)
    project_out(mixed, out_here, outs)


def dot_rows(x, weights):
    return lax.dot_general(x, weights, (((1,), (1,)), ((), ())), preferred_element_type=jnp.float32)


def query_kernel(one, two, three, weights, out, total):
    rows = out.shape[0] // 8
    for i, (piece, (first, width, order)) in enumerate(zip((one, two, three), PIECES)):
        total[...] = jnp.dot(piece[...], weights[first : first + width, :], preferred_element_type=jnp.float32)
        for j, key in enumerate(keys_after(order, 3)):
            at = BLOCKS.index(key) * rows
            some = total[j * rows : (j + 1) * rows, :]
            if i == 0:
                out[at : at + rows, :] = some
            else:
                out[at : at + rows, :] += some


def dot_rows(x, weights):
    return lax.dot_general(x, weights, (((1,), (1,)), ((), ())), preferred_element_type=jnp.float32)


def base_kernel(pair_own, pair_other, query_own, query_other, cosine, sine, masked, flags, base):
    half = pair_own.shape[0]
    for core, (pair, query) in enumerate(((pair_own, query_own), (pair_other, query_other))):
        some = slice(half * core, half * (core + 1))
        is_masked, is_list = flags[some, :1] > 0, flags[some, 1:2] > 0
        for at in range(0, base.shape[1], HD):
            if at < 2 * HD:
                values = pair[:, at : at + HD]
            else:
                values = turned(query[:, at - 2 * HD : at - HD], cosine[some, :], sine[some, :])
            values = jnp.where(is_list, 0.0, values.astype(jnp.float32))
            mask_values = masked[some, at : at + HD].astype(jnp.float32)
            base[some, at : at + HD] = jnp.where(is_masked, mask_values, values).astype(jnp.bfloat16)


def call_kernel(kernel, operands, outs, scratch=(), mib=16, last=(), moved=100000, least=0):
    places = [pltpu.VMEM] * (len(operands) - len(last)) + list(last)
    return pl.pallas_call(
        kernel,
        out_shape=[jax.ShapeDtypeStruct(*out) for out in outs],
        in_specs=[pl.BlockSpec(memory_space=place) for place in places],
        out_specs=[pl.BlockSpec(memory_space=pltpu.VMEM)] * len(outs),
        scratch_shapes=list(scratch),
        compiler_params=pltpu.CompilerParams(vmem_limit_bytes=max(mib, least) * 2**20),
        cost_estimate=pl.CostEstimate(flops=1000000, bytes_accessed=moved, transcendentals=0),
    )(*operands)


def load_kernel(source, out, sem):
    copy = pltpu.make_async_copy(source, out, sem)
    copy.start()
    copy.wait()


def join_kernel(*refs):
    for i in range(3):
        have, got, out = refs[i], refs[3 + i], refs[6 + i]
        rows = have.shape[0]
        out[:rows, :] = have[...]
        out[rows:, :] = got[...]


def joined(have, got):
    outs = [((2 * block.shape[0], block.shape[1]), block.dtype) for block in have]
    return call_kernel(join_kernel, [*have, *got], outs, mib=12)


def weight_rows_kernel(key, value, other_key, other_value, place, turned_out, out):
    even = place[0, 0] % 2 == 0

    @pl.when(even)
    def _():
        out[:HALF, :] = key[...]
        out[HALF : 2 * HALF, :] = other_key[...]
        out[2 * HALF : 3 * HALF, :] = value[...]
        out[3 * HALF :, :] = other_value[...]

    @pl.when(jnp.logical_not(even))
    def _():
        out[:HALF, :] = other_key[...]
        out[HALF : 2 * HALF, :] = key[...]
        out[2 * HALF : 3 * HALF, :] = other_value[...]
        out[3 * HALF :, :] = value[...]

    width = 1024
    for at in range(0, turned_out.shape[0], width):
        turned_out[at : at + width, :] = out[:, at : at + width].T


def table_kernel(positions, freq, place, cosine, sine, list_cosine, list_sine, match, flags, needed):
    f32, bf16 = jnp.float32, jnp.bfloat16
    count, length, chosen = match.shape[1], match.shape[0], positions.shape[1]
    rows = length // PARTS
    at = lax.broadcasted_iota(jnp.int32, (length, 1), 0)
    block = at // rows
    offset = (block // 8) * CORE ^ (block // 4 % 2) * NEAR ^ (block // 2 % 2) * FAR ^ (block % 2) * ZED
    spots = (place[0, 0] ^ offset) * rows + at % rows
    listed = (lax.broadcasted_iota(jnp.int32, (count, 1), 0) + place[0, 0] % 2 * (count // 2)) % count
    ones_across, twos_across = positions[:1, :], positions[1:, :]
    row = lax.broadcasted_iota(jnp.int32, (chosen, chosen), 0)
    column = lax.broadcasted_iota(jnp.int32, (chosen, chosen), 1)
    twos = jnp.sum(jnp.where(row == column, twos_across, 0), axis=1, keepdims=True)
    stale = jnp.max(jnp.where(twos == ones_across, 1.0, 0.0), axis=0, keepdims=True)
    fresh = 1.0 - stale
    before = jnp.where(row < column, 1.0, 0.0).astype(bf16)

    def ahead(flag):
        wide = jnp.broadcast_to(flag, (16, chosen)).astype(bf16)
        return jnp.dot(wide, before, preferred_element_type=f32)[:1]

    fresh_count = jnp.sum(fresh, axis=1, keepdims=True)
    rank = jnp.where(fresh > 0, ahead(fresh), fresh_count + ahead(stale))
    needed[...] = jnp.broadcast_to(fresh_count, needed.shape)
    spot = jnp.where(listed.astype(f32) == rank, 1.0, 0.0)
    list_spots = jnp.sum(spot * ones_across.astype(f32), axis=1, keepdims=True)
    here = jnp.where((spots == ones_across) & (fresh > 0), 1.0, 0.0)
    match[...] = dot_rows(here.astype(bf16), spot.astype(bf16)).astype(bf16)
    is_list = jnp.max(here, axis=1, keepdims=True)
    masked_1 = jnp.max(jnp.where(spots == twos_across, 1.0, 0.0), axis=1, keepdims=True)
    lane = lax.broadcasted_iota(jnp.int32, (spots.shape[0], HD), 1)
    flags[...] = jnp.where(lane == 0, masked_1, is_list)
    sign = jnp.where(lax.broadcasted_iota(jnp.int32, (1, HD), 1) < HALF, -1.0, 1.0)
    angle = spots.astype(f32) * freq[...]
    cosine[...] = jnp.cos(angle)
    sine[...] = jnp.sin(angle) * sign
    angle = list_spots * freq[...]
    list_cosine[...] = jnp.cos(angle)
    list_sine[...] = jnp.sin(angle) * sign


def mask_kernel(embed, gain, query_here, kv_here, cosine, sine, list_cosine, list_sine, query, base):
    values = embed[...].astype(jnp.float32)
    mean = jnp.sum(values * values, axis=-1, keepdims=True) * (1.0 / embed.shape[1])
    row = (values * lax.rsqrt(mean + 1e-05) * gain[...]).astype(jnp.bfloat16)
    row = jnp.broadcast_to(row, (16, row.shape[1]))
    queries = jnp.dot(row, query_here[...], preferred_element_type=jnp.float32)[:1]
    pairs = jnp.dot(row, kv_here[...], preferred_element_type=jnp.float32)[:1]
    length = base.shape[0]
    base[:, :HD] = turned(jnp.broadcast_to(pairs[:, :HD], (length, HD)), cosine[...], sine[...])
    base[:, HD : 2 * HD] = jnp.broadcast_to(pairs[:, HD:], (length, HD)).astype(jnp.bfloat16)
    for at in range(0, queries.shape[1], HD):
        some = queries[:, at : at + HD]
        base[:, 2 * HD + at : 3 * HD + at] = turned(jnp.broadcast_to(some, (length, HD)), cosine[...], sine[...])
        query[:, at : at + HD] = turned(
            jnp.broadcast_to(some, (query.shape[0], HD)), list_cosine[...], list_sine[...]
        )


def add_pairs(pieces, kv_here, total, low, fresh):
    rows = total.shape[0] // 8
    for piece, (first, width, order) in zip(pieces, PIECES):
        product = jnp.dot(piece[...], kv_here[first : first + width, :], preferred_element_type=jnp.float32)
        for i, key in enumerate(keys_after(order, 3)[low : low + 4]):
            at = BLOCKS.index(key) * rows
            some = product[i * rows : (i + 1) * rows]
            if key in fresh:
                fresh.remove(key)
                total[at : at + rows, :] = some
            else:
                total[at : at + rows, :] += some


def early_kernel(one, two, three, kv_here, total):
    fresh = set(BLOCKS)
    add_pairs((one, two, three), kv_here, total, 0, fresh)
    rows = total.shape[0] // 8
    for key in fresh:
        at = BLOCKS.index(key) * rows
        total[at : at + rows, :] = jnp.zeros((rows, total.shape[1]), jnp.float32)


def late_kernel(one, two, three, kv_here, early, cosine, sine, out, total):
    total[...] = early[...]
    add_pairs((one, two, three), kv_here, total, 4, set())
    rows = total.shape[0]
    out[:, :HD] = turned(total[:, :HD], cosine[:rows, :], sine[:rows, :])
    out[:, HD:] = total[:, HD:].astype(jnp.bfloat16)


def chosen(spots, positions):
    return jnp.any(spots[:, None] == positions[None, :], axis=1)


def pick(one_hot, rows):
    return jnp.dot(
        one_hot.astype(jnp.bfloat16), rows, preferred_element_type=jnp.float32
    ).astype(jnp.bfloat16)


def steps(count, tokens, positions, mask_embed, norm_gain, w_query, w_key, w_value, w_out):
    place = lax.axis_index("tensor")
    run_kernel = functools.partial(call_kernel, least=0 if count <= FEW else 52)
    rows = tokens.shape[0]
    length = rows * PARTS

    own_spots = place * rows + jnp.arange(rows, dtype=jnp.int32)
    own_masked_0 = chosen(own_spots, positions[0])
    hidden_0 = jnp.where(own_masked_0[:, None], mask_embed[None, :], tokens)
    normed_0 = normalize(hidden_0, norm_gain)
    key_rows, value_rows = w_key.T, w_value.T
    bits = {NEAR: (place >> 2 ^ place >> 3) & 1 == 1, FAR: place >> 3 & 1 == 1, ZED: place >> 1 & 1 == 1}
    sides = [bits[order[0]] for _, _, order in PIECES]
    normed_0, positions, place, sides, key_rows, value_rows = together(
        normed_0, positions, place, sides, key_rows, value_rows
    )
    have = [normed_0[:, first : first + width] for first, width, _ in PIECES]

    f32, bf16 = jnp.float32, jnp.bfloat16
    columns = w_query.shape[1]
    freq = 500000.0 ** (-(jnp.arange(HD, dtype=f32) % HALF * 2.0 / HD))
    cosine, sine, list_cosine, list_sine, match, flags, needed = run_kernel(
        table_kernel,
        [positions, freq[None], place.reshape(1, 1)],
        [((length, HD), f32)] * 2 + [((count, HD), f32)] * 2 + [((length, count), bf16), ((length, HD), f32), ((8, HD), f32)],
        last=[pltpu.SMEM],
    )
    other_rows = swap(key_rows, CORE), swap(value_rows, CORE)
    tables = (cosine, sine, list_cosine, list_sine, match, flags)
    got, tables, other_rows, place = together(step_up(have, 0), tables, other_rows, place)
    cosine, sine, list_cosine, list_sine, match, flags = tables
    have = joined(have, got)

    def head_weights(place, moved):
        (weights,) = run_kernel(
            weight_rows_kernel,
            [key_rows, value_rows, *other_rows, place.reshape(1, 1)],
            [((key_rows.shape[1], 4 * HALF), bf16)],
            [pltpu.VMEM((4 * HALF, key_rows.shape[1]), bf16)],
            last=[pltpu.SMEM],
            moved=moved,
        )
        return weights

    kv_weights = head_weights(place, 100000)
    def load(weights):
        if count > FEW:
            return weights
        return run_kernel(
            load_kernel, [weights], [(weights.shape, weights.dtype)], [pltpu.SemaphoreType.DMA], 1, [pl.ANY]
        )[0]

    w_query = load(w_query)
    got, kv_weights, mask_embed, norm_gain, w_query, w_out = together(
        step_up(have, 1), kv_weights, mask_embed, norm_gain, w_query, w_out
    )
    have = joined(have, got)

    gain = norm_gain[None, :].astype(f32)
    query_0, base_mask = run_kernel(
        mask_kernel,
        [mask_embed[None, :], gain, w_query, kv_weights, cosine, sine, list_cosine, list_sine],
        [((count, columns), bf16), ((length, columns + 2 * HD), bf16)],
    )
    (early,) = run_kernel(early_kernel, [*have, kv_weights], [((length // 2, 2 * HD), f32)])
    w_out = load(w_out)
    got, query_0, base_mask, early, w_out = together(step_up(have, 2), query_0, base_mask, early, w_out)

    (pair_own,) = run_kernel(
        late_kernel,
        [*got, kv_weights, early, cosine, sine],
        [((length // 2, 2 * HD), bf16)],
        [pltpu.VMEM((length // 2, 2 * HD), f32)],
    )
    x_own = joined(have, got)
    pair_other, x_own = together(swap(pair_own, CORE), x_own)
    x_other = [swap(block, CORE) for block in x_own]
    outs = run_kernel(
        first_kernel,
        [query_0, pair_own, pair_other, w_out],
        [((count // 2, width), bf16) for _, width, _ in PIECES for _ in range(2)],
        [pltpu.VMEM((count, columns), bf16), pltpu.VMEM((length, 2 * HD), bf16)],
        12,
    )

    def queries_of(x):
        (queries,) = run_kernel(
            query_kernel,
            [*x, w_query],
            [((length // 2, columns), f32)],
            [pltpu.VMEM((length // 2, columns), f32)],
        )
        return queries

    came = [swap(outs[2 * i + 1], CORE) for i in range(3)]
    came, x_own = together(came, x_own)
    totals = [add(outs[2 * i], came[i]) for i in range(3)]
    keep, send = [], []
    for total, side in zip(totals, sides):
        middle = total.shape[1] // 2
        left, right = total[:, :middle], total[:, middle:]
        keep.append(jnp.where(side, right, left))
        send.append(jnp.where(side, left, right))
    got = [swap(block, order[0]) for block, (_, _, order) in zip(send, PIECES)]

    got, query_own, x_other = together(got, queries_of(x_own), x_other)
    totals = added(keep, got)
    got, query_other = together(step_up(totals, 1), queries_of(x_other))
    totals = added(totals, got)
    masked_1, is_list = flags[:, :1] > 0, flags[:, 1:2] > 0
    (base,) = run_kernel(
        base_kernel,
        [pair_own, pair_other, query_own, query_other, cosine, sine, base_mask, flags],
        [((length, columns + 2 * HD), bf16)],
    )
    got, place, base = together(step_up(totals, 2), place, base)
    totals = added(totals, got)
    states = []
    for (first, width, _), total, side in zip(PIECES, totals, sides):
        row = mask_embed[None, first : first + width]
        middle = width // 2
        states.append(add(jnp.where(side, row[:, middle:], row[:, :middle]), total))
    kv_weights = head_weights(place, 100000)
    got, kv_weights = together(step_up(states, 0), kv_weights)
    raw = []
    for state, block, side in zip(states, got, sides):
        raw.append(
            jnp.where(
                side, jnp.concatenate([block, state], axis=1), jnp.concatenate([state, block], axis=1)
            )
        )
    raw = [(block, swap(block, CORE)) for block in raw]

    operands = [half for both in raw for half in both]
    operands += [gain, list_cosine, list_sine, match, base, w_query, kv_weights, w_out]
    outs = run_kernel(
        second_kernel,
        operands,
        [((length // 2, width), bf16) for _, width, _ in PIECES for _ in range(2)],
        [
            pltpu.VMEM((count, CHUNKS[0][1]), bf16),
            pltpu.VMEM((count, columns + 2 * HD), bf16),
            pltpu.VMEM((length, columns + 2 * HD), bf16),
            pltpu.VMEM((length, columns), bf16),
        ],
        26,
    )
    keep, send = outs[::2], outs[1::2]
    totals = [
        add(one, swap(two, CORE)).reshape(2, 2, 2, rows, one.shape[1]) for one, two in zip(keep, send)
    ]
    keep, incoming = step_down(totals, 0)
    own_match = match[:rows]
    middle = count // 2
    states = jnp.concatenate(
        [pick(own_match[:, :middle], one) + pick(own_match[:, middle:], two) for one, two in raw], axis=1
    )
    hidden_1 = jnp.where(
        masked_1[:rows], mask_embed[None, :], jnp.where(is_list[:rows], states, tokens)
    )
    incoming, hidden_1 = together(incoming, hidden_1)
    keep, incoming = step_down(added(keep, incoming), 1)
    incoming = together(*incoming)
    keep, incoming = step_down(added(keep, incoming), 2)
    incoming = together(*incoming)
    summed_1 = jnp.concatenate(added(keep, incoming), axis=1)
    return (hidden_1.astype(jnp.float32) + summed_1.astype(jnp.float32)).astype(jnp.bfloat16), needed


def shards(*args):
    positions = args[1]
    result, needed = together(*steps(FEW, *args))
    return lax.cond(
        needed[0, 0] <= FEW, lambda: result, lambda: steps(positions.shape[1], *args)[0]
    )


def solution(mesh):
    placed = (
        P(("dp", "tensor"), None),
        P("dp", None),
        P(),
        P(),
        P(None, "tensor"),
        P(None, "tensor"),
        P(None, "tensor"),
        P("tensor", None),
    )
    return jax.shard_map(
        shards, mesh=mesh, in_specs=placed, out_specs=P(("dp", "tensor"), None), check_vma=False
    )
```
